128 devices in a mesh: dp: 16 (over y, x), context: 8 (over z, core).
Axes of the slice: x: 4, y: 4, z: 4, core: 2. Of those that a mesh axis runs over, the one named last changes fastest.
Arguments:
- tokens: bfloat16 [32768, 1024], P(('dp', 'context')), may hold values from -6 to 6
- segments: int32 [32768], P(('dp', 'context')), may hold values from 0 to 2, as said below
- cotangent: bfloat16 [32768, 1024], P(('dp', 'context')), may hold values from -6 to 6
- attention_gain: float32 [1024], replicated, may hold values from 0.5 to 1.5
- query_weight: bfloat16 [1024, 512], P('dp'), may hold values from -0.1875 to 0.1875
- key_matrix: bfloat16 [1024, 128], P('dp'), may hold values from -0.1875 to 0.1875
- value_matrix: bfloat16 [1024, 128], P('dp'), may hold values from -0.1875 to 0.1875
- attention_out: bfloat16 [512, 1024], P('dp'), may hold values from -3 to 3
- gate_weight: bfloat16 [1024, 1536], P('dp'), may hold values from -0.1875 to 0.1875
- mixer_weight: bfloat16 [1024, 1792], P('dp'), may hold values from -0.1875 to 0.1875
- step_weight: bfloat16 [1024, 24], P('dp'), may hold values from -0.1875 to 0.1875
- mixer_out: bfloat16 [1536, 1024], P('dp'), may hold values from -0.4375 to 0.4375
- conv_weight: float32 [4, 1792], replicated, may hold values from -3 to 3
- conv_bias: float32 [1792], replicated, may hold values from -3 to 3
- step_bias: float32 [24], replicated, may hold values from -4 to -1
- decay_log: float32 [24], replicated, may hold values from -3 to 1
- skip_gain: float32 [24], replicated, may hold values from 0.5 to 1.5
- feed_gain: float32 [1024], replicated, may hold values from 0.5 to 1.5
- feed_gate: bfloat16 [1024, 2048], P('dp'), may hold values from -0.1875 to 0.1875
- feed_up: bfloat16 [1024, 2048], P('dp'), may hold values from -0.1875 to 0.1875
- feed_down: bfloat16 [2048, 1024], P('dp'), may hold values from -0.125 to 0.125
Outputs:
- output: bfloat16 [32768, 1024], P(('dp', 'context'))
- grad_tokens: float32 [32768, 1024], P(('dp', 'context'))
- grad_attention_gain: float32 [1024], replicated
- grad_query_weight: float32 [1024, 512], P('dp')
- grad_key_weight: float32 [1024, 128], P('dp')
- grad_value_weight: float32 [1024, 128], P('dp')
- grad_attention_out: float32 [512, 1024], P('dp')
- grad_gate_weight: float32 [1024, 1536], P('dp')
- grad_mixer_weight: float32 [1024, 1792], P('dp')
- grad_step_weight: float32 [1024, 24], P('dp')
- grad_mixer_out: float32 [1536, 1024], P('dp')
- grad_conv_weight: float32 [4, 1792], replicated
- grad_conv_bias: float32 [1792], replicated
- grad_step_bias: float32 [24], replicated
- grad_decay_log: float32 [24], replicated
- grad_skip_gain: float32 [24], replicated
- grad_feed_gain: float32 [1024], replicated
- grad_feed_gate: float32 [1024, 2048], P('dp')
- grad_feed_up: float32 [1024, 2048], P('dp')
- grad_feed_down: float32 [2048, 1024], P('dp')
The draws below stay inside these ranges and needn't reach their ends.
Inputs may be any that keep to these rules, and one draw needn't show every extreme that they name: `segments`: within each sequence of 2048 tokens the numbers never fall: document 0 ends within the sequence's first 256 tokens, document 2 begins within its last 256 tokens, and document 1 lies between.
All inputs are finite; a program needn't handle non-finite values.
Results may differ from the reference program's by a relative error of at most 0.02.
Values may be sent and summed in bfloat16 or wider, within the bound.
No kernel may reach another device: no remote copies, remote signals or barrier semaphores. Data moves between devices by JAX's collectives and lax.ppermute only.
A program may use at most 192 MiB of HBM per device.

```python
import math
import jax
import jax.numpy as jnp
from jax import lax

MODEL_WIDTH = 1024
QUERY_HEADS = 8
KEY_VALUE_HEADS = 2
HEAD_WIDTH = 64
MH = 24
MP = 64
NS = 128
KC = 4
FF = 2048
SEQ_LEN = 2048
ROWS = 256
TOKENS = 32768
N_DP = 16


def draw_segments(key, part):
    key = jax.random.fold_in(key, 11)
    first_key, second_key = jax.random.split(key)
    sequences = TOKENS // SEQ_LEN
    first_end = jax.random.randint(first_key, (sequences, 1), 1, ROWS)
    second_start = jax.random.randint(second_key, (sequences, 1), SEQ_LEN - ROWS + 1, SEQ_LEN)
    places = jnp.arange(SEQ_LEN, dtype=jnp.int32)[None, :]
    numbers = (places >= first_end).astype(jnp.int32) + (places >= second_start).astype(jnp.int32)
    return numbers.reshape(TOKENS)


def block_scale(own_key, dims, shards, smallest, largest):
    loudness = 1.0
    for dim, blocks in shards:
        draws = jax.random.uniform(jax.random.fold_in(jax.random.fold_in(own_key, 6), dim), (blocks,), jnp.float32, smallest / len(shards), largest / len(shards))
        loudness = loudness * jnp.repeat(jnp.exp(draws), dims[dim] // blocks).reshape((-1,) + (1,) * (len(dims) - 1 - dim))
    return loudness


def gaussian(rng, dims, deviation, most, cuts=(), kind=jnp.bfloat16):
    factor_of = block_scale(rng, dims, cuts, -0.22, 0.18) if cuts else 1.0
    values = jax.random.normal(rng, dims, jnp.float32) * deviation * factor_of
    return jnp.minimum(jnp.maximum(values, -most), most).astype(kind)


def setup_inputs(seed: int = 0) -> dict:
    splits = jax.random.split(jax.random.key(seed), 22)
    tokens = gaussian(splits[0], (TOKENS, MODEL_WIDTH), 1.0, 6.0, ((0, 128),))
    segments = draw_segments(jax.random.fold_in(splits[21], 71), 0)
    cotangent = gaussian(splits[2], (TOKENS, MODEL_WIDTH), 1.0, 6.0, ((0, 128),))
    attention_gain = jnp.clip(1.0 + 0.1 * jax.random.normal(splits[3], (MODEL_WIDTH,), jnp.float32), 0.5, 1.5)
    query_weight = gaussian(splits[4], (MODEL_WIDTH, QUERY_HEADS * HEAD_WIDTH), MODEL_WIDTH ** -0.5, 0.1875, ((0, 16),))
    key_matrix = gaussian(splits[5], (MODEL_WIDTH, KEY_VALUE_HEADS * HEAD_WIDTH), MODEL_WIDTH ** -0.5, 0.1875, ((0, 16),))
    value_matrix = gaussian(splits[6], (MODEL_WIDTH, KEY_VALUE_HEADS * HEAD_WIDTH), MODEL_WIDTH ** -0.5, 0.1875, ((0, 16),))
    attention_out = gaussian(splits[7], (QUERY_HEADS * HEAD_WIDTH, MODEL_WIDTH), 4 ** -0.5, 3.0, ((0, 16),))
    gate_weight = gaussian(splits[8], (MODEL_WIDTH, MH * MP), MODEL_WIDTH ** -0.5, 0.1875, ((0, 16),))
    mixer_weight = gaussian(splits[9], (MODEL_WIDTH, MH * MP + 2 * NS), MODEL_WIDTH ** -0.5, 0.1875, ((0, 16),))
    step_weight = gaussian(splits[10], (MODEL_WIDTH, MH), MODEL_WIDTH ** -0.5, 0.1875, ((0, 16),))
    mixer_out = gaussian(splits[11], (MH * MP, MODEL_WIDTH), (MH * MP // 8) ** -0.5, 0.4375, ((0, 16),))
    conv_weight = gaussian(splits[12], (KC, MH * MP + 2 * NS), 0.5, 3.0, (), jnp.float32)
    conv_bias = gaussian(splits[13], (MH * MP + 2 * NS,), 0.3, 3.0, (), jnp.float32)
    step_bias = jnp.clip(jax.random.uniform(splits[14], (MH,), jnp.float32, -4.0, -1.0), -4.0, -1.0)
    decay_log = jnp.clip(jax.random.uniform(splits[15], (MH,), jnp.float32, -3.0, 1.0), -3.0, 1.0)
    skip_gain = jnp.clip(jax.random.uniform(splits[16], (MH,), jnp.float32, 0.5, 1.5), 0.5, 1.5)
    feed_gain = jnp.clip(1.0 + 0.1 * jax.random.normal(splits[17], (MODEL_WIDTH,), jnp.float32), 0.5, 1.5)
    feed_gate = gaussian(splits[18], (MODEL_WIDTH, FF), MODEL_WIDTH ** -0.5, 0.1875, ((0, 16),))
    feed_up = gaussian(splits[19], (MODEL_WIDTH, FF), MODEL_WIDTH ** -0.5, 0.1875, ((0, 16),))
    feed_down = gaussian(splits[20], (FF, MODEL_WIDTH), FF ** -0.5, 0.125, ((0, 16),))
    return dict(tokens=tokens, segments=segments, cotangent=cotangent, attention_gain=attention_gain, query_weight=query_weight, key_matrix=key_matrix, value_matrix=value_matrix, attention_out=attention_out, gate_weight=gate_weight, mixer_weight=mixer_weight, step_weight=step_weight, mixer_out=mixer_out, conv_weight=conv_weight, conv_bias=conv_bias, step_bias=step_bias, decay_log=decay_log, skip_gain=skip_gain, feed_gain=feed_gain, feed_gate=feed_gate, feed_up=feed_up, feed_down=feed_down)


@jax.custom_vjp
def low(v):
    return lax.optimization_barrier(v.astype(jnp.bfloat16)).astype(jnp.float32)

@jax.custom_vjp
def low_back(v):
    return v

def low_keep(v):
    return (low(v), None)

def low_pass(kept, grad):
    return (grad,)

def back_keep(v):
    return (v, None)

def back_low(kept, grad):
    return (low(grad),)
low.defvjp(low_keep, low_pass)
low_back.defvjp(back_keep, back_low)
EPSILON = 1e-05
masked_fill = -1e+30
attention_multiplier = 0.9375
mixer_multiplier = 0.2357
rotary_base = 100000000000.0

def matmul(left, right):
    return jnp.dot(left, right, precision=lax.Precision.HIGHEST, preferred_element_type=jnp.float32)

def rms_norm(values, gain_vector):
    return values * lax.rsqrt(lax.optimization_barrier(jnp.mean(values * values, axis=-1, keepdims=True)) + EPSILON) * gain_vector

def rotary(values, places, direction):
    count_of_rows = values.shape[0]
    head_count = values.shape[1] // HEAD_WIDTH
    half_size = HEAD_WIDTH // 2
    frequency = rotary_base ** (-2.0 * jnp.arange(half_size, dtype=jnp.float32) / HEAD_WIDTH)
    angles = places[:, None] * frequency[None, :]
    cosine = jnp.cos(angles)[:, None, :]
    sine_part = direction * jnp.sin(angles)[:, None, :]
    per_head = values.reshape(count_of_rows, head_count, HEAD_WIDTH)
    front_half = per_head[:, :, :half_size]
    back_half = per_head[:, :, half_size:]
    turned = jnp.concatenate([front_half * cosine - back_half * sine_part, back_half * cosine + front_half * sine_part], axis=-1)
    return turned.reshape(count_of_rows, head_count * HEAD_WIDTH)

def mixer_inputs(extended, seg_extended, seg_own, conv_taps, conv_shift, step_raw, step_shift, decay_logs):
    count_of_rows = seg_own.shape[0]
    mixed = conv_shift[None, :]
    for tap_index in range(conv_taps.shape[0]):
        same_doc = (seg_extended[tap_index:tap_index + count_of_rows] == seg_own).astype(jnp.float32)
        mixed = mixed + conv_taps[tap_index][None, :] * extended[tap_index:tap_index + count_of_rows] * same_doc[:, None]
    activated = jax.nn.silu(mixed)
    step_size = jax.nn.softplus(step_raw + step_shift[None, :])
    log_rate = step_size * (-jnp.exp(decay_logs))[None, :]
    return (activated, step_size, log_rate)

def decay_terms(log_rate, seg_own, seg_before):
    count_of_rows = log_rate.shape[0]
    running = jnp.cumsum(log_rate, axis=0)
    index_rows = jnp.arange(count_of_rows)
    allowed = (index_rows[:, None] >= index_rows[None, :]) & (seg_own[:, None] == seg_own[None, :])
    gaps = running.T[:, :, None] - running.T[:, None, :]
    within = jnp.exp(jnp.where(allowed[None], gaps, masked_fill))
    entry = jnp.exp(running) * (seg_own == seg_before).astype(jnp.float32)[:, None]
    leaving = jnp.exp(running[-1][None, :] - running) * (seg_own == seg_own[-1]).astype(jnp.float32)[:, None]
    carried = jnp.exp(running[-1]) * (seg_own[-1] == seg_before).astype(jnp.float32)
    return (within, entry, leaving, carried)

def mixer_block(state, pieces):
    rates, seg_block, seg_before, bees, seas, inputs_low = pieces
    within, entry, leaving, carried = decay_terms(rates, seg_block, seg_before)
    intersection = low_back(jnp.einsum('in,jn->ij', seas, bees, precision=lax.Precision.HIGHEST))
    mixing = low(intersection[None] * within)
    inner = jnp.einsum('hij,jhp->ihp', mixing, inputs_low, precision=lax.Precision.HIGHEST)
    from_state = low_back(jnp.einsum('in,hnp->ihp', seas, low(state), precision=lax.Precision.HIGHEST))
    weighted = low(bees[:, None, :] * leaving[:, :, None])
    local_state = low_back(jnp.einsum('jhn,jhp->hnp', weighted, inputs_low, precision=lax.Precision.HIGHEST))
    new_state = carried[:, None, None] * state + local_state
    return (new_state, inner + from_state * entry[:, :, None])

def layer(params, hidden_in, seg_float):
    attention_gain, query_weight, key_matrix, value_matrix, attention_out, gate_weight, mixer_weight, step_weight, mixer_out, conv_weight, conv_bias, step_bias, decay_log, skip_gain, feed_gain, feed_gate, feed_up, feed_down = params
    sequence_length = hidden_in.shape[0]
    places = jnp.arange(sequence_length, dtype=jnp.float32)
    place_index = jnp.arange(sequence_length)
    normed = low(rms_norm(hidden_in, attention_gain))
    query_lin = low_back(matmul(normed, query_weight))
    key_lin = low_back(matmul(normed, key_matrix))
    value_lin = low_back(matmul(normed, value_matrix))
    rotated_queries = low(rotary(query_lin, places, 1.0))
    rotated_keys = low(rotary(key_lin, places, 1.0))
    value_reduced = low(value_lin)
    heads_of_queries = rotated_queries.reshape(sequence_length, KEY_VALUE_HEADS, QUERY_HEADS // KEY_VALUE_HEADS, HEAD_WIDTH)
    heads_of_keys = rotated_keys.reshape(sequence_length, KEY_VALUE_HEADS, HEAD_WIDTH)
    heads_of_values = value_reduced.reshape(sequence_length, KEY_VALUE_HEADS, HEAD_WIDTH)
    raw_scores = low_back(jnp.einsum('rgqd,lgd->gqrl', heads_of_queries, heads_of_keys, precision=lax.Precision.HIGHEST) * (1.0 / math.sqrt(HEAD_WIDTH)))
    allowed = (place_index[None, :] <= place_index[:, None]) & (seg_float[None, :] == seg_float[:, None])
    scores = jnp.where(allowed[None, None], raw_scores, masked_fill)
    probs = low(jax.nn.softmax(scores, axis=-1))
    attended = low(low_back(jnp.einsum('gqrl,lgd->rgqd', probs, heads_of_values, precision=lax.Precision.HIGHEST).reshape(sequence_length, QUERY_HEADS * HEAD_WIDTH)))
    attention_branch = low_back(matmul(attended, attention_out))
    gate_lin = low_back(matmul(normed, gate_weight))
    mixer_lin = low_back(matmul(normed, mixer_weight))
    step_lin = low_back(matmul(normed, step_weight))
    tap_count = conv_weight.shape[0]
    extended = jnp.concatenate([jnp.zeros((tap_count - 1, mixer_lin.shape[1]), jnp.float32), mixer_lin], axis=0)
    seg_extended = jnp.concatenate([jnp.zeros((tap_count - 1,), jnp.float32), seg_float])
    activated, step_size, log_rate = mixer_inputs(extended, seg_extended, seg_float, conv_weight, conv_bias, step_lin, step_bias, decay_log)
    inner_width = MH * MP
    mixer_x = activated[:, :inner_width].reshape(sequence_length, MH, MP)
    bees = low(activated[:, inner_width:inner_width + NS])
    seas = low(activated[:, inner_width + NS:])
    inputs_low = low(mixer_x * step_size[:, :, None])
    block_count = sequence_length // ROWS
    seg_blocks = seg_float.reshape(block_count, ROWS)
    seg_befores = jnp.concatenate([jnp.zeros((1,), jnp.float32), seg_blocks[:-1, -1]])
    pieces = (log_rate.reshape(block_count, ROWS, MH), seg_blocks, seg_befores, bees.reshape(block_count, ROWS, NS), seas.reshape(block_count, ROWS, NS), inputs_low.reshape(block_count, ROWS, MH, MP))
    last_state, block_outs = lax.scan(jax.checkpoint(mixer_block), jnp.zeros((MH, NS, MP), jnp.float32), pieces)
    scanned = low_back(block_outs.reshape(sequence_length, MH, MP) + skip_gain[None, :, None] * mixer_x)
    gated = low(scanned.reshape(sequence_length, inner_width) * jax.nn.silu(gate_lin))
    mixer_branch = low_back(matmul(gated, mixer_out))
    residual = hidden_in + attention_multiplier * attention_branch + mixer_multiplier * mixer_branch
    normed_two = low(rms_norm(residual, feed_gain))
    ffn_gate_lin = low_back(matmul(normed_two, feed_gate))
    ffn_up_lin = low_back(matmul(normed_two, feed_up))
    hidden_low = low(jax.nn.silu(ffn_gate_lin) * ffn_up_lin)
    return residual + low_back(matmul(hidden_low, feed_down))

def reference(tokens, segments, cotangent, attention_gain, query_weight, key_matrix, value_matrix, attention_out, gate_weight, mixer_weight, step_weight, mixer_out, conv_weight, conv_bias, step_bias, decay_log, skip_gain, feed_gain, feed_gate, feed_up, feed_down):
    weights = (attention_gain, query_weight, key_matrix, value_matrix, attention_out, gate_weight, mixer_weight, step_weight, mixer_out, conv_weight, conv_bias, step_bias, decay_log, skip_gain, feed_gain, feed_gate, feed_up, feed_down)
    params = jax.tree.map(lambda leaf_value: leaf_value.astype(jnp.float32), weights)
    hidden_all = tokens.astype(jnp.float32).reshape(N_DP, SEQ_LEN, MODEL_WIDTH)
    seg_all = segments.astype(jnp.float32).reshape(N_DP, SEQ_LEN)
    upstream_all = cotangent.astype(jnp.float32).reshape(N_DP, SEQ_LEN, MODEL_WIDTH)

    def per_sequence(totals, pieces):
        hidden_in, seg_float, upstream = pieces

        def closed(param_set, hidden_values):
            return layer(param_set, hidden_values, seg_float)
        result, pullback = jax.vjp(closed, params, hidden_in)
        grad_params, grad_hidden = pullback(upstream)
        totals = jax.tree.map(lambda left_sum, right_sum: left_sum + right_sum, totals, grad_params)
        return (totals, (result.astype(jnp.bfloat16), grad_hidden))
    zero_grads = jax.tree.map(jnp.zeros_like, params)
    totals, (results, grad_hidden_all) = lax.scan(per_sequence, zero_grads, (hidden_all, seg_all, upstream_all))
    return (results.reshape(TOKENS, MODEL_WIDTH), grad_hidden_all.reshape(TOKENS, MODEL_WIDTH), totals[0], totals[1], totals[2], totals[3], totals[4], totals[5], totals[6], totals[7], totals[8], totals[9], totals[10], totals[11], totals[12], totals[13], totals[14], totals[15], totals[16], totals[17])
```

```python
import math

import jax
import jax.numpy as jnp
from jax import lax
from jax.sharding import PartitionSpec as P

QUERY_HEADS = 8
KEY_VALUE_HEADS = 2
HEAD_WIDTH = 64
MH = 24
MP = 64
NS = 128


EPSILON = 1e-05
masked_fill = -1e30
attention_multiplier = 0.9375
mixer_multiplier = 0.2357
rotary_base = 100000000000.0
IN_USED = 4120
IN_WIDTH = 4352
CHIP_GROUPS = [[2 * z + c for z in range(4)] for c in range(2)]
CORE_GROUPS = [[8 * d + 2 * z + c for d in range(16) for z in range(4)] for c in range(2)]


def from_behind(block, axis, distance):
    devices = range(lax.axis_size(axis))
    route = [(i - distance, i) for i in devices if i - distance in devices]
    return lax.ppermute(block, axis, route)


def swap_cores(block):
    devices = range(lax.axis_size("context"))
    return lax.ppermute(block, "context", [(i, i ^ 1) for i in devices])


def shift_chips(block, distance):
    devices = lax.axis_size("context")
    return lax.ppermute(
        block, "context", [(i, (i + 2 * distance) % devices) for i in range(devices)]
    )


def shift_rows(block, distance, stride):
    route = []
    for i in range(16):
        place = i // stride % 4
        route.append((i, i + ((place + distance) % 4 - place) * stride))
    return lax.ppermute(block, "dp", route)


def sum_of_four(block, shift):
    one, two, three = shift(block, 1), shift(block, 2), shift(block, 3)
    return (block + two) + (one + three)


def sum_everywhere(block):
    block = block + swap_cores(block)
    block = sum_of_four(block, shift_chips)
    block = sum_of_four(block, lambda part, k: shift_rows(part, k, 1))
    return sum_of_four(block, lambda part, k: shift_rows(part, k, 4))


def half(block, which, axis):
    size = block.shape[axis] // 2
    return lax.dynamic_slice_in_dim(block, which * size, size, axis)


def copies_of(block):
    devices = lax.axis_size("context")
    return lax.all_to_all(
        jnp.broadcast_to(block[None], (devices,) + block.shape), "context", 0, 0
    )


def carried_in(carried, local, reverse):
    mine = lax.axis_index("context")
    core, chip = mine % 2, mine // 2
    is_first = (core == 1) if reverse else (core == 0)
    order = 3 - chip if reverse else chip
    way = -1 if reverse else 1
    decay_other = swap_cores(carried)
    own_part, own_decay = half(local, core, 0), half(carried, core, 0)
    got_part = swap_cores(half(local, 1 - core, 0).astype(jnp.bfloat16)).astype(jnp.float32)
    got_decay = half(decay_other, core, 0)
    first = jnp.where(is_first, own_part, got_part)
    second = jnp.where(is_first, got_part, own_part)
    first_decay = jnp.where(is_first, own_decay, got_decay)
    second_decay = jnp.where(is_first, got_decay, own_decay)
    if reverse:
        chip_part = first * second_decay[:, None, None] + second
    else:
        chip_part = first * second_decay[:, None, None] + second
    chip_low = chip_part.astype(jnp.bfloat16)
    chip_decay = first_decay * second_decay
    total = jnp.zeros_like(first)
    factor = jnp.ones_like(chip_decay)
    for k in range(1, 4):
        part = shift_chips(chip_low, way * k).astype(jnp.float32)
        reach = jnp.where(order >= k, factor, 0.0)
        total = total + reach[:, None, None] * part
        if k < 3:
            factor = factor * shift_chips(chip_decay, way * k)
    for_first = total
    for_second = total * first_decay[:, None, None] + first
    keep = jnp.where(is_first, for_first, for_second)
    give = jnp.where(is_first, for_second, for_first)
    got = swap_cores(give.astype(jnp.bfloat16))
    keep = keep.astype(jnp.bfloat16)
    return jnp.where(
        core == 0, jnp.concatenate([keep, got], axis=0), jnp.concatenate([got, keep], axis=0)
    )


def rms_norm(values, gain_vector):
    return (
        values
        * lax.rsqrt(jnp.mean(values * values, axis=-1, keepdims=True) + EPSILON)
        * gain_vector
    )


def rotary(values, places, direction):
    count_of_rows = values.shape[0]
    head_count = values.shape[1] // HEAD_WIDTH
    half_size = HEAD_WIDTH // 2
    frequency = rotary_base ** (-2.0 * jnp.arange(half_size, dtype=jnp.float32) / HEAD_WIDTH)
    angles = places[:, None] * frequency[None, :]
    cosine = jnp.cos(angles)[:, None, :]
    sine_part = direction * jnp.sin(angles)[:, None, :]
    per_head = values.reshape(count_of_rows, head_count, HEAD_WIDTH)
    front_half = per_head[:, :, :half_size]
    back_half = per_head[:, :, half_size:]
    turned = jnp.concatenate(
        [front_half * cosine - back_half * sine_part, back_half * cosine + front_half * sine_part],
        axis=-1,
    )
    return turned.reshape(count_of_rows, head_count * HEAD_WIDTH)


def mixer_inputs(
    extended, seg_extended, seg_own, conv_taps, conv_shift, step_raw, step_shift, decay_logs
):
    count_of_rows = seg_own.shape[0]
    mixed = conv_shift[None, :]
    for tap_index in range(conv_taps.shape[0]):
        same_doc = (seg_extended[tap_index : tap_index + count_of_rows] == seg_own).astype(
            jnp.float32
        )
        mixed = (
            mixed
            + conv_taps[tap_index][None, :]
            * extended[tap_index : tap_index + count_of_rows]
            * same_doc[:, None]
        )
    activated = jax.nn.silu(mixed)
    step_size = jax.nn.softplus(step_raw + step_shift[None, :])
    log_rate = step_size * (-jnp.exp(decay_logs))[None, :]
    return (activated, step_size, log_rate)


def decay_terms(log_rate, seg_own, seg_before):
    count_of_rows = log_rate.shape[0]
    running = jnp.cumsum(log_rate, axis=0)
    index_rows = jnp.arange(count_of_rows)
    allowed = (index_rows[:, None] >= index_rows[None, :]) & (seg_own[:, None] == seg_own[None, :])
    gaps = running.T[:, :, None] - running.T[:, None, :]
    within = jnp.exp(jnp.where(allowed[None], gaps, masked_fill))
    entry = jnp.exp(running) * (seg_own == seg_before).astype(jnp.float32)[:, None]
    leaving = (
        jnp.exp(running[-1][None, :] - running)
        * (seg_own == seg_own[-1]).astype(jnp.float32)[:, None]
    )
    carried = jnp.exp(running[-1]) * (seg_own[-1] == seg_before).astype(jnp.float32)
    return (within, entry, leaving, carried)


def attention_scores(rotated_queries, every_key, query_places, key_places, seg_own, seg_all):
    count_of_rows = rotated_queries.shape[0]
    count_of_keys = every_key.shape[0]
    heads_of_queries = rotated_queries.reshape(
        count_of_rows, KEY_VALUE_HEADS, QUERY_HEADS // KEY_VALUE_HEADS, HEAD_WIDTH
    )
    heads_of_keys = every_key.reshape(count_of_keys, KEY_VALUE_HEADS, HEAD_WIDTH)
    raw_scores = jnp.einsum(
        "rgqd,lgd->gqrl", heads_of_queries, heads_of_keys, preferred_element_type=jnp.float32
    ) * (1.0 / math.sqrt(HEAD_WIDTH))
    allowed = (key_places[None, :] <= query_places[:, None]) & (
        seg_all[None, :] == seg_own[:, None]
    )
    return jnp.where(allowed[None, None], raw_scores, masked_fill)


def chain_forward(earlier, later):
    return (earlier[0] * later[0], later[0][:, None, None] * earlier[1] + later[1])


def chain_backward(earlier, later):
    return (earlier[0] * later[0], later[1] + later[0][:, None, None] * earlier[1])


def project(left, right):
    return jnp.dot(left, right, preferred_element_type=jnp.float32)


def input_grad(left, right):
    return jnp.einsum("rk,rj->kj", left, right, preferred_element_type=jnp.float32)


def back_through(grad_low, weight_full):
    return jnp.einsum("rj,kj->rk", grad_low, weight_full, preferred_element_type=jnp.float32)


def swiglu(gate_values, up_values):
    return jax.nn.silu(gate_values) * up_values


def gating(scan_values, gate_values):
    return scan_values * jax.nn.silu(gate_values)


def on_device(
    tokens,
    segments,
    cotangent,
    attention_gain,
    query_weight,
    key_matrix,
    value_matrix,
    attention_out,
    gate_weight,
    mixer_weight,
    step_weight,
    mixer_out,
    conv_weight,
    conv_bias,
    step_bias,
    decay_log,
    skip_gain,
    feed_gain,
    feed_gate,
    feed_up,
    feed_down,
):
    block_index = lax.axis_index("context")
    core = block_index % 2
    chip = block_index // 2
    both = ("dp", "context")
    step_padded = jnp.pad(step_weight, ((0, 0), (0, IN_WIDTH - IN_USED)))
    in_shard = jnp.concatenate(
        [query_weight, key_matrix, value_matrix, gate_weight, mixer_weight, step_padded], axis=1
    )
    in_full = lax.all_gather(
        lax.dynamic_slice_in_dim(in_shard, block_index * 8, 8, 0), both, axis=0, tiled=True
    )
    feed_shard = lax.dynamic_slice_in_dim(
        jnp.concatenate([feed_gate, feed_up], axis=1), block_index * 8, 8, 0
    )
    out_shard = lax.dynamic_slice_in_dim(
        jnp.concatenate([attention_out, mixer_out, feed_down], axis=0), block_index * 32, 32, 0
    )
    out_shard = out_shard.reshape(4, 8, 1024).transpose(1, 0, 2).reshape(8, 4096)
    late_full = lax.all_gather(
        jnp.concatenate([feed_shard, out_shard], axis=1), both, axis=0, tiled=True
    )
    feed_full = late_full[:, :4096]
    out_parts = late_full[:, 4096:].reshape(16, 8, 8, 4, 1024).transpose(0, 1, 3, 2, 4)
    out_full = out_parts[:, 0].reshape(512, 1024)
    mixer_out_full = out_parts[:, 1:4].reshape(1536, 1024)
    ffn_down_full = out_parts[:, 4:].reshape(2048, 1024)
    count_of_rows = tokens.shape[0]
    tap_count = conv_weight.shape[0]
    inner_width = MH * MP
    width_of_keys = KEY_VALUE_HEADS * HEAD_WIDTH
    query_places = block_index * count_of_rows + jnp.arange(count_of_rows, dtype=jnp.int32)
    place_float = query_places.astype(jnp.float32)
    seg_float = segments.astype(jnp.float32)
    seg_low = segments.astype(jnp.bfloat16)
    hidden_in = tokens.astype(jnp.float32)
    normed, norm_one_back = jax.vjp(rms_norm, hidden_in, attention_gain)
    normed_low = normed.astype(jnp.bfloat16)
    every_lin = project(normed_low, in_full)
    query_lin = every_lin[:, :512]
    key_lin = every_lin[:, 512:640]
    value_lin = every_lin[:, 640:768]
    gate_lin = every_lin[:, 768:2304]
    mixer_lin = every_lin[:, 2304:4096]
    step_lin = every_lin[:, 4096:IN_USED]
    rotated_queries = rotary(query_lin, place_float, 1.0).astype(jnp.bfloat16)
    rotated_keys = rotary(key_lin, place_float, 1.0).astype(jnp.bfloat16)
    value_reduced = value_lin.astype(jnp.bfloat16)
    sent = jnp.concatenate(
        [
            jnp.concatenate([rotated_keys, value_reduced], axis=1),
            jnp.pad(seg_low[None, :], ((0, 7), (0, 0))),
        ],
        axis=0,
    )
    along = jnp.stack([sent] + [shift_chips(sent, k) for k in range(1, 4)])
    slots = jnp.concatenate([along, swap_cores(along)], axis=0)
    every_key = slots[:, :count_of_rows, :width_of_keys].reshape(-1, width_of_keys)
    every_value = slots[:, :count_of_rows, width_of_keys:].reshape(-1, width_of_keys)
    seg_all = slots[:, count_of_rows].reshape(-1)
    owners = jnp.concatenate(
        [(chip - jnp.arange(4)) % 4 * 2 + core, (chip - jnp.arange(4)) % 4 * 2 + 1 - core]
    )
    key_places = (
        owners[:, None] * count_of_rows + jnp.arange(count_of_rows, dtype=jnp.int32)[None, :]
    ).reshape(-1)
    heads_of_keys = every_key.reshape(-1, KEY_VALUE_HEADS, HEAD_WIDTH)
    heads_of_values = every_value.reshape(-1, KEY_VALUE_HEADS, HEAD_WIDTH)
    heads_of_queries = rotated_queries.reshape(
        count_of_rows, KEY_VALUE_HEADS, QUERY_HEADS // KEY_VALUE_HEADS, HEAD_WIDTH
    )
    scores = attention_scores(
        rotated_queries, every_key, query_places, key_places, seg_low, seg_all
    )
    top_score = jnp.max(scores, axis=-1, keepdims=True)
    exponent = jnp.exp(scores - top_score)
    totals = jnp.sum(exponent, axis=-1, keepdims=True)
    probs_low = (exponent / totals).astype(jnp.bfloat16)
    log_total = top_score + jnp.log(totals)
    attended = jnp.einsum(
        "gqrl,lgd->rgqd", probs_low, heads_of_values, preferred_element_type=jnp.float32
    )
    attended_low = attended.reshape(count_of_rows, QUERY_HEADS * HEAD_WIDTH).astype(jnp.bfloat16)
    attention_branch = project(attended_low, out_full)
    prev_rows, prev_segs = from_behind(
        (mixer_lin[count_of_rows - tap_count + 1 :], seg_float[count_of_rows - tap_count + 1 :]),
        "context",
        1,
    )
    extended = jnp.concatenate([prev_rows, mixer_lin], axis=0)
    seg_extended = jnp.concatenate([prev_segs, seg_float])
    seg_before = prev_segs[-1]

    def mixer_piece(ext_rows, conv_taps, conv_shift, step_raw, step_shift, decay_logs):
        return mixer_inputs(
            ext_rows,
            seg_extended,
            seg_float,
            conv_taps,
            conv_shift,
            step_raw,
            step_shift,
            decay_logs,
        )

    (activated, step_size, log_rate), mixer_back = jax.vjp(
        mixer_piece, extended, conv_weight, conv_bias, step_lin, step_bias, decay_log
    )
    mixer_x = activated[:, :inner_width].reshape(count_of_rows, MH, MP)
    bees = activated[:, inner_width : inner_width + NS].astype(jnp.bfloat16)
    seas = activated[:, inner_width + NS :].astype(jnp.bfloat16)
    inputs_low = (mixer_x * step_size[:, :, None]).astype(jnp.bfloat16)

    def decay_piece(rates):
        return decay_terms(rates, seg_float, seg_before)

    (within, entry, leaving, carried), decay_back = jax.vjp(decay_piece, log_rate)
    intersection = jnp.einsum("in,jn->ij", seas, bees, preferred_element_type=jnp.float32)
    mixing_low = (intersection[None] * within).astype(jnp.bfloat16)
    inner = jnp.einsum("hij,jhp->ihp", mixing_low, inputs_low, preferred_element_type=jnp.float32)
    weighted_low = (bees.astype(jnp.float32)[:, None, :] * leaving[:, :, None]).astype(jnp.bfloat16)
    local_state = jnp.einsum(
        "jhn,jhp->hnp", weighted_low, inputs_low, preferred_element_type=jnp.float32
    )
    incoming_low = carried_in(carried, local_state, False)
    from_state = jnp.einsum("in,hnp->ihp", seas, incoming_low, preferred_element_type=jnp.float32)
    scanned = inner + from_state * entry[:, :, None] + skip_gain[None, :, None] * mixer_x
    gated, gating_back = jax.vjp(gating, scanned.reshape(count_of_rows, inner_width), gate_lin)
    gated_low = gated.astype(jnp.bfloat16)
    mixer_branch = project(gated_low, mixer_out_full)
    residual = hidden_in + attention_multiplier * attention_branch + mixer_multiplier * mixer_branch
    normed_two, norm_two_back = jax.vjp(rms_norm, residual, feed_gain)
    normed_two_low = normed_two.astype(jnp.bfloat16)
    feed_lin = project(normed_two_low, feed_full)
    ffn_gate_lin = feed_lin[:, :2048]
    ffn_up_lin = feed_lin[:, 2048:]
    hidden_act, swiglu_back = jax.vjp(swiglu, ffn_gate_lin, ffn_up_lin)
    hidden_low = hidden_act.astype(jnp.bfloat16)
    output = (residual + project(hidden_low, ffn_down_full)).astype(jnp.bfloat16)
    upstream = cotangent.astype(jnp.float32)
    d_hidden = back_through(cotangent, ffn_down_full)
    d_ffn_gate, d_ffn_up = swiglu_back(d_hidden)
    d_feed_low = jnp.concatenate([d_ffn_gate, d_ffn_up], axis=1).astype(jnp.bfloat16)
    d_normed_two = back_through(d_feed_low, feed_full)
    d_resid_norm, grad_feed_gain = norm_two_back(d_normed_two)
    d_residual = upstream + d_resid_norm
    d_attn_low = (attention_multiplier * d_residual).astype(jnp.bfloat16)
    d_mixer_low = (mixer_multiplier * d_residual).astype(jnp.bfloat16)

    def early_grads(which):
        feed = input_grad(normed_two_low, half(d_feed_low, which, 1)).astype(jnp.bfloat16)
        attn = input_grad(attended_low, half(d_attn_low, which, 1)).astype(jnp.bfloat16)
        mix = input_grad(gated_low, half(d_mixer_low, which, 1)).astype(jnp.bfloat16)
        down = input_grad(hidden_low, half(cotangent, which, 1)).astype(jnp.bfloat16)
        return (feed, attn, mix, down)

    early_got = jax.tree.map(swap_cores, early_grads(1 - core))
    early = jax.tree.map(lambda a, b: a + b, early_grads(core), early_got)
    early_rows = jnp.concatenate(
        [
            early[1].reshape(16, 32, 512),
            early[2].reshape(16, 96, 512),
            early[3].reshape(16, 128, 512),
            early[0].reshape(16, 64, 4, 512).transpose(0, 2, 1, 3).reshape(16, 256, 512),
        ],
        axis=1,
    )
    early_shard = lax.psum_scatter(
        early_rows.reshape(16 * 512, 512), "dp", scatter_dimension=0, tiled=True
    )
    early_parts = lax.all_to_all(
        early_shard.reshape(4, 128, 512), "context", 0, 0, axis_index_groups=CHIP_GROUPS
    )
    early_sum = jnp.sum(early_parts.astype(jnp.float32), axis=0).astype(jnp.bfloat16)
    early_all = copies_of(early_sum).reshape(4, 2, 128, 512).astype(jnp.float32)
    early_out = early_all[:2].transpose(0, 2, 1, 3).reshape(256, 1024)
    early_feed = early_all[2:].transpose(1, 0, 2, 3).reshape(2, 4, 64, 512)
    early_feed = early_feed.transpose(0, 2, 1, 3).reshape(2, 64, 2048)
    attended_gradient = back_through(d_attn_low, out_full).astype(jnp.bfloat16)
    d_gated = back_through(d_mixer_low, mixer_out_full)
    scale_factor = 1.0 / math.sqrt(HEAD_WIDTH)
    scores_again = attention_scores(
        rotated_queries, every_key, query_places, key_places, seg_low, seg_all
    )
    probs_again = jnp.exp(scores_again - log_total)
    probs_again_low = probs_again.astype(jnp.bfloat16)
    output_heads_gradient = attended_gradient.reshape(
        count_of_rows, KEY_VALUE_HEADS, QUERY_HEADS // KEY_VALUE_HEADS, HEAD_WIDTH
    )
    d_probs = jnp.einsum(
        "rgqd,lgd->gqrl", output_heads_gradient, heads_of_values, preferred_element_type=jnp.float32
    )
    delta_sum = jnp.sum(probs_again * d_probs, axis=-1, keepdims=True)
    d_scores_low = (probs_again * (d_probs - delta_sum)).astype(jnp.bfloat16)
    d_query_rot = (
        jnp.einsum(
            "gqrl,lgd->rgqd", d_scores_low, heads_of_keys, preferred_element_type=jnp.float32
        ).reshape(count_of_rows, QUERY_HEADS * HEAD_WIDTH)
        * scale_factor
    )
    d_keys = (
        jnp.einsum(
            "gqrl,rgqd->lgd", d_scores_low, heads_of_queries, preferred_element_type=jnp.float32
        ).reshape(count_of_rows * lax.axis_size("context"), width_of_keys)
        * scale_factor
    )
    d_values = jnp.einsum(
        "gqrl,rgqd->lgd", probs_again_low, output_heads_gradient, preferred_element_type=jnp.float32
    ).reshape(count_of_rows * lax.axis_size("context"), width_of_keys)
    slot_grads = jnp.concatenate([d_keys, d_values], axis=1).astype(jnp.bfloat16)
    slot_grads = slot_grads.reshape(2, 4, count_of_rows, 2 * width_of_keys)
    chip_grads = slot_grads[0].astype(jnp.float32) + swap_cores(slot_grads[1]).astype(jnp.float32)
    chip_low = chip_grads.astype(jnp.bfloat16)
    key_grads = chip_grads[0]
    for k in range(1, 4):
        key_grads = key_grads + shift_chips(chip_low[k], -k).astype(jnp.float32)
    d_query_low = rotary(d_query_rot, place_float, -1.0).astype(jnp.bfloat16)
    d_key_low = rotary(key_grads[:, :width_of_keys], place_float, -1.0).astype(jnp.bfloat16)
    d_value_low = key_grads[:, width_of_keys:].astype(jnp.bfloat16)
    d_scan_flat, d_gate_lin = gating_back(d_gated)
    d_scan_low = d_scan_flat.reshape(count_of_rows, MH, MP).astype(jnp.bfloat16)
    d_scan = d_scan_low.astype(jnp.float32)
    grad_skip_gain = jnp.sum(d_scan * mixer_x, axis=(0, 2))
    d_mixer_x = skip_gain[None, :, None] * d_scan
    d_entry = jnp.sum(d_scan * from_state, axis=2)
    d_from_low = (d_scan * entry[:, :, None]).astype(jnp.bfloat16)
    d_seas = jnp.einsum("ihp,hnp->in", d_from_low, incoming_low, preferred_element_type=jnp.float32)
    d_incoming = jnp.einsum("in,ihp->hnp", seas, d_from_low, preferred_element_type=jnp.float32)
    d_mixing = jnp.einsum(
        "ihp,jhp->hij", d_scan_low, inputs_low, preferred_element_type=jnp.float32
    )
    d_inputs = jnp.einsum(
        "hij,ihp->jhp", mixing_low, d_scan_low, preferred_element_type=jnp.float32
    )
    d_intersection_low = jnp.sum(d_mixing * within, axis=0).astype(jnp.bfloat16)
    d_within = d_mixing * intersection[None]
    d_seas = d_seas + jnp.einsum(
        "ij,jn->in", d_intersection_low, bees, preferred_element_type=jnp.float32
    )
    d_bees = jnp.einsum("ij,in->jn", d_intersection_low, seas, preferred_element_type=jnp.float32)
    d_state_low = carried_in(carried, d_incoming, True)
    d_carried = jnp.sum(
        d_state_low.astype(jnp.float32) * incoming_low.astype(jnp.float32), axis=(1, 2)
    )
    d_weighted = jnp.einsum(
        "jhp,hnp->jhn", inputs_low, d_state_low, preferred_element_type=jnp.float32
    )
    d_inputs = d_inputs + jnp.einsum(
        "jhn,hnp->jhp", weighted_low, d_state_low, preferred_element_type=jnp.float32
    )
    d_bees = d_bees + jnp.sum(d_weighted * leaving[:, :, None], axis=1)
    d_leaving = jnp.sum(d_weighted * bees.astype(jnp.float32)[:, None, :], axis=2)
    (d_rate,) = decay_back((d_within, d_entry, d_leaving, d_carried))
    d_mixer_x = d_mixer_x + d_inputs * step_size[:, :, None]
    d_step = jnp.sum(d_inputs * mixer_x, axis=2)
    d_activated = jnp.concatenate(
        [d_mixer_x.reshape(count_of_rows, inner_width), d_bees, d_seas], axis=1
    )
    d_extended, grad_conv_weight, grad_conv_bias, d_step_lin, grad_step_bias, grad_decay_log = (
        mixer_back((d_activated, d_step, d_rate))
    )
    rim_back = from_behind(d_extended[: tap_count - 1], "context", -1)
    d_mixer_lin = d_extended[tap_count - 1 :] + jnp.pad(
        rim_back, ((count_of_rows - tap_count + 1, 0), (0, 0))
    )
    d_every_low = jnp.concatenate(
        [
            d_query_low,
            d_key_low,
            d_value_low,
            d_gate_lin.astype(jnp.bfloat16),
            d_mixer_lin.astype(jnp.bfloat16),
            jnp.pad(d_step_lin, ((0, 0), (0, IN_WIDTH - IN_USED))).astype(jnp.bfloat16),
        ],
        axis=1,
    )
    late_got = swap_cores(
        input_grad(normed_low, half(d_every_low, 1 - core, 1)).astype(jnp.bfloat16)
    )
    late = input_grad(normed_low, half(d_every_low, core, 1)) + late_got.astype(jnp.float32)
    late_parts = lax.all_to_all(
        late.astype(jnp.bfloat16).reshape(64, 16, IN_WIDTH // 2),
        both,
        0,
        0,
        axis_index_groups=CORE_GROUPS,
    )
    late_sum = jnp.sum(late_parts.astype(jnp.float32), axis=0).astype(jnp.bfloat16)
    late_all = copies_of(late_sum).reshape(4, 2, 16, IN_WIDTH // 2).astype(jnp.float32)
    late_all = late_all.transpose(0, 2, 1, 3).reshape(64, IN_WIDTH)
    d_normed = back_through(d_every_low, in_full)
    d_tokens_norm, grad_attention_gain = norm_one_back(d_normed)
    grad_tokens = d_residual + d_tokens_norm

    def flat(part):
        part = part.reshape(-1)
        return jnp.pad(part, (0, -part.size % 128))

    pieces = (
        grad_attention_gain,
        grad_conv_weight,
        grad_conv_bias,
        grad_step_bias,
        grad_decay_log,
        grad_skip_gain,
        grad_feed_gain,
    )
    packed = jnp.concatenate([flat(part) for part in pieces])
    packed = sum_everywhere(jnp.pad(packed, (0, -packed.size % 1024)).reshape(-1, 128)).reshape(-1)
    small, start = [], 0
    for part in pieces:
        small.append(packed[start : start + part.size].reshape(part.shape))
        start += part.size + -part.size % 128
    summed = (
        late_all[:, :512],
        late_all[:, 512:640],
        late_all[:, 640:768],
        early_out[:32],
        late_all[:, 768:2304],
        late_all[:, 2304:4096],
        late_all[:, 4096:IN_USED],
        early_out[32:128],
        early_feed[0],
        early_feed[1],
        early_out[128:],
    )
    return (
        output,
        grad_tokens,
        small[0],
        summed[0],
        summed[1],
        summed[2],
        summed[3],
        summed[4],
        summed[5],
        summed[6],
        summed[7],
        small[1],
        small[2],
        small[3],
        small[4],
        small[5],
        small[6],
        summed[8],
        summed[9],
        summed[10],
    )


def solution(mesh):
    return jax.shard_map(
        on_device,
        mesh=mesh,
        in_specs=(
            P(("dp", "context"), None),
            P(("dp", "context")),
            P(("dp", "context"), None),
            P(),
            P("dp", None),
            P("dp", None),
            P("dp", None),
            P("dp", None),
            P("dp", None),
            P("dp", None),
            P("dp", None),
            P("dp", None),
            P(),
            P(),
            P(),
            P(),
            P(),
            P(),
            P("dp", None),
            P("dp", None),
            P("dp", None),
        ),
        out_specs=(
            P(("dp", "context"), None),
            P(("dp", "context"), None),
            P(),
            P("dp", None),
            P("dp", None),
            P("dp", None),
            P("dp", None),
            P("dp", None),
            P("dp", None),
            P("dp", None),
            P("dp", None),
            P(),
            P(),
            P(),
            P(),
            P(),
            P(),
            P("dp", None),
            P("dp", None),
            P("dp", None),
        ),
        check_vma=False,
    )
```

```python
import math

import jax
import jax.numpy as jnp
from jax import lax
from jax.experimental import pallas as pl
from jax.experimental.pallas import tpu as pltpu
from jax.sharding import PartitionSpec as P

QUERY_HEADS = 8
KEY_VALUE_HEADS = 2
HEAD_WIDTH = 64
MH = 24
MP = 64
NS = 128


EPSILON = 1e-05
masked_fill = -1e30
attention_multiplier = 0.9375
mixer_multiplier = 0.2357
rotary_base = 100000000000.0
IN_USED = 4120
IN_WIDTH = 4352
CHIP_GROUPS = [[2 * z + c for z in range(4)] for c in range(2)]
CORE_GROUPS = [[8 * d + 2 * z + c for d in range(16) for z in range(4)] for c in range(2)]


def from_behind(block, axis, distance):
    devices = range(lax.axis_size(axis))
    route = [(i - distance, i) for i in devices if i - distance in devices]
    return lax.ppermute(block, axis, route)


def swap_cores(block):
    devices = range(lax.axis_size("context"))
    return lax.ppermute(block, "context", [(i, i ^ 1) for i in devices])


def shift_chips(block, distance):
    devices = lax.axis_size("context")
    return lax.ppermute(
        block, "context", [(i, (i + 2 * distance) % devices) for i in range(devices)]
    )


def shift_rows(block, distance, stride):
    route = []
    for i in range(16):
        place = i // stride % 4
        route.append((i, i + ((place + distance) % 4 - place) * stride))
    return lax.ppermute(block, "dp", route)


def sum_of_four(block, shift):
    one, two, three = shift(block, 1), shift(block, 2), shift(block, 3)
    return (block + two) + (one + three)


def sum_everywhere(block):
    block = block + swap_cores(block)
    block = sum_of_four(block, shift_chips)
    block = sum_of_four(block, lambda part, k: shift_rows(part, k, 1))
    return sum_of_four(block, lambda part, k: shift_rows(part, k, 4))


def half(block, which, axis):
    size = block.shape[axis] // 2
    return lax.dynamic_slice_in_dim(block, which * size, size, axis)


def copies_of(block):
    devices = lax.axis_size("context")
    return lax.all_to_all(
        jnp.broadcast_to(block[None], (devices,) + block.shape), "context", 0, 0
    )


def carried_in(carried, local, reverse):
    mine = lax.axis_index("context")
    core, chip = mine % 2, mine // 2
    is_first = (core == 1) if reverse else (core == 0)
    order = 3 - chip if reverse else chip
    way = -1 if reverse else 1
    decay_other = swap_cores(carried)
    own_part, own_decay = half(local, core, 1), half(carried, core, 0)
    got_part = swap_cores(half(local, 1 - core, 1).astype(jnp.bfloat16)).astype(jnp.float32)
    got_decay = half(decay_other, core, 0)
    first = jnp.where(is_first, own_part, got_part)
    second = jnp.where(is_first, got_part, own_part)
    first_decay = jnp.where(is_first, own_decay, got_decay)
    second_decay = jnp.where(is_first, got_decay, own_decay)
    chip_part = first * second_decay[None, :] + second
    chip_low = chip_part.astype(jnp.bfloat16)
    chip_decay = first_decay * second_decay
    total = jnp.zeros_like(first)
    factor = jnp.ones_like(chip_decay)
    for k in range(1, 4):
        part = shift_chips(chip_low, way * k).astype(jnp.float32)
        reach = jnp.where(order >= k, factor, 0.0)
        total = total + reach[None, :] * part
        if k < 3:
            factor = factor * shift_chips(chip_decay, way * k)
    for_first = total
    for_second = total * first_decay[None, :] + first
    keep = jnp.where(is_first, for_first, for_second)
    give = jnp.where(is_first, for_second, for_first)
    got = swap_cores(give.astype(jnp.bfloat16))
    keep = keep.astype(jnp.bfloat16)
    return jnp.where(
        core == 0, jnp.concatenate([keep, got], axis=1), jnp.concatenate([got, keep], axis=1)
    )


def rms_norm(values, gain_vector):
    return (
        values
        * lax.rsqrt(jnp.mean(values * values, axis=-1, keepdims=True) + EPSILON)
        * gain_vector
    )


def rotary(values, places, direction):
    count_of_rows = values.shape[0]
    head_count = values.shape[1] // HEAD_WIDTH
    half_size = HEAD_WIDTH // 2
    frequency = rotary_base ** (-2.0 * jnp.arange(half_size, dtype=jnp.float32) / HEAD_WIDTH)
    angles = places[:, None] * frequency[None, :]
    cosine = jnp.cos(angles)[:, None, :]
    sine_part = direction * jnp.sin(angles)[:, None, :]
    per_head = values.reshape(count_of_rows, head_count, HEAD_WIDTH)
    front_half = per_head[:, :, :half_size]
    back_half = per_head[:, :, half_size:]
    turned = jnp.concatenate(
        [front_half * cosine - back_half * sine_part, back_half * cosine + front_half * sine_part],
        axis=-1,
    )
    return turned.reshape(count_of_rows, head_count * HEAD_WIDTH)


def mixer_inputs(
    extended, seg_extended, seg_own, conv_taps, conv_shift, step_raw, step_shift, decay_logs
):
    count_of_rows = seg_own.shape[0]
    mixed = conv_shift[None, :]
    for tap_index in range(conv_taps.shape[0]):
        same_doc = (seg_extended[tap_index : tap_index + count_of_rows] == seg_own).astype(
            jnp.float32
        )
        mixed = (
            mixed
            + conv_taps[tap_index][None, :]
            * extended[tap_index : tap_index + count_of_rows]
            * same_doc[:, None]
        )
    activated = jax.nn.silu(mixed)
    step_size = jax.nn.softplus(step_raw + step_shift[None, :])
    log_rate = step_size * (-jnp.exp(decay_logs))[None, :]
    return (activated, step_size, log_rate)


def decay_terms(log_rate, seg_own, seg_before):
    count_of_rows = log_rate.shape[0]
    index_rows = jnp.arange(count_of_rows)
    lower = (index_rows[:, None] >= index_rows[None, :]).astype(jnp.float32)
    running = jnp.dot(lower, log_rate, precision=lax.Precision.HIGHEST)
    entry = jnp.exp(running) * (seg_own == seg_before).astype(jnp.float32)[:, None]
    leaving = (
        jnp.exp(running[-1][None, :] - running)
        * (seg_own == seg_own[-1]).astype(jnp.float32)[:, None]
    )
    carried = jnp.exp(running[-1]) * (seg_own[-1] == seg_before).astype(jnp.float32)
    return (running, entry, leaving, carried)


def heads_to_columns(values):
    spread = jnp.repeat(jnp.eye(MH, dtype=jnp.float32), MP, axis=1)
    return jnp.dot(values, spread, precision=lax.Precision.HIGH)


def columns_to_heads(values):
    spread = jnp.repeat(jnp.eye(MH, dtype=jnp.float32), MP, axis=1)
    return jnp.einsum("ic,hc->ih", values, spread, precision=lax.Precision.HIGH)


def matmul(left, right, sides=((1,), (0,))):
    return lax.dot_general(left, right, (sides, ((), ())), preferred_element_type=jnp.float32)


def attend_kernel(query_ref, key_ref, value_ref, bias_ref, out_ref, total_ref):
    scores = matmul(key_ref[0], query_ref[...]) + bias_ref[...].astype(jnp.float32)
    top = jnp.max(scores, axis=0, keepdims=True)
    exponent = jnp.exp(scores - top)
    total = jnp.sum(exponent, axis=0, keepdims=True)
    probs = (exponent * (1.0 / total)).astype(jnp.bfloat16)
    out_ref[...] = matmul(value_ref[...], probs).astype(jnp.bfloat16)
    total_ref[0] = top + jnp.log(total)


def attend_back_kernel(
    query_t_ref,
    query_ref,
    out_t_ref,
    out_ref,
    key_ref,
    value_ref,
    key_t_ref,
    bias_ref,
    total_ref,
    d_query_ref,
    d_key_ref,
):
    scores = matmul(key_ref[0], query_t_ref[...]) + bias_ref[...].astype(jnp.float32)
    probs = jnp.exp(scores - total_ref[0])
    d_probs = matmul(value_ref[0], out_t_ref[...])
    delta = jnp.sum(probs * d_probs, axis=0, keepdims=True)
    d_scores = (probs * (d_probs - delta)).astype(jnp.bfloat16)
    d_query_ref[...] = matmul(key_t_ref[...], d_scores)
    d_key = matmul(d_scores, query_ref[0])
    d_value = matmul(probs.astype(jnp.bfloat16), out_ref[0])
    both = jnp.concatenate([d_key, d_value], axis=1)
    first = pl.program_id(0) % 4 == 0

    @pl.when(first)
    def _():
        d_key_ref[0] = both

    @pl.when(jnp.logical_not(first))
    def _():
        d_key_ref[0] += both


def within_kernel(inputs_ref, inter_ref, bias_ref, column_ref, row_ref, out_ref):
    parts = []
    for p in range(2):
        within = jnp.exp(column_ref[0, :, p : p + 1] - row_ref[0, p : p + 1, :] + bias_ref[...])
        mixing = (inter_ref[...] * within).astype(jnp.bfloat16)
        parts.append(matmul(mixing, inputs_ref[...]))
    lane = lax.broadcasted_iota(jnp.int32, parts[0].shape, 1)
    out_ref[...] = jnp.where(lane < MP, parts[0], parts[1])


def within_back_kernel(
    inputs_ref,
    grad_ref,
    inter_ref,
    bias_ref,
    column_ref,
    row_ref,
    d_inputs_ref,
    d_inter_ref,
    d_column_ref,
    d_row_ref,
):
    lane = lax.broadcasted_iota(jnp.int32, inputs_ref.shape, 1)
    parts, columns, rows, d_inter = [], [], [], None
    for p in range(2):
        within = jnp.exp(row_ref[0, p : p + 1, :] - column_ref[0, :, p : p + 1] + bias_ref[...])
        mixing = inter_ref[...] * within
        parts.append(matmul(mixing.astype(jnp.bfloat16), grad_ref[...]))
        own = (lane < MP) if p == 0 else (lane >= MP)
        own_inputs = jnp.where(own, inputs_ref[...].astype(jnp.float32), 0.0)
        d_mixing = matmul(own_inputs.astype(jnp.bfloat16), grad_ref[...], ((1,), (1,)))
        product = d_mixing * mixing
        rows.append(jnp.sum(product, axis=0, keepdims=True))
        columns.append(jnp.sum(product, axis=1, keepdims=True))
        term = d_mixing * within
        d_inter = term if d_inter is None else d_inter + term
    d_inputs_ref[...] = jnp.where(lane < MP, parts[0], parts[1])
    d_row_ref[0] = jnp.concatenate(rows, axis=0)
    d_column_ref[0] = jnp.concatenate(columns, axis=1)
    first = pl.program_id(0) == 0

    @pl.when(first)
    def _():
        d_inter_ref[...] = d_inter

    @pl.when(jnp.logical_not(first))
    def _():
        d_inter_ref[...] += d_inter


def kernel_call(kernel, steps, ins, outs, flops, args):
    out_shape = [jax.ShapeDtypeStruct(shape, kind) for shape, kind, _, _ in outs]
    return pl.pallas_call(
        kernel,
        grid=(steps,),
        in_specs=[pl.BlockSpec(block, where) for block, where in ins],
        out_specs=[pl.BlockSpec(block, where) for _, _, block, where in outs],
        out_shape=out_shape,
        compiler_params=pltpu.CompilerParams(vmem_limit_bytes=48 * 1024 * 1024),
        cost_estimate=pl.CostEstimate(flops=flops, bytes_accessed=4 << 20, transcendentals=4 << 20),
    )(*args)


def feed_kernel(normed_ref, gate_ref, up_ref, down_ref, gate_lin_ref, up_lin_ref, hidden_ref, out_ref):
    gate = matmul(normed_ref[...], gate_ref[...])
    up = matmul(normed_ref[...], up_ref[...])
    gate_lin_ref[...] = gate
    up_lin_ref[...] = up
    hidden = (jax.nn.silu(gate) * up).astype(jnp.bfloat16)
    hidden_ref[...] = hidden
    out = matmul(hidden, down_ref[...])
    first = pl.program_id(0) == 0

    @pl.when(first)
    def _():
        out_ref[...] = out

    @pl.when(jnp.logical_not(first))
    def _():
        out_ref[...] += out


def feed_back_kernel(
    cotangent_ref,
    gate_lin_ref,
    up_lin_ref,
    gate_ref,
    up_ref,
    down_ref,
    d_gate_ref,
    d_up_ref,
    d_normed_ref,
):
    d_hidden = matmul(cotangent_ref[...], down_ref[...], ((1,), (1,)))
    gate, up = gate_lin_ref[...], up_lin_ref[...]
    sigmoid = jax.nn.sigmoid(gate)
    d_gate = (d_hidden * up * sigmoid * (1.0 + gate * (1.0 - sigmoid))).astype(jnp.bfloat16)
    d_up = (d_hidden * gate * sigmoid).astype(jnp.bfloat16)
    d_gate_ref[...] = d_gate
    d_up_ref[...] = d_up
    back = matmul(d_gate, gate_ref[...], ((1,), (1,))) + matmul(d_up, up_ref[...], ((1,), (1,)))
    first = pl.program_id(0) == 0

    @pl.when(first)
    def _():
        d_normed_ref[...] = back

    @pl.when(jnp.logical_not(first))
    def _():
        d_normed_ref[...] += back


FEED_WEIGHTS = [
    ((1024, 512), lambda j: (0, j)),
    ((1024, 512), lambda j: (0, 4 + j)),
    ((512, 1024), lambda j: (j % 2, 6 + j // 2)),
]


def feed_forward(normed_low, weights):
    rows = normed_low.shape[0]
    part = ((rows, 512), lambda j: (0, j))
    whole = ((rows, 1024), lambda j: (0, 0))
    return kernel_call(
        feed_kernel,
        4,
        [whole] + FEED_WEIGHTS,
        [
            ((rows, 2048), jnp.float32) + part,
            ((rows, 2048), jnp.float32) + part,
            ((rows, 2048), jnp.bfloat16) + part,
            ((rows, 1024), jnp.float32) + whole,
        ],
        6 * rows * 1024 * 2048,
        (normed_low, weights, weights, weights),
    )


def feed_backward(cotangent, gate_lin, up_lin, weights):
    rows = cotangent.shape[0]
    part = ((rows, 512), lambda j: (0, j))
    whole = ((rows, 1024), lambda j: (0, 0))
    return kernel_call(
        feed_back_kernel,
        4,
        [whole, part, part] + FEED_WEIGHTS,
        [
            ((rows, 2048), jnp.bfloat16) + part,
            ((rows, 2048), jnp.bfloat16) + part,
            ((rows, 1024), jnp.float32) + whole,
        ],
        6 * rows * 1024 * 2048,
        (cotangent, gate_lin, up_lin, weights, weights, weights),
    )


def attend(query_t, kv_heads, kv_t, bias):
    keys, rows = bias.shape
    size = HEAD_WIDTH
    return kernel_call(
        attend_kernel,
        QUERY_HEADS,
        [
            ((size, rows), lambda h: (h, 0)),
            ((1, keys, size), lambda h: (h // 4, 0, 0)),
            ((size, keys), lambda h: (2 + h // 4, 0)),
            ((keys, rows), lambda h: (0, 0)),
        ],
        [
            ((QUERY_HEADS * size, rows), jnp.bfloat16, (size, rows), lambda h: (h, 0)),
            ((QUERY_HEADS, 1, rows), jnp.float32, (1, 1, rows), lambda h: (h, 0, 0)),
        ],
        4 * QUERY_HEADS * size * rows * keys * 4,
        (query_t, kv_heads, kv_t, bias),
    )


def attend_back(query_t, query_heads, out_t, out_heads, kv_heads, kv_t, bias, totals):
    keys, rows = bias.shape
    size = HEAD_WIDTH
    return kernel_call(
        attend_back_kernel,
        QUERY_HEADS,
        [
            ((size, rows), lambda h: (h, 0)),
            ((1, rows, size), lambda h: (h, 0, 0)),
            ((size, rows), lambda h: (h, 0)),
            ((1, rows, size), lambda h: (h, 0, 0)),
            ((1, keys, size), lambda h: (h // 4, 0, 0)),
            ((1, keys, size), lambda h: (2 + h // 4, 0, 0)),
            ((size, keys), lambda h: (h // 4, 0)),
            ((keys, rows), lambda h: (0, 0)),
            ((1, 1, rows), lambda h: (h, 0, 0)),
        ],
        [
            ((QUERY_HEADS * size, rows), jnp.float32, (size, rows), lambda h: (h, 0)),
            (
                (KEY_VALUE_HEADS, keys, 2 * size),
                jnp.float32,
                (1, keys, 2 * size),
                lambda h: (h // 4, 0, 0),
            ),
        ],
        10 * QUERY_HEADS * size * rows * keys * 4,
        (query_t, query_heads, out_t, out_heads, kv_heads, kv_heads, kv_t, bias, totals),
    )


def pair_blocks(rows):
    return (
        ((rows, 2 * MP), lambda i: (0, i)),
        ((rows, rows), lambda i: (0, 0)),
        ((1, rows, 2), lambda i: (i, 0, 0)),
        ((1, 2, rows), lambda i: (i, 0, 0)),
    )


def within_block(inputs_low, inter, bias, columns, rows_of):
    rows = inter.shape[0]
    wide, square, column, row = pair_blocks(rows)
    return kernel_call(
        within_kernel,
        MH // 2,
        [wide, square, square, column, row],
        [((rows, MH * MP), jnp.float32) + wide],
        16 * MH * MP * rows * rows,
        (inputs_low, inter, bias, columns, rows_of),
    )[0]


def within_block_back(inputs_low, grad_low, inter_t, bias_t, columns, rows_of):
    rows = inter_t.shape[0]
    wide, square, column, row = pair_blocks(rows)
    return kernel_call(
        within_back_kernel,
        MH // 2,
        [wide, wide, square, square, column, row],
        [
            ((rows, MH * MP), jnp.float32) + wide,
            ((rows, rows), jnp.float32) + square,
            ((MH // 2, rows, 2), jnp.float32) + column,
            ((MH // 2, 2, rows), jnp.float32) + row,
        ],
        32 * MH * MP * rows * rows,
        (inputs_low, grad_low, inter_t, bias_t, columns, rows_of),
    )


def project(left, right):
    return jnp.dot(left, right, preferred_element_type=jnp.float32)


def input_grad(left, right):
    return jnp.einsum("rk,rj->kj", left, right, preferred_element_type=jnp.float32)


def back_through(grad_low, weight_full):
    return jnp.einsum("rj,kj->rk", grad_low, weight_full, preferred_element_type=jnp.float32)


def swiglu(gate_values, up_values):
    return jax.nn.silu(gate_values) * up_values


def gating(scan_values, gate_values):
    return scan_values * jax.nn.silu(gate_values)


def on_device(
    tokens,
    segments,
    cotangent,
    attention_gain,
    query_weight,
    key_matrix,
    value_matrix,
    attention_out,
    gate_weight,
    mixer_weight,
    step_weight,
    mixer_out,
    conv_weight,
    conv_bias,
    step_bias,
    decay_log,
    skip_gain,
    feed_gain,
    feed_gate,
    feed_up,
    feed_down,
):
    block_index = lax.axis_index("context")
    core = block_index % 2
    chip = block_index // 2
    both = ("dp", "context")
    step_padded = jnp.pad(step_weight, ((0, 0), (0, IN_WIDTH - IN_USED)))
    in_shard = jnp.concatenate(
        [query_weight, key_matrix, value_matrix, gate_weight, mixer_weight, step_padded], axis=1
    )
    in_full = lax.all_gather(
        lax.dynamic_slice_in_dim(in_shard, block_index * 8, 8, 0), both, axis=0, tiled=True
    )
    def hidden_order(block):
        return block.reshape(8, 16, 2, 64).transpose(0, 2, 1, 3).reshape(8, 2048)

    feed_shard = jnp.concatenate(
        [
            hidden_order(lax.dynamic_slice_in_dim(feed_gate, block_index * 8, 8, 0)),
            hidden_order(lax.dynamic_slice_in_dim(feed_up, block_index * 8, 8, 0)),
        ],
        axis=1,
    )
    out_rows_own = jnp.concatenate([attention_out, mixer_out, feed_down], axis=0)
    out_shard = [
        lax.dynamic_slice_in_dim(out_rows_own, group * 64 + block_index * 8, 8, 0)
        for group in range(4)
    ]
    late_full = lax.all_gather(
        jnp.concatenate([feed_shard] + out_shard, axis=1), both, axis=0, tiled=True
    )
    first_rows = late_full[:, 4096:5120].reshape(16, 64, 1024)
    second_rows = late_full[:, 5120:6144].reshape(16, 64, 1024)
    out_full = first_rows[:, :32].reshape(512, 1024)
    mixer_out_full = jnp.concatenate([first_rows[:, 32:], second_rows], axis=1).reshape(1536, 1024)
    count_of_rows = tokens.shape[0]
    tap_count = conv_weight.shape[0]
    inner_width = MH * MP
    width_of_keys = KEY_VALUE_HEADS * HEAD_WIDTH
    query_places = block_index * count_of_rows + jnp.arange(count_of_rows, dtype=jnp.int32)
    place_float = query_places.astype(jnp.float32)
    seg_float = segments.astype(jnp.float32)
    seg_low = segments.astype(jnp.bfloat16)
    hidden_in = tokens.astype(jnp.float32)
    normed, norm_one_back = jax.vjp(rms_norm, hidden_in, attention_gain)
    normed_low = normed.astype(jnp.bfloat16)
    every_lin = project(normed_low, in_full)
    query_lin = every_lin[:, :512]
    key_lin = every_lin[:, 512:640]
    value_lin = every_lin[:, 640:768]
    gate_lin = every_lin[:, 768:2304]
    mixer_lin = every_lin[:, 2304:4096]
    step_lin = every_lin[:, 4096:IN_USED]
    rotated_queries = rotary(query_lin, place_float, 1.0).astype(jnp.bfloat16)
    rotated_keys = rotary(key_lin, place_float, 1.0).astype(jnp.bfloat16)
    value_reduced = value_lin.astype(jnp.bfloat16)
    sent = jnp.concatenate(
        [
            jnp.concatenate([rotated_keys, value_reduced], axis=1),
            jnp.pad(seg_low[None, :], ((0, 7), (0, 0))),
        ],
        axis=0,
    )
    along = jnp.stack([sent] + [shift_chips(sent, k) for k in range(1, 4)])
    slots = jnp.concatenate([along, swap_cores(along)], axis=0)
    kv_heads = slots[:, :count_of_rows].reshape(-1, 4, HEAD_WIDTH).transpose(1, 0, 2)
    kv_t = kv_heads.transpose(0, 2, 1).reshape(4 * HEAD_WIDTH, -1)
    seg_all = slots[:, count_of_rows].reshape(-1)
    owners = jnp.concatenate(
        [(chip - jnp.arange(4)) % 4 * 2 + core, (chip - jnp.arange(4)) % 4 * 2 + 1 - core]
    )
    key_places = (
        owners[:, None] * count_of_rows + jnp.arange(count_of_rows, dtype=jnp.int32)[None, :]
    ).reshape(-1)
    attention_bias = jnp.where(
        (key_places[:, None] <= query_places[None, :]) & (seg_all[:, None] == seg_low[None, :]),
        0.0,
        masked_fill,
    ).astype(jnp.bfloat16)
    scale_factor = 1.0 / math.sqrt(HEAD_WIDTH)
    query_scaled = rotated_queries * jnp.asarray(scale_factor, jnp.bfloat16)
    query_t = query_scaled.T
    attended_t, totals = attend(query_t, kv_heads, kv_t, attention_bias)
    attended_low = attended_t.T
    attention_branch = project(attended_low, out_full)
    prev_rows, prev_segs = from_behind(
        (mixer_lin[count_of_rows - tap_count + 1 :], seg_float[count_of_rows - tap_count + 1 :]),
        "context",
        1,
    )
    extended = jnp.concatenate([prev_rows, mixer_lin], axis=0)
    seg_extended = jnp.concatenate([prev_segs, seg_float])
    seg_before = prev_segs[-1]

    def mixer_piece(ext_rows, conv_taps, conv_shift, step_raw, step_shift, decay_logs):
        return mixer_inputs(
            ext_rows,
            seg_extended,
            seg_float,
            conv_taps,
            conv_shift,
            step_raw,
            step_shift,
            decay_logs,
        )

    (activated, step_size, log_rate), mixer_back = jax.vjp(
        mixer_piece, extended, conv_weight, conv_bias, step_lin, step_bias, decay_log
    )
    mixer_x = activated[:, :inner_width]
    bees = activated[:, inner_width : inner_width + NS].astype(jnp.bfloat16)
    seas = activated[:, inner_width + NS :].astype(jnp.bfloat16)

    def decay_piece(rates):
        return decay_terms(rates, seg_float, seg_before)

    (running, entry, leaving, carried), decay_back = jax.vjp(decay_piece, log_rate)
    spread = heads_to_columns(jnp.concatenate([step_size, leaving, entry], axis=0))
    step_wide = spread[:count_of_rows]
    leaving_wide = spread[count_of_rows : 2 * count_of_rows]
    entry_wide = spread[2 * count_of_rows :]
    inputs_low = (mixer_x * step_wide).astype(jnp.bfloat16)
    weighted_low = (inputs_low.astype(jnp.float32) * leaving_wide).astype(jnp.bfloat16)
    local_state = input_grad(bees, weighted_low)
    carried_wide = jnp.repeat(carried, MP)
    skip_wide = jnp.repeat(skip_gain, MP)[None, :]
    incoming_low = carried_in(carried_wide, local_state, False)
    index_rows = jnp.arange(count_of_rows)
    block_allowed = (index_rows[:, None] >= index_rows[None, :]) & (
        seg_float[:, None] == seg_float[None, :]
    )
    block_bias = jnp.where(block_allowed, 0.0, masked_fill)
    running_rows = running.T.reshape(MH // 2, 2, count_of_rows)
    running_columns = running_rows.transpose(0, 2, 1)
    intersection = matmul(seas, bees, ((1,), (1,)))
    inner = within_block(inputs_low, intersection, block_bias, running_columns, running_rows)
    from_state = project(seas, incoming_low)
    scanned = inner + from_state * entry_wide + skip_wide * mixer_x
    gated, gating_back = jax.vjp(gating, scanned, gate_lin)
    gated_low = gated.astype(jnp.bfloat16)
    mixer_branch = project(gated_low, mixer_out_full)
    residual = hidden_in + attention_multiplier * attention_branch + mixer_multiplier * mixer_branch
    normed_two, norm_two_back = jax.vjp(rms_norm, residual, feed_gain)
    normed_two_low = normed_two.astype(jnp.bfloat16)
    ffn_gate_lin, ffn_up_lin, hidden_low, feed_out = feed_forward(normed_two_low, late_full)
    output = (residual + feed_out).astype(jnp.bfloat16)
    upstream = cotangent.astype(jnp.float32)
    d_ffn_gate, d_ffn_up, d_normed_two = feed_backward(
        cotangent, ffn_gate_lin, ffn_up_lin, late_full
    )
    d_feed_low = jnp.stack([d_ffn_gate, d_ffn_up])
    d_resid_norm, grad_feed_gain = norm_two_back(d_normed_two)
    d_residual = upstream + d_resid_norm
    d_attn_low = (attention_multiplier * d_residual).astype(jnp.bfloat16)
    d_mixer_low = (mixer_multiplier * d_residual).astype(jnp.bfloat16)

    feed_got = swap_cores(
        input_grad(normed_two_low, d_feed_low[1 - core]).astype(jnp.bfloat16)
    )
    feed_own = (
        input_grad(normed_two_low, d_feed_low[core]) + feed_got.astype(jnp.float32)
    ).astype(jnp.bfloat16)

    def out_grads(which):
        attn = input_grad(attended_low, half(d_attn_low, which, 1)).astype(jnp.bfloat16)
        mix = input_grad(gated_low, half(d_mixer_low, which, 1)).astype(jnp.bfloat16)
        down = input_grad(hidden_low, half(cotangent, which, 1)).astype(jnp.bfloat16)
        return (attn, mix, down)

    out_got = jax.tree.map(swap_cores, out_grads(1 - core))
    early = jax.tree.map(lambda a, b: a + b, out_grads(core), out_got)
    down_rows = early[2].reshape(2, 16, 64, 512)
    out_rows = jnp.concatenate(
        [early[0].reshape(16, 32, 512), early[1].reshape(16, 96, 512), down_rows[0], down_rows[1]],
        axis=1,
    )
    attended_gradient = back_through(d_attn_low, out_full).astype(jnp.bfloat16)
    d_gated = back_through(d_mixer_low, mixer_out_full)
    d_scan_flat, d_gate_lin = gating_back(d_gated)
    d_scan_low = d_scan_flat.astype(jnp.bfloat16)
    d_scan = d_scan_low.astype(jnp.float32)
    d_from_low = (d_scan * entry_wide).astype(jnp.bfloat16)
    d_incoming = input_grad(seas, d_from_low)
    attended_gradient, feed_own, d_incoming = lax.optimization_barrier(
        (attended_gradient, feed_own, d_incoming)
    )
    feed_shard_sum = lax.psum_scatter(feed_own, "dp", scatter_dimension=0, tiled=True)
    d_state_low = carried_in(carried_wide, d_incoming, True)
    d_query_t, d_kv = attend_back(
        query_t,
        query_scaled.reshape(count_of_rows, QUERY_HEADS, HEAD_WIDTH).transpose(1, 0, 2),
        attended_gradient.T,
        attended_gradient.reshape(count_of_rows, QUERY_HEADS, HEAD_WIDTH).transpose(1, 0, 2),
        kv_heads,
        kv_t,
        attention_bias,
        totals,
    )
    d_scan_low, out_rows, d_kv = lax.optimization_barrier((d_scan_low, out_rows, d_kv))
    out_shard_sum = lax.psum_scatter(
        out_rows.reshape(16 * 256, 512), "dp", scatter_dimension=0, tiled=True
    )
    feed_rows = feed_shard_sum.reshape(64, 4, 512).transpose(1, 0, 2).reshape(256, 512)
    early_parts = lax.all_to_all(
        jnp.concatenate([out_shard_sum, feed_rows], axis=0).reshape(4, 128, 512),
        "context",
        0,
        0,
        axis_index_groups=CHIP_GROUPS,
    )
    early_sum = jnp.sum(early_parts.astype(jnp.float32), axis=0).astype(jnp.bfloat16)
    early_all = copies_of(early_sum).reshape(4, 2, 128, 512).astype(jnp.float32)
    early_out = early_all[:2].transpose(0, 2, 1, 3).reshape(256, 1024)
    early_feed = early_all[2:].transpose(1, 0, 2, 3).reshape(2, 4, 64, 512)
    early_feed = early_feed.transpose(0, 2, 1, 3).reshape(2, 64, 2, 16, 64)
    early_feed = early_feed.transpose(0, 1, 3, 2, 4).reshape(2, 64, 2048)
    d_query_rot = d_query_t.T * scale_factor
    slot_grads = d_kv.astype(jnp.bfloat16).reshape(KEY_VALUE_HEADS, 2, 4, count_of_rows, -1)
    chip_grads = slot_grads[:, 0].astype(jnp.float32) + swap_cores(slot_grads[:, 1]).astype(
        jnp.float32
    )
    chip_low = chip_grads.astype(jnp.bfloat16)
    own_grads = chip_grads[:, 0]
    for k in range(1, 4):
        own_grads = own_grads + shift_chips(chip_low[:, k], -k).astype(jnp.float32)
    key_grads = jnp.concatenate(
        [
            own_grads[0, :, :HEAD_WIDTH],
            own_grads[1, :, :HEAD_WIDTH],
            own_grads[0, :, HEAD_WIDTH:],
            own_grads[1, :, HEAD_WIDTH:],
        ],
        axis=1,
    )
    d_query_low = rotary(d_query_rot, place_float, -1.0).astype(jnp.bfloat16)
    d_key_low = rotary(key_grads[:, :width_of_keys], place_float, -1.0).astype(jnp.bfloat16)
    d_value_low = key_grads[:, width_of_keys:].astype(jnp.bfloat16)
    d_inputs, d_inter_t, d_columns, d_rows = within_block_back(
        inputs_low, d_scan_low, intersection.T, block_bias.T, running_columns, running_rows
    )
    d_running = (d_rows - d_columns.transpose(0, 2, 1)).reshape(MH, count_of_rows).T
    d_inter_low = d_inter_t.astype(jnp.bfloat16)
    d_seas = back_through(d_from_low, incoming_low) + input_grad(d_inter_low, bees)
    d_bees = project(d_inter_low, seas) + back_through(weighted_low, d_state_low)
    d_weighted = project(bees, d_state_low)
    d_inputs = d_inputs + d_weighted * leaving_wide
    d_mixer_x = skip_wide * d_scan + d_inputs * step_wide
    d_entry = columns_to_heads(d_scan * from_state)
    d_leaving = columns_to_heads(d_weighted * inputs_low.astype(jnp.float32))
    d_step = columns_to_heads(d_inputs * mixer_x)
    sums = columns_to_heads(
        jnp.concatenate(
            [
                jnp.sum(d_scan * mixer_x, axis=0, keepdims=True),
                jnp.sum(
                    d_state_low.astype(jnp.float32) * incoming_low.astype(jnp.float32),
                    axis=0,
                    keepdims=True,
                ),
            ],
            axis=0,
        )
    )
    grad_skip_gain, d_carried = sums[0], sums[1]
    (d_rate,) = decay_back((d_running, d_entry, d_leaving, d_carried))
    d_activated = jnp.concatenate([d_mixer_x, d_bees, d_seas], axis=1)
    d_extended, grad_conv_weight, grad_conv_bias, d_step_lin, grad_step_bias, grad_decay_log = (
        mixer_back((d_activated, d_step, d_rate))
    )
    rim_back = from_behind(d_extended[: tap_count - 1], "context", -1)
    d_mixer_lin = d_extended[tap_count - 1 :] + jnp.pad(
        rim_back, ((count_of_rows - tap_count + 1, 0), (0, 0))
    )
    d_mid_low = jnp.concatenate(
        [d_query_low, d_key_low, d_value_low, d_gate_lin.astype(jnp.bfloat16)], axis=1
    )
    d_late_low = jnp.concatenate(
        [
            d_mixer_lin.astype(jnp.bfloat16),
            jnp.pad(d_step_lin, ((0, 0), (0, IN_WIDTH - IN_USED))).astype(jnp.bfloat16),
        ],
        axis=1,
    )

    def summed_over_all(grad_low):
        width = grad_low.shape[1] // 2
        got = swap_cores(input_grad(normed_low, half(grad_low, 1 - core, 1)).astype(jnp.bfloat16))
        own = input_grad(normed_low, half(grad_low, core, 1)) + got.astype(jnp.float32)
        parts = lax.all_to_all(
            own.astype(jnp.bfloat16).reshape(64, 16, width),
            both,
            0,
            0,
            axis_index_groups=CORE_GROUPS,
        )
        total = jnp.sum(parts.astype(jnp.float32), axis=0).astype(jnp.bfloat16)
        spread_all = copies_of(total).reshape(4, 2, 16, width).astype(jnp.float32)
        return spread_all.transpose(0, 2, 1, 3).reshape(64, 2 * width)

    mid_all = summed_over_all(d_mid_low)
    late_all = summed_over_all(d_late_low)
    d_every_low = jnp.concatenate([d_mid_low, d_late_low], axis=1)
    d_normed = back_through(d_every_low, in_full)
    d_tokens_norm, grad_attention_gain = norm_one_back(d_normed)
    grad_tokens = d_residual + d_tokens_norm

    def flat(part):
        part = part.reshape(-1)
        return jnp.pad(part, (0, -part.size % 128))

    pieces = (
        grad_attention_gain,
        grad_conv_weight,
        grad_conv_bias,
        grad_step_bias,
        grad_decay_log,
        grad_skip_gain,
        grad_feed_gain,
    )
    packed = jnp.concatenate([flat(part) for part in pieces])
    packed = sum_everywhere(jnp.pad(packed, (0, -packed.size % 1024)).reshape(-1, 128)).reshape(-1)
    small, start = [], 0
    for part in pieces:
        small.append(packed[start : start + part.size].reshape(part.shape))
        start += part.size + -part.size % 128
    summed = (
        mid_all[:, :512],
        mid_all[:, 512:640],
        mid_all[:, 640:768],
        early_out[:32],
        mid_all[:, 768:2304],
        late_all[:, :1792],
        late_all[:, 1792 : 1792 + MH],
        early_out[32:128],
        early_feed[0],
        early_feed[1],
        early_out[128:],
    )
    return (
        output,
        grad_tokens,
        small[0],
        summed[0],
        summed[1],
        summed[2],
        summed[3],
        summed[4],
        summed[5],
        summed[6],
        summed[7],
        small[1],
        small[2],
        small[3],
        small[4],
        small[5],
        small[6],
        summed[8],
        summed[9],
        summed[10],
    )


def solution(mesh):
    return jax.shard_map(
        on_device,
        mesh=mesh,
        in_specs=(
            P(("dp", "context"), None),
            P(("dp", "context")),
            P(("dp", "context"), None),
            P(),
            P("dp", None),
            P("dp", None),
            P("dp", None),
            P("dp", None),
            P("dp", None),
            P("dp", None),
            P("dp", None),
            P("dp", None),
            P(),
            P(),
            P(),
            P(),
            P(),
            P(),
            P("dp", None),
            P("dp", None),
            P("dp", None),
        ),
        out_specs=(
            P(("dp", "context"), None),
            P(("dp", "context"), None),
            P(),
            P("dp", None),
            P("dp", None),
            P("dp", None),
            P("dp", None),
            P("dp", None),
            P("dp", None),
            P("dp", None),
            P("dp", None),
            P(),
            P(),
            P(),
            P(),
            P(),
            P(),
            P("dp", None),
            P("dp", None),
            P("dp", None),
        ),
        check_vma=False,
    )
```

```python
import math

import jax
import jax.numpy as jnp
from jax import lax
from jax.experimental import pallas as pl
from jax.experimental.pallas import tpu as pltpu
from jax.sharding import PartitionSpec as P

QUERY_HEADS = 8
KEY_VALUE_HEADS = 2
HEAD_WIDTH = 64
MH = 24
MP = 64
NS = 128


EPSILON = 1e-05
masked_fill = -1e30
attention_multiplier = 0.9375
mixer_multiplier = 0.2357
rotary_base = 100000000000.0
IN_USED = 4120
IN_WIDTH = 4352
CHIP_GROUPS = [[2 * z + c for z in range(4)] for c in range(2)]
CORE_GROUPS = [[8 * d + 2 * z + c for d in range(16) for z in range(4)] for c in range(2)]


def from_behind(block, axis, distance):
    devices = range(lax.axis_size(axis))
    route = [(i - distance, i) for i in devices if i - distance in devices]
    return lax.ppermute(block, axis, route)


def swap_cores(block):
    devices = range(lax.axis_size("context"))
    return lax.ppermute(block, "context", [(i, i ^ 1) for i in devices])


def shift_chips(block, distance):
    devices = lax.axis_size("context")
    return lax.ppermute(
        block, "context", [(i, (i + 2 * distance) % devices) for i in range(devices)]
    )


def shift_rows(block, distance, stride):
    route = []
    for i in range(16):
        place = i // stride % 4
        route.append((i, i + ((place + distance) % 4 - place) * stride))
    return lax.ppermute(block, "dp", route)


def sum_of_four(block, shift):
    one, two, three = shift(block, 1), shift(block, 2), shift(block, 3)
    return (block + two) + (one + three)


def sum_everywhere(block):
    block = block + swap_cores(block)
    block = sum_of_four(block, shift_chips)
    block = sum_of_four(block, lambda part, k: shift_rows(part, k, 1))
    return sum_of_four(block, lambda part, k: shift_rows(part, k, 4))


def half(block, which, axis):
    size = block.shape[axis] // 2
    return lax.dynamic_slice_in_dim(block, which * size, size, axis)


def copies_of(block):
    devices = lax.axis_size("context")
    return lax.all_to_all(
        jnp.broadcast_to(block[None], (devices,) + block.shape), "context", 0, 0
    )


def carried_in(carried, local, reverse):
    mine = lax.axis_index("context")
    core, chip = mine % 2, mine // 2
    is_first = (core == 1) if reverse else (core == 0)
    order = 3 - chip if reverse else chip
    way = -1 if reverse else 1
    decay_other = swap_cores(carried)
    own_part, own_decay = half(local, core, 1), half(carried, core, 0)
    got_part = swap_cores(half(local, 1 - core, 1).astype(jnp.bfloat16)).astype(jnp.float32)
    got_decay = half(decay_other, core, 0)
    first = jnp.where(is_first, own_part, got_part)
    second = jnp.where(is_first, got_part, own_part)
    first_decay = jnp.where(is_first, own_decay, got_decay)
    second_decay = jnp.where(is_first, got_decay, own_decay)
    chip_part = first * second_decay[None, :] + second
    chip_low = chip_part.astype(jnp.bfloat16)
    chip_decay = first_decay * second_decay
    total = jnp.zeros_like(first)
    factor = jnp.ones_like(chip_decay)
    for k in range(1, 4):
        part = shift_chips(chip_low, way * k).astype(jnp.float32)
        reach = jnp.where(order >= k, factor, 0.0)
        total = total + reach[None, :] * part
        if k < 3:
            factor = factor * shift_chips(chip_decay, way * k)
    for_first = total
    for_second = total * first_decay[None, :] + first
    keep = jnp.where(is_first, for_first, for_second)
    give = jnp.where(is_first, for_second, for_first)
    got = swap_cores(give.astype(jnp.bfloat16))
    keep = keep.astype(jnp.bfloat16)
    return jnp.where(
        core == 0, jnp.concatenate([keep, got], axis=1), jnp.concatenate([got, keep], axis=1)
    )


def rms_norm(values, gain_vector):
    return (
        values
        * lax.rsqrt(jnp.mean(values * values, axis=-1, keepdims=True) + EPSILON)
        * gain_vector
    )


def rotary(values, places, direction):
    count_of_rows = values.shape[0]
    head_count = values.shape[1] // HEAD_WIDTH
    half_size = HEAD_WIDTH // 2
    frequency = rotary_base ** (-2.0 * jnp.arange(half_size, dtype=jnp.float32) / HEAD_WIDTH)
    angles = places[:, None] * frequency[None, :]
    cosine = jnp.cos(angles)[:, None, :]
    sine_part = direction * jnp.sin(angles)[:, None, :]
    per_head = values.reshape(count_of_rows, head_count, HEAD_WIDTH)
    front_half = per_head[:, :, :half_size]
    back_half = per_head[:, :, half_size:]
    turned = jnp.concatenate(
        [front_half * cosine - back_half * sine_part, back_half * cosine + front_half * sine_part],
        axis=-1,
    )
    return turned.reshape(count_of_rows, head_count * HEAD_WIDTH)


def mixer_inputs(
    extended, seg_extended, seg_own, conv_taps, conv_shift, step_raw, step_shift, decay_logs
):
    count_of_rows = seg_own.shape[0]
    mixed = conv_shift[None, :]
    for tap_index in range(conv_taps.shape[0]):
        same_doc = (seg_extended[tap_index : tap_index + count_of_rows] == seg_own).astype(
            jnp.float32
        )
        mixed = (
            mixed
            + conv_taps[tap_index][None, :]
            * extended[tap_index : tap_index + count_of_rows]
            * same_doc[:, None]
        )
    activated = jax.nn.silu(mixed)
    step_size = jax.nn.softplus(step_raw + step_shift[None, :])
    log_rate = step_size * (-jnp.exp(decay_logs))[None, :]
    return (activated, step_size, log_rate)


def decay_terms(log_rate, seg_own, seg_before):
    count_of_rows = log_rate.shape[0]
    index_rows = jnp.arange(count_of_rows)
    lower = (index_rows[:, None] >= index_rows[None, :]).astype(jnp.float32)
    running = jnp.dot(lower, log_rate, precision=lax.Precision.HIGHEST)
    entry = jnp.exp(running) * (seg_own == seg_before).astype(jnp.float32)[:, None]
    leaving = (
        jnp.exp(running[-1][None, :] - running)
        * (seg_own == seg_own[-1]).astype(jnp.float32)[:, None]
    )
    carried = jnp.exp(running[-1]) * (seg_own[-1] == seg_before).astype(jnp.float32)
    return (running, entry, leaving, carried)


def heads_to_columns(values):
    spread = jnp.repeat(jnp.eye(MH, dtype=jnp.float32), MP, axis=1)
    return jnp.dot(values, spread, precision=lax.Precision.HIGH)


def columns_to_heads(values):
    spread = jnp.repeat(jnp.eye(MH, dtype=jnp.float32), MP, axis=1)
    return jnp.einsum("ic,hc->ih", values, spread, precision=lax.Precision.HIGH)


def matmul(left, right, sides=((1,), (0,))):
    return lax.dot_general(left, right, (sides, ((), ())), preferred_element_type=jnp.float32)


def attend_kernel(query_ref, key_ref, value_ref, bias_ref, out_ref, total_ref):
    scores = matmul(key_ref[0], query_ref[...]) + bias_ref[...].astype(jnp.float32)
    top = jnp.max(scores, axis=0, keepdims=True)
    exponent = jnp.exp(scores - top)
    total = jnp.sum(exponent, axis=0, keepdims=True)
    probs = (exponent * (1.0 / total)).astype(jnp.bfloat16)
    out_ref[...] = matmul(value_ref[...], probs).astype(jnp.bfloat16)
    total_ref[0] = top + jnp.log(total)


def attend_back_kernel(
    query_t_ref,
    query_ref,
    out_t_ref,
    out_ref,
    key_ref,
    value_ref,
    key_t_ref,
    bias_ref,
    total_ref,
    d_query_ref,
    d_key_ref,
):
    scores = matmul(key_ref[0], query_t_ref[...]) + bias_ref[...].astype(jnp.float32)
    probs = jnp.exp(scores - total_ref[0])
    d_probs = matmul(value_ref[0], out_t_ref[...])
    delta = jnp.sum(probs * d_probs, axis=0, keepdims=True)
    d_scores = (probs * (d_probs - delta)).astype(jnp.bfloat16)
    d_query_ref[...] = matmul(key_t_ref[...], d_scores)
    d_key = matmul(d_scores, query_ref[0])
    d_value = matmul(probs.astype(jnp.bfloat16), out_ref[0])
    both = jnp.concatenate([d_key, d_value], axis=1)
    first = pl.program_id(0) % 4 == 0

    @pl.when(first)
    def _():
        d_key_ref[0] = both

    @pl.when(jnp.logical_not(first))
    def _():
        d_key_ref[0] += both


def within_kernel(inputs_ref, inter_ref, bias_ref, column_ref, row_ref, out_ref):
    parts = []
    for p in range(2):
        within = jnp.exp(column_ref[0, :, p : p + 1] - row_ref[0, p : p + 1, :] + bias_ref[...])
        mixing = (inter_ref[...] * within).astype(jnp.bfloat16)
        parts.append(matmul(mixing, inputs_ref[...]))
    lane = lax.broadcasted_iota(jnp.int32, parts[0].shape, 1)
    out_ref[...] = jnp.where(lane < MP, parts[0], parts[1])


def within_back_kernel(
    inputs_ref,
    grad_ref,
    inter_ref,
    bias_ref,
    column_ref,
    row_ref,
    d_inputs_ref,
    d_inter_ref,
    d_column_ref,
    d_row_ref,
):
    lane = lax.broadcasted_iota(jnp.int32, inputs_ref.shape, 1)
    parts, columns, rows, d_inter = [], [], [], None
    for p in range(2):
        within = jnp.exp(row_ref[0, p : p + 1, :] - column_ref[0, :, p : p + 1] + bias_ref[...])
        mixing = inter_ref[...] * within
        parts.append(matmul(mixing.astype(jnp.bfloat16), grad_ref[...]))
        own = (lane < MP) if p == 0 else (lane >= MP)
        own_inputs = jnp.where(own, inputs_ref[...].astype(jnp.float32), 0.0)
        d_mixing = matmul(own_inputs.astype(jnp.bfloat16), grad_ref[...], ((1,), (1,)))
        product = d_mixing * mixing
        rows.append(jnp.sum(product, axis=0, keepdims=True))
        columns.append(jnp.sum(product, axis=1, keepdims=True))
        term = d_mixing * within
        d_inter = term if d_inter is None else d_inter + term
    d_inputs_ref[...] = jnp.where(lane < MP, parts[0], parts[1])
    d_row_ref[0] = jnp.concatenate(rows, axis=0)
    d_column_ref[0] = jnp.concatenate(columns, axis=1)
    first = pl.program_id(0) == 0

    @pl.when(first)
    def _():
        d_inter_ref[...] = d_inter

    @pl.when(jnp.logical_not(first))
    def _():
        d_inter_ref[...] += d_inter


def kernel_call(kernel, steps, ins, outs, flops, args):
    out_shape = [jax.ShapeDtypeStruct(shape, kind) for shape, kind, _, _ in outs]
    return pl.pallas_call(
        kernel,
        grid=(steps,),
        in_specs=[pl.BlockSpec(block, where) for block, where in ins],
        out_specs=[pl.BlockSpec(block, where) for _, _, block, where in outs],
        out_shape=out_shape,
        compiler_params=pltpu.CompilerParams(vmem_limit_bytes=48 * 1024 * 1024),
        cost_estimate=pl.CostEstimate(flops=flops, bytes_accessed=4 << 20, transcendentals=4 << 20),
    )(*args)


def feed_kernel(normed_ref, gate_ref, up_ref, down_ref, gate_lin_ref, up_lin_ref, hidden_ref, out_ref):
    gate = matmul(normed_ref[...], gate_ref[...])
    up = matmul(normed_ref[...], up_ref[...])
    gate_lin_ref[...] = gate
    up_lin_ref[...] = up
    hidden = (jax.nn.silu(gate) * up).astype(jnp.bfloat16)
    hidden_ref[...] = hidden
    out = matmul(hidden, down_ref[...])
    first = pl.program_id(0) == 0

    @pl.when(first)
    def _():
        out_ref[...] = out

    @pl.when(jnp.logical_not(first))
    def _():
        out_ref[...] += out


def feed_back_kernel(
    cotangent_ref,
    gate_lin_ref,
    up_lin_ref,
    gate_ref,
    up_ref,
    down_ref,
    d_gate_ref,
    d_up_ref,
    d_normed_ref,
):
    d_hidden = matmul(cotangent_ref[...], down_ref[...], ((1,), (1,)))
    gate, up = gate_lin_ref[...], up_lin_ref[...]
    sigmoid = jax.nn.sigmoid(gate)
    d_gate = (d_hidden * up * sigmoid * (1.0 + gate * (1.0 - sigmoid))).astype(jnp.bfloat16)
    d_up = (d_hidden * gate * sigmoid).astype(jnp.bfloat16)
    d_gate_ref[...] = d_gate
    d_up_ref[...] = d_up
    back = matmul(d_gate, gate_ref[...], ((1,), (1,))) + matmul(d_up, up_ref[...], ((1,), (1,)))
    first = pl.program_id(0) == 0

    @pl.when(first)
    def _():
        d_normed_ref[...] = back

    @pl.when(jnp.logical_not(first))
    def _():
        d_normed_ref[...] += back


FEED_WEIGHTS = [
    ((1024, 512), lambda j: (0, j)),
    ((1024, 512), lambda j: (0, 4 + j)),
    ((512, 1024), lambda j: (j % 2, 6 + j // 2)),
]


def feed_forward(normed_low, weights):
    rows = normed_low.shape[0]
    part = ((rows, 512), lambda j: (0, j))
    whole = ((rows, 1024), lambda j: (0, 0))
    return kernel_call(
        feed_kernel,
        4,
        [whole] + FEED_WEIGHTS,
        [
            ((rows, 2048), jnp.float32) + part,
            ((rows, 2048), jnp.float32) + part,
            ((rows, 2048), jnp.bfloat16) + part,
            ((rows, 1024), jnp.float32) + whole,
        ],
        6 * rows * 1024 * 2048,
        (normed_low, weights, weights, weights),
    )


def feed_backward(cotangent, gate_lin, up_lin, weights):
    rows = cotangent.shape[0]
    part = ((rows, 512), lambda j: (0, j))
    whole = ((rows, 1024), lambda j: (0, 0))
    return kernel_call(
        feed_back_kernel,
        4,
        [whole, part, part] + FEED_WEIGHTS,
        [
            ((rows, 2048), jnp.bfloat16) + part,
            ((rows, 2048), jnp.bfloat16) + part,
            ((rows, 1024), jnp.float32) + whole,
        ],
        6 * rows * 1024 * 2048,
        (cotangent, gate_lin, up_lin, weights, weights, weights),
    )


def attend(query_t, kv_heads, kv_t, bias):
    keys, rows = bias.shape
    size = HEAD_WIDTH
    return kernel_call(
        attend_kernel,
        QUERY_HEADS,
        [
            ((size, rows), lambda h: (h, 0)),
            ((1, keys, size), lambda h: (h // 4, 0, 0)),
            ((size, keys), lambda h: (2 + h // 4, 0)),
            ((keys, rows), lambda h: (0, 0)),
        ],
        [
            ((QUERY_HEADS * size, rows), jnp.bfloat16, (size, rows), lambda h: (h, 0)),
            ((QUERY_HEADS, 1, rows), jnp.float32, (1, 1, rows), lambda h: (h, 0, 0)),
        ],
        4 * QUERY_HEADS * size * rows * keys * 4,
        (query_t, kv_heads, kv_t, bias),
    )


def attend_back(query_t, query_heads, out_t, out_heads, kv_heads, kv_t, bias, totals):
    keys, rows = bias.shape
    size = HEAD_WIDTH
    return kernel_call(
        attend_back_kernel,
        QUERY_HEADS,
        [
            ((size, rows), lambda h: (h, 0)),
            ((1, rows, size), lambda h: (h, 0, 0)),
            ((size, rows), lambda h: (h, 0)),
            ((1, rows, size), lambda h: (h, 0, 0)),
            ((1, keys, size), lambda h: (h // 4, 0, 0)),
            ((1, keys, size), lambda h: (2 + h // 4, 0, 0)),
            ((size, keys), lambda h: (h // 4, 0)),
            ((keys, rows), lambda h: (0, 0)),
            ((1, 1, rows), lambda h: (h, 0, 0)),
        ],
        [
            ((QUERY_HEADS * size, rows), jnp.float32, (size, rows), lambda h: (h, 0)),
            (
                (KEY_VALUE_HEADS, keys, 2 * size),
                jnp.float32,
                (1, keys, 2 * size),
                lambda h: (h // 4, 0, 0),
            ),
        ],
        10 * QUERY_HEADS * size * rows * keys * 4,
        (query_t, query_heads, out_t, out_heads, kv_heads, kv_heads, kv_t, bias, totals),
    )


def pair_blocks(rows):
    return (
        ((rows, 2 * MP), lambda i: (0, i)),
        ((rows, rows), lambda i: (0, 0)),
        ((1, rows, 2), lambda i: (i, 0, 0)),
        ((1, 2, rows), lambda i: (i, 0, 0)),
    )


def within_block(inputs_low, inter, bias, columns, rows_of):
    rows = inter.shape[0]
    wide, square, column, row = pair_blocks(rows)
    return kernel_call(
        within_kernel,
        MH // 2,
        [wide, square, square, column, row],
        [((rows, MH * MP), jnp.float32) + wide],
        16 * MH * MP * rows * rows,
        (inputs_low, inter, bias, columns, rows_of),
    )[0]


def within_block_back(inputs_low, grad_low, inter_t, bias_t, columns, rows_of):
    rows = inter_t.shape[0]
    wide, square, column, row = pair_blocks(rows)
    return kernel_call(
        within_back_kernel,
        MH // 2,
        [wide, wide, square, square, column, row],
        [
            ((rows, MH * MP), jnp.float32) + wide,
            ((rows, rows), jnp.float32) + square,
            ((MH // 2, rows, 2), jnp.float32) + column,
            ((MH // 2, 2, rows), jnp.float32) + row,
        ],
        32 * MH * MP * rows * rows,
        (inputs_low, grad_low, inter_t, bias_t, columns, rows_of),
    )


def project(left, right):
    return jnp.dot(left, right, preferred_element_type=jnp.float32)


def input_grad(left, right):
    return jnp.einsum("rk,rj->kj", left, right, preferred_element_type=jnp.float32)


def back_through(grad_low, weight_full):
    return jnp.einsum("rj,kj->rk", grad_low, weight_full, preferred_element_type=jnp.float32)


def swiglu(gate_values, up_values):
    return jax.nn.silu(gate_values) * up_values


def gating(scan_values, gate_values):
    return scan_values * jax.nn.silu(gate_values)


def on_device(
    tokens,
    segments,
    cotangent,
    attention_gain,
    query_weight,
    key_matrix,
    value_matrix,
    attention_out,
    gate_weight,
    mixer_weight,
    step_weight,
    mixer_out,
    conv_weight,
    conv_bias,
    step_bias,
    decay_log,
    skip_gain,
    feed_gain,
    feed_gate,
    feed_up,
    feed_down,
):
    block_index = lax.axis_index("context")
    core = block_index % 2
    chip = block_index // 2
    both = ("dp", "context")
    step_padded = jnp.pad(step_weight, ((0, 0), (0, IN_WIDTH - IN_USED)))
    in_shard = jnp.concatenate(
        [query_weight, key_matrix, value_matrix, gate_weight, mixer_weight, step_padded], axis=1
    )
    in_full = lax.all_gather(
        lax.dynamic_slice_in_dim(in_shard, block_index * 8, 8, 0), both, axis=0, tiled=True
    )
    def hidden_order(block):
        return block.reshape(8, 16, 2, 64).transpose(0, 2, 1, 3).reshape(8, 2048)

    feed_shard = jnp.concatenate(
        [
            hidden_order(lax.dynamic_slice_in_dim(feed_gate, block_index * 8, 8, 0)),
            hidden_order(lax.dynamic_slice_in_dim(feed_up, block_index * 8, 8, 0)),
        ],
        axis=1,
    )
    out_rows_own = jnp.concatenate([attention_out, mixer_out, feed_down], axis=0)
    out_shard = [
        lax.dynamic_slice_in_dim(out_rows_own, group * 64 + block_index * 8, 8, 0)
        for group in range(4)
    ]
    late_full = lax.all_gather(
        jnp.concatenate([feed_shard] + out_shard, axis=1), both, axis=0, tiled=True
    )
    first_rows = late_full[:, 4096:5120].reshape(16, 64, 1024)
    second_rows = late_full[:, 5120:6144].reshape(16, 64, 1024)
    out_full = first_rows[:, :32].reshape(512, 1024)
    mixer_out_full = jnp.concatenate([first_rows[:, 32:], second_rows], axis=1).reshape(1536, 1024)
    count_of_rows = tokens.shape[0]
    tap_count = conv_weight.shape[0]
    inner_width = MH * MP
    width_of_keys = KEY_VALUE_HEADS * HEAD_WIDTH
    query_places = block_index * count_of_rows + jnp.arange(count_of_rows, dtype=jnp.int32)
    place_float = query_places.astype(jnp.float32)
    seg_float = segments.astype(jnp.float32)
    seg_low = segments.astype(jnp.bfloat16)
    hidden_in = tokens.astype(jnp.float32)
    normed, norm_one_back = jax.vjp(rms_norm, hidden_in, attention_gain)
    normed_low = normed.astype(jnp.bfloat16)
    every_lin = project(normed_low, in_full)
    query_lin = every_lin[:, :512]
    key_lin = every_lin[:, 512:640]
    value_lin = every_lin[:, 640:768]
    gate_lin = every_lin[:, 768:2304]
    mixer_lin = every_lin[:, 2304:4096]
    step_lin = every_lin[:, 4096:IN_USED]
    rotated_queries = rotary(query_lin, place_float, 1.0).astype(jnp.bfloat16)
    rotated_keys = rotary(key_lin, place_float, 1.0).astype(jnp.bfloat16)
    value_reduced = value_lin.astype(jnp.bfloat16)
    sent = jnp.concatenate(
        [
            jnp.concatenate([rotated_keys, value_reduced], axis=1),
            jnp.pad(seg_low[None, :], ((0, 7), (0, 0))),
        ],
        axis=0,
    )
    sent, mixer_lin, gate_lin, step_lin = lax.optimization_barrier(
        (sent, mixer_lin, gate_lin, step_lin)
    )
    along = jnp.stack([sent] + [shift_chips(sent, k) for k in range(1, 4)])
    slots = jnp.concatenate([along, swap_cores(along)], axis=0)
    kv_heads = slots[:, :count_of_rows].reshape(-1, 4, HEAD_WIDTH).transpose(1, 0, 2)
    kv_t = kv_heads.transpose(0, 2, 1).reshape(4 * HEAD_WIDTH, -1)
    seg_all = slots[:, count_of_rows].reshape(-1)
    owners = jnp.concatenate(
        [(chip - jnp.arange(4)) % 4 * 2 + core, (chip - jnp.arange(4)) % 4 * 2 + 1 - core]
    )
    key_places = (
        owners[:, None] * count_of_rows + jnp.arange(count_of_rows, dtype=jnp.int32)[None, :]
    ).reshape(-1)
    attention_bias = jnp.where(
        (key_places[:, None] <= query_places[None, :]) & (seg_all[:, None] == seg_low[None, :]),
        0.0,
        masked_fill,
    ).astype(jnp.bfloat16)
    scale_factor = 1.0 / math.sqrt(HEAD_WIDTH)
    query_scaled = rotated_queries * jnp.asarray(scale_factor, jnp.bfloat16)
    query_t = query_scaled.T
    attended_t, totals = attend(query_t, kv_heads, kv_t, attention_bias)
    attended_low = attended_t.T
    attention_branch = project(attended_low, out_full)
    prev_rows, prev_segs = from_behind(
        (mixer_lin[count_of_rows - tap_count + 1 :], seg_float[count_of_rows - tap_count + 1 :]),
        "context",
        1,
    )
    extended = jnp.concatenate([prev_rows, mixer_lin], axis=0)
    seg_extended = jnp.concatenate([prev_segs, seg_float])
    seg_before = prev_segs[-1]

    def mixer_piece(ext_rows, conv_taps, conv_shift, step_raw, step_shift, decay_logs):
        return mixer_inputs(
            ext_rows,
            seg_extended,
            seg_float,
            conv_taps,
            conv_shift,
            step_raw,
            step_shift,
            decay_logs,
        )

    (activated, step_size, log_rate), mixer_back = jax.vjp(
        mixer_piece, extended, conv_weight, conv_bias, step_lin, step_bias, decay_log
    )
    mixer_x = activated[:, :inner_width]
    bees = activated[:, inner_width : inner_width + NS].astype(jnp.bfloat16)
    seas = activated[:, inner_width + NS :].astype(jnp.bfloat16)

    def decay_piece(rates):
        return decay_terms(rates, seg_float, seg_before)

    (running, entry, leaving, carried), decay_back = jax.vjp(decay_piece, log_rate)
    spread = heads_to_columns(jnp.concatenate([step_size, leaving, entry], axis=0))
    step_wide = spread[:count_of_rows]
    leaving_wide = spread[count_of_rows : 2 * count_of_rows]
    entry_wide = spread[2 * count_of_rows :]
    inputs_low = (mixer_x * step_wide).astype(jnp.bfloat16)
    weighted_low = (inputs_low.astype(jnp.float32) * leaving_wide).astype(jnp.bfloat16)
    local_state = input_grad(bees, weighted_low)
    carried_wide = jnp.repeat(carried, MP)
    skip_wide = jnp.repeat(skip_gain, MP)[None, :]
    incoming_low = carried_in(carried_wide, local_state, False)
    index_rows = jnp.arange(count_of_rows)
    block_allowed = (index_rows[:, None] >= index_rows[None, :]) & (
        seg_float[:, None] == seg_float[None, :]
    )
    block_bias = jnp.where(block_allowed, 0.0, masked_fill)
    running_rows = running.T.reshape(MH // 2, 2, count_of_rows)
    running_columns = running_rows.transpose(0, 2, 1)
    intersection = matmul(seas, bees, ((1,), (1,)))
    inner = within_block(inputs_low, intersection, block_bias, running_columns, running_rows)
    from_state = project(seas, incoming_low)
    scanned = inner + from_state * entry_wide + skip_wide * mixer_x
    gated, gating_back = jax.vjp(gating, scanned, gate_lin)
    gated_low = gated.astype(jnp.bfloat16)
    mixer_branch = project(gated_low, mixer_out_full)
    residual = hidden_in + attention_multiplier * attention_branch + mixer_multiplier * mixer_branch
    normed_two, norm_two_back = jax.vjp(rms_norm, residual, feed_gain)
    normed_two_low = normed_two.astype(jnp.bfloat16)
    ffn_gate_lin, ffn_up_lin, hidden_low, feed_out = feed_forward(normed_two_low, late_full)
    output = (residual + feed_out).astype(jnp.bfloat16)
    upstream = cotangent.astype(jnp.float32)
    d_ffn_gate, d_ffn_up, d_normed_two = feed_backward(
        cotangent, ffn_gate_lin, ffn_up_lin, late_full
    )
    d_feed_low = jnp.stack([d_ffn_gate, d_ffn_up])
    d_resid_norm, grad_feed_gain = norm_two_back(d_normed_two)
    d_residual = upstream + d_resid_norm
    d_attn_low = (attention_multiplier * d_residual).astype(jnp.bfloat16)
    d_mixer_low = (mixer_multiplier * d_residual).astype(jnp.bfloat16)

    feed_got = swap_cores(
        input_grad(normed_two_low, d_feed_low[1 - core]).astype(jnp.bfloat16)
    )
    feed_own = (
        input_grad(normed_two_low, d_feed_low[core]) + feed_got.astype(jnp.float32)
    ).astype(jnp.bfloat16)
    attended_gradient = back_through(d_attn_low, out_full).astype(jnp.bfloat16)
    d_gated = back_through(d_mixer_low, mixer_out_full)
    d_scan_flat, d_gate_lin = gating_back(d_gated)
    d_gate_low = d_gate_lin.astype(jnp.bfloat16)

    def out_grads(which):
        attn = input_grad(attended_low, half(d_attn_low, which, 1)).astype(jnp.bfloat16)
        mix = input_grad(gated_low, half(d_mixer_low, which, 1)).astype(jnp.bfloat16)
        down = input_grad(hidden_low, half(cotangent, which, 1)).astype(jnp.bfloat16)
        gate = input_grad(normed_low, half(d_gate_low, which, 1)).astype(jnp.bfloat16)
        return (attn, mix, down, gate)

    out_got = jax.tree.map(swap_cores, out_grads(1 - core))
    early = jax.tree.map(lambda a, b: a + b, out_grads(core), out_got)
    mix_rows = early[1].reshape(16, 96, 512)
    early_rows = jnp.concatenate(
        [
            feed_own,
            early[3],
            jnp.concatenate([early[0].reshape(16, 32, 512), mix_rows[:, :32]], axis=1).reshape(
                1024, 512
            ),
            mix_rows[:, 32:].reshape(1024, 512),
            early[2][:1024],
            early[2][1024:],
        ],
        axis=1,
    )
    d_scan_low = d_scan_flat.astype(jnp.bfloat16)
    d_scan = d_scan_low.astype(jnp.float32)
    d_from_low = (d_scan * entry_wide).astype(jnp.bfloat16)
    d_incoming = input_grad(seas, d_from_low)
    attended_gradient, early_rows, d_incoming = lax.optimization_barrier(
        (attended_gradient, early_rows, d_incoming)
    )
    early_shard = lax.psum_scatter(early_rows, "dp", scatter_dimension=0, tiled=True)
    d_state_low = carried_in(carried_wide, d_incoming, True)
    d_query_t, d_kv = attend_back(
        query_t,
        query_scaled.reshape(count_of_rows, QUERY_HEADS, HEAD_WIDTH).transpose(1, 0, 2),
        attended_gradient.T,
        attended_gradient.reshape(count_of_rows, QUERY_HEADS, HEAD_WIDTH).transpose(1, 0, 2),
        kv_heads,
        kv_t,
        attention_bias,
        totals,
    )
    d_scan_low, d_kv = lax.optimization_barrier((d_scan_low, d_kv))
    d_query_rot = d_query_t.T * scale_factor
    slot_grads = d_kv.astype(jnp.bfloat16).reshape(KEY_VALUE_HEADS, 2, 4, count_of_rows, -1)
    chip_grads = slot_grads[:, 0].astype(jnp.float32) + swap_cores(slot_grads[:, 1]).astype(
        jnp.float32
    )
    chip_low = chip_grads.astype(jnp.bfloat16)
    own_grads = chip_grads[:, 0]
    for k in range(1, 4):
        own_grads = own_grads + shift_chips(chip_low[:, k], -k).astype(jnp.float32)
    key_grads = jnp.concatenate(
        [
            own_grads[0, :, :HEAD_WIDTH],
            own_grads[1, :, :HEAD_WIDTH],
            own_grads[0, :, HEAD_WIDTH:],
            own_grads[1, :, HEAD_WIDTH:],
        ],
        axis=1,
    )
    d_query_low = rotary(d_query_rot, place_float, -1.0).astype(jnp.bfloat16)
    d_key_low = rotary(key_grads[:, :width_of_keys], place_float, -1.0).astype(jnp.bfloat16)
    d_value_low = key_grads[:, width_of_keys:].astype(jnp.bfloat16)
    d_inputs, d_inter_t, d_columns, d_rows = within_block_back(
        inputs_low, d_scan_low, intersection.T, block_bias.T, running_columns, running_rows
    )
    d_running = (d_rows - d_columns.transpose(0, 2, 1)).reshape(MH, count_of_rows).T
    d_inter_low = d_inter_t.astype(jnp.bfloat16)
    d_seas = back_through(d_from_low, incoming_low) + input_grad(d_inter_low, bees)
    d_bees = project(d_inter_low, seas) + back_through(weighted_low, d_state_low)
    d_weighted = project(bees, d_state_low)
    d_inputs = d_inputs + d_weighted * leaving_wide
    d_mixer_x = skip_wide * d_scan + d_inputs * step_wide
    d_entry = columns_to_heads(d_scan * from_state)
    d_leaving = columns_to_heads(d_weighted * inputs_low.astype(jnp.float32))
    d_step = columns_to_heads(d_inputs * mixer_x)
    sums = columns_to_heads(
        jnp.concatenate(
            [
                jnp.sum(d_scan * mixer_x, axis=0, keepdims=True),
                jnp.sum(
                    d_state_low.astype(jnp.float32) * incoming_low.astype(jnp.float32),
                    axis=0,
                    keepdims=True,
                ),
            ],
            axis=0,
        )
    )
    grad_skip_gain, d_carried = sums[0], sums[1]
    (d_rate,) = decay_back((d_running, d_entry, d_leaving, d_carried))
    d_activated = jnp.concatenate([d_mixer_x, d_bees, d_seas], axis=1)
    d_extended, grad_conv_weight, grad_conv_bias, d_step_lin, grad_step_bias, grad_decay_log = (
        mixer_back((d_activated, d_step, d_rate))
    )
    rim_back = from_behind(d_extended[: tap_count - 1], "context", -1)
    d_mixer_lin = d_extended[tap_count - 1 :] + jnp.pad(
        rim_back, ((count_of_rows - tap_count + 1, 0), (0, 0))
    )
    d_late_low = jnp.concatenate(
        [
            d_query_low,
            d_key_low,
            d_value_low,
            d_mixer_lin.astype(jnp.bfloat16),
            jnp.pad(d_step_lin, ((0, 0), (0, IN_WIDTH - IN_USED))).astype(jnp.bfloat16),
        ],
        axis=1,
    )

    def summed_over_all(grad_low):
        width = grad_low.shape[1] // 2
        got = swap_cores(input_grad(normed_low, half(grad_low, 1 - core, 1)).astype(jnp.bfloat16))
        own = input_grad(normed_low, half(grad_low, core, 1)) + got.astype(jnp.float32)
        parts = lax.all_to_all(
            own.astype(jnp.bfloat16).reshape(64, 16, width),
            both,
            0,
            0,
            axis_index_groups=CORE_GROUPS,
        )
        total = jnp.sum(parts.astype(jnp.float32), axis=0).astype(jnp.bfloat16)
        spread_all = copies_of(total).reshape(4, 2, 16, width).astype(jnp.float32)
        return spread_all.transpose(0, 2, 1, 3).reshape(64, 2 * width)

    late_all = summed_over_all(d_late_low)
    d_every_low = jnp.concatenate([d_late_low[:, :768], d_gate_low, d_late_low[:, 768:]], axis=1)
    one, two, three = (shift_chips(early_shard, k).astype(jnp.float32) for k in range(1, 4))
    early_mine = ((early_shard.astype(jnp.float32) + two) + (one + three)).astype(jnp.bfloat16)
    early_other = swap_cores(early_mine)
    early_low = jnp.where(core == 0, early_mine, early_other).astype(jnp.float32)
    early_high = jnp.where(core == 0, early_other, early_mine).astype(jnp.float32)

    def joined(start, width):
        return jnp.concatenate(
            [early_low[:, start : start + width], early_high[:, start : start + width]], axis=1
        )

    def hidden_back(block):
        return block.reshape(64, 2, 16, 64).transpose(0, 2, 1, 3).reshape(64, 2048)

    first_out = joined(2816, 512)
    d_normed = back_through(d_every_low, in_full)
    d_tokens_norm, grad_attention_gain = norm_one_back(d_normed)
    grad_tokens = d_residual + d_tokens_norm

    def flat(part):
        part = part.reshape(-1)
        return jnp.pad(part, (0, -part.size % 128))

    pieces = (
        grad_attention_gain,
        grad_conv_weight,
        grad_conv_bias,
        grad_step_bias,
        grad_decay_log,
        grad_skip_gain,
        grad_feed_gain,
    )
    packed = jnp.concatenate([flat(part) for part in pieces])
    packed = sum_everywhere(jnp.pad(packed, (0, -packed.size % 1024)).reshape(-1, 128)).reshape(-1)
    small, start = [], 0
    for part in pieces:
        small.append(packed[start : start + part.size].reshape(part.shape))
        start += part.size + -part.size % 128
    summed = (
        late_all[:, :512],
        late_all[:, 512:640],
        late_all[:, 640:768],
        first_out[:32],
        joined(2048, 768),
        late_all[:, 768:2560],
        late_all[:, 2560 : 2560 + MH],
        jnp.concatenate([first_out[32:], joined(3328, 512)], axis=0),
        hidden_back(early_low[:, :2048]),
        hidden_back(early_high[:, :2048]),
        jnp.concatenate([joined(3840, 512), joined(4352, 512)], axis=0),
    )
    return (
        output,
        grad_tokens,
        small[0],
        summed[0],
        summed[1],
        summed[2],
        summed[3],
        summed[4],
        summed[5],
        summed[6],
        summed[7],
        small[1],
        small[2],
        small[3],
        small[4],
        small[5],
        small[6],
        summed[8],
        summed[9],
        summed[10],
    )


def solution(mesh):
    return jax.shard_map(
        on_device,
        mesh=mesh,
        in_specs=(
            P(("dp", "context"), None),
            P(("dp", "context")),
            P(("dp", "context"), None),
            P(),
            P("dp", None),
            P("dp", None),
            P("dp", None),
            P("dp", None),
            P("dp", None),
            P("dp", None),
            P("dp", None),
            P("dp", None),
            P(),
            P(),
            P(),
            P(),
            P(),
            P(),
            P("dp", None),
            P("dp", None),
            P("dp", None),
        ),
        out_specs=(
            P(("dp", "context"), None),
            P(("dp", "context"), None),
            P(),
            P("dp", None),
            P("dp", None),
            P("dp", None),
            P("dp", None),
            P("dp", None),
            P("dp", None),
            P("dp", None),
            P("dp", None),
            P(),
            P(),
            P(),
            P(),
            P(),
            P(),
            P("dp", None),
            P("dp", None),
            P("dp", None),
        ),
        check_vma=False,
    )
```

```python
import math

import jax
import jax.numpy as jnp
from jax import lax
from jax.experimental import pallas as pl
from jax.experimental.pallas import tpu as pltpu
from jax.sharding import PartitionSpec as P

QUERY_HEADS = 8
KEY_VALUE_HEADS = 2
HEAD_WIDTH = 64
MH = 24
MP = 64
NS = 128


EPSILON = 1e-05
masked_fill = -1e30
attention_multiplier = 0.9375
mixer_multiplier = 0.2357
rotary_base = 100000000000.0
IN_USED = 4120
IN_WIDTH = 4352
CHIP_GROUPS = [[2 * z + c for z in range(4)] for c in range(2)]
CORE_GROUPS = [[8 * d + 2 * z + c for d in range(16) for z in range(4)] for c in range(2)]


def from_behind(block, axis, distance):
    devices = range(lax.axis_size(axis))
    route = [(i - distance, i) for i in devices if i - distance in devices]
    return lax.ppermute(block, axis, route)


def swap_cores(block):
    devices = range(lax.axis_size("context"))
    return lax.ppermute(block, "context", [(i, i ^ 1) for i in devices])


def shift_chips(block, distance):
    devices = lax.axis_size("context")
    return lax.ppermute(
        block, "context", [(i, (i + 2 * distance) % devices) for i in range(devices)]
    )


def shift_other(block, distance):
    devices = lax.axis_size("context")
    route = [(i, (i + 2 * distance) % devices ^ 1) for i in range(devices)]
    return lax.ppermute(block, "context", route)


def from_everyone(block):
    near = [block] + [shift_chips(block, k) for k in range(1, 4)]
    return near + [shift_other(block, k) for k in range(4)]


def shift_rows(block, distance, stride):
    route = []
    for i in range(16):
        place = i // stride % 4
        route.append((i, i + ((place + distance) % 4 - place) * stride))
    return lax.ppermute(block, "dp", route)


def sum_of_four(block, shift):
    one, two, three = shift(block, 1), shift(block, 2), shift(block, 3)
    return (block + two) + (one + three)


def sum_everywhere(block):
    block = block + swap_cores(block)
    block = sum_of_four(block, shift_chips)
    block = sum_of_four(block, lambda part, k: shift_rows(part, k, 1))
    return sum_of_four(block, lambda part, k: shift_rows(part, k, 4))


def half(block, which, axis):
    size = block.shape[axis] // 2
    return lax.dynamic_slice_in_dim(block, which * size, size, axis)


def copies_of(block):
    devices = lax.axis_size("context")
    return lax.all_to_all(
        jnp.broadcast_to(block[None], (devices,) + block.shape), "context", 0, 0
    )


def chip_decays(carried):
    mine = lax.axis_index("context")
    core = mine % 2
    own = half(carried, core, 0)
    got = half(swap_cores(carried), core, 0)
    whole = own * got
    return own, got, [whole] + [shift_chips(whole, k) for k in range(1, 4)]


def carried_in(decays, local, reverse):
    mine = lax.axis_index("context")
    core, chip = mine % 2, mine // 2
    is_first = (core == 1) if reverse else (core == 0)
    order = 3 - chip if reverse else chip
    way = -1 if reverse else 1
    own_decay, got_decay, shifted = decays
    own_part = half(local, core, 1)
    got_part = swap_cores(half(local, 1 - core, 1).astype(jnp.bfloat16)).astype(jnp.float32)
    first = jnp.where(is_first, own_part, got_part)
    second = jnp.where(is_first, got_part, own_part)
    first_decay = jnp.where(is_first, own_decay, got_decay)
    second_decay = jnp.where(is_first, got_decay, own_decay)
    chip_low = (first * second_decay[None, :] + second).astype(jnp.bfloat16)
    total = jnp.zeros_like(first)
    factor = jnp.ones_like(own_decay)
    for k in range(1, 4):
        part = shift_chips(chip_low, way * k).astype(jnp.float32)
        reach = jnp.where(order >= k, factor, 0.0)
        total = total + reach[None, :] * part
        if k < 3:
            factor = factor * shifted[way * k % 4]
    for_first = total
    for_second = total * first_decay[None, :] + first
    keep = jnp.where(is_first, for_first, for_second)
    give = jnp.where(is_first, for_second, for_first)
    got = swap_cores(give.astype(jnp.bfloat16))
    keep = keep.astype(jnp.bfloat16)
    return jnp.where(
        core == 0, jnp.concatenate([keep, got], axis=1), jnp.concatenate([got, keep], axis=1)
    )


def rms_norm(values, gain_vector):
    return (
        values
        * lax.rsqrt(jnp.mean(values * values, axis=-1, keepdims=True) + EPSILON)
        * gain_vector
    )


def rotary(values, places, direction):
    count_of_rows = values.shape[0]
    head_count = values.shape[1] // HEAD_WIDTH
    half_size = HEAD_WIDTH // 2
    frequency = rotary_base ** (-2.0 * jnp.arange(half_size, dtype=jnp.float32) / HEAD_WIDTH)
    angles = places[:, None] * frequency[None, :]
    cosine = jnp.cos(angles)[:, None, :]
    sine_part = direction * jnp.sin(angles)[:, None, :]
    per_head = values.reshape(count_of_rows, head_count, HEAD_WIDTH)
    front_half = per_head[:, :, :half_size]
    back_half = per_head[:, :, half_size:]
    turned = jnp.concatenate(
        [front_half * cosine - back_half * sine_part, back_half * cosine + front_half * sine_part],
        axis=-1,
    )
    return turned.reshape(count_of_rows, head_count * HEAD_WIDTH)


def mixer_inputs(
    extended, seg_extended, seg_own, conv_taps, conv_shift, step_raw, step_shift, decay_logs
):
    count_of_rows = seg_own.shape[0]
    mixed = conv_shift[None, :]
    for tap_index in range(conv_taps.shape[0]):
        same_doc = (seg_extended[tap_index : tap_index + count_of_rows] == seg_own).astype(
            jnp.float32
        )
        mixed = (
            mixed
            + conv_taps[tap_index][None, :]
            * extended[tap_index : tap_index + count_of_rows]
            * same_doc[:, None]
        )
    activated = jax.nn.silu(mixed)
    step_size = jax.nn.softplus(step_raw + step_shift[None, :])
    log_rate = step_size * (-jnp.exp(decay_logs))[None, :]
    return (activated, step_size, log_rate)


def decay_terms(log_rate, seg_own, seg_before):
    count_of_rows = log_rate.shape[0]
    index_rows = jnp.arange(count_of_rows)
    lower = (index_rows[:, None] >= index_rows[None, :]).astype(jnp.float32)
    running = jnp.dot(lower, log_rate, precision=lax.Precision.HIGHEST)
    entry = jnp.exp(running) * (seg_own == seg_before).astype(jnp.float32)[:, None]
    leaving = (
        jnp.exp(running[-1][None, :] - running)
        * (seg_own == seg_own[-1]).astype(jnp.float32)[:, None]
    )
    carried = jnp.exp(running[-1]) * (seg_own[-1] == seg_before).astype(jnp.float32)
    return (running, entry, leaving, carried)


def heads_to_columns(values):
    spread = jnp.repeat(jnp.eye(MH, dtype=jnp.float32), MP, axis=1)
    return jnp.dot(values, spread, precision=lax.Precision.HIGH)


def columns_to_heads(values):
    spread = jnp.repeat(jnp.eye(MH, dtype=jnp.float32), MP, axis=1)
    return jnp.einsum("ic,hc->ih", values, spread, precision=lax.Precision.HIGH)


def matmul(left, right, sides=((1,), (0,))):
    return lax.dot_general(left, right, (sides, ((), ())), preferred_element_type=jnp.float32)


def attend_kernel(*refs):
    query_ref, slots, bias_ref = refs[0], refs[1:9], refs[9]
    out_ref, total_ref, heads_ref, turned_ref = refs[10:]
    head = pl.program_id(0)
    rows = slots[0].shape[0]

    @pl.when(head == 0)
    def _():
        for place, slot in enumerate(slots):
            block = slot[...]
            span = slice(place * rows, (place + 1) * rows)
            for part in range(4):
                heads_ref[part, span, :] = block[:, part * HEAD_WIDTH : (part + 1) * HEAD_WIDTH]
            turned_ref[:, span] = block.astype(jnp.float32).T.astype(jnp.bfloat16)

    group = head // 4
    value_rows = pl.ds(pl.multiple_of((2 + group) * HEAD_WIDTH, HEAD_WIDTH), HEAD_WIDTH)
    scores = matmul(heads_ref[group], query_ref[...]) + bias_ref[...].astype(jnp.float32)
    top = jnp.max(scores, axis=0, keepdims=True)
    exponent = jnp.exp(scores - top)
    total = jnp.sum(exponent, axis=0, keepdims=True)
    probs = (exponent * (1.0 / total)).astype(jnp.bfloat16)
    out_ref[...] = matmul(turned_ref[value_rows, :], probs).astype(jnp.bfloat16)
    total_ref[0] = top + jnp.log(total)


def attend_back_kernel(
    query_t_ref,
    query_ref,
    out_t_ref,
    out_ref,
    key_ref,
    value_ref,
    key_t_ref,
    bias_ref,
    total_ref,
    d_query_ref,
    d_key_ref,
):
    scores = matmul(key_ref[0], query_t_ref[...]) + bias_ref[...].astype(jnp.float32)
    probs = jnp.exp(scores - total_ref[0])
    d_probs = matmul(value_ref[0], out_t_ref[...])
    delta = jnp.sum(probs * d_probs, axis=0, keepdims=True)
    d_scores = (probs * (d_probs - delta)).astype(jnp.bfloat16)
    d_query_ref[...] = matmul(key_t_ref[...], d_scores)
    d_key = matmul(d_scores, query_ref[0])
    d_value = matmul(probs.astype(jnp.bfloat16), out_ref[0])
    both = jnp.concatenate([d_key, d_value], axis=1)
    first = pl.program_id(0) % 4 == 0

    @pl.when(first)
    def _():
        d_key_ref[0] = both

    @pl.when(jnp.logical_not(first))
    def _():
        d_key_ref[0] += both


def within_kernel(inputs_ref, inter_ref, bias_ref, column_ref, row_ref, out_ref):
    parts = []
    for p in range(2):
        within = jnp.exp(column_ref[0, :, p : p + 1] - row_ref[0, p : p + 1, :] + bias_ref[...])
        mixing = (inter_ref[...] * within).astype(jnp.bfloat16)
        parts.append(matmul(mixing, inputs_ref[...]))
    lane = lax.broadcasted_iota(jnp.int32, parts[0].shape, 1)
    out_ref[...] = jnp.where(lane < MP, parts[0], parts[1])


def within_back_kernel(
    inputs_ref,
    grad_ref,
    inter_ref,
    bias_ref,
    column_ref,
    row_ref,
    d_inputs_ref,
    d_inter_ref,
    d_column_ref,
    d_row_ref,
):
    lane = lax.broadcasted_iota(jnp.int32, inputs_ref.shape, 1)
    parts, columns, rows, d_inter = [], [], [], None
    for p in range(2):
        within = jnp.exp(row_ref[0, p : p + 1, :] - column_ref[0, :, p : p + 1] + bias_ref[...])
        mixing = inter_ref[...] * within
        parts.append(matmul(mixing.astype(jnp.bfloat16), grad_ref[...]))
        own = (lane < MP) if p == 0 else (lane >= MP)
        own_inputs = jnp.where(own, inputs_ref[...].astype(jnp.float32), 0.0)
        d_mixing = matmul(own_inputs.astype(jnp.bfloat16), grad_ref[...], ((1,), (1,)))
        product = d_mixing * mixing
        rows.append(jnp.sum(product, axis=0, keepdims=True))
        columns.append(jnp.sum(product, axis=1, keepdims=True))
        term = d_mixing * within
        d_inter = term if d_inter is None else d_inter + term
    d_inputs_ref[...] = jnp.where(lane < MP, parts[0], parts[1])
    d_row_ref[0] = jnp.concatenate(rows, axis=0)
    d_column_ref[0] = jnp.concatenate(columns, axis=1)
    first = pl.program_id(0) == 0

    @pl.when(first)
    def _():
        d_inter_ref[...] = d_inter

    @pl.when(jnp.logical_not(first))
    def _():
        d_inter_ref[...] += d_inter


def kernel_call(kernel, steps, ins, outs, flops, args):
    out_shape = [jax.ShapeDtypeStruct(shape, kind) for shape, kind, _, _ in outs]
    return pl.pallas_call(
        kernel,
        grid=(steps,),
        in_specs=[pl.BlockSpec(block, where) for block, where in ins],
        out_specs=[pl.BlockSpec(block, where) for _, _, block, where in outs],
        out_shape=out_shape,
        compiler_params=pltpu.CompilerParams(vmem_limit_bytes=48 * 1024 * 1024),
        cost_estimate=pl.CostEstimate(flops=flops, bytes_accessed=4 << 20, transcendentals=4 << 20),
    )(*args)


def feed_kernel(normed_ref, gate_ref, up_ref, down_ref, gate_lin_ref, up_lin_ref, hidden_ref, out_ref):
    gate = matmul(normed_ref[...], gate_ref[...])
    up = matmul(normed_ref[...], up_ref[...])
    gate_lin_ref[...] = gate
    up_lin_ref[...] = up
    hidden = (jax.nn.silu(gate) * up).astype(jnp.bfloat16)
    hidden_ref[...] = hidden
    out = matmul(hidden, down_ref[...])
    first = pl.program_id(0) == 0

    @pl.when(first)
    def _():
        out_ref[...] = out

    @pl.when(jnp.logical_not(first))
    def _():
        out_ref[...] += out


def feed_back_kernel(
    cotangent_ref,
    gate_lin_ref,
    up_lin_ref,
    gate_ref,
    up_ref,
    down_ref,
    d_gate_ref,
    d_up_ref,
    d_normed_ref,
):
    d_hidden = matmul(cotangent_ref[...], down_ref[...], ((1,), (1,)))
    gate, up = gate_lin_ref[...], up_lin_ref[...]
    sigmoid = jax.nn.sigmoid(gate)
    d_gate = (d_hidden * up * sigmoid * (1.0 + gate * (1.0 - sigmoid))).astype(jnp.bfloat16)
    d_up = (d_hidden * gate * sigmoid).astype(jnp.bfloat16)
    d_gate_ref[...] = d_gate
    d_up_ref[...] = d_up
    back = matmul(d_gate, gate_ref[...], ((1,), (1,))) + matmul(d_up, up_ref[...], ((1,), (1,)))
    first = pl.program_id(0) == 0

    @pl.when(first)
    def _():
        d_normed_ref[...] = back

    @pl.when(jnp.logical_not(first))
    def _():
        d_normed_ref[...] += back


FEED_WEIGHTS = [
    ((1024, 512), lambda j: (0, j)),
    ((1024, 512), lambda j: (0, 4 + j)),
    ((512, 1024), lambda j: (j % 2, 6 + j // 2)),
]


def feed_forward(normed_low, weights):
    rows = normed_low.shape[0]
    part = ((rows, 512), lambda j: (0, j))
    whole = ((rows, 1024), lambda j: (0, 0))
    return kernel_call(
        feed_kernel,
        4,
        [whole] + FEED_WEIGHTS,
        [
            ((rows, 2048), jnp.float32) + part,
            ((rows, 2048), jnp.float32) + part,
            ((rows, 2048), jnp.bfloat16) + part,
            ((rows, 1024), jnp.float32) + whole,
        ],
        6 * rows * 1024 * 2048,
        (normed_low, weights, weights, weights),
    )


def feed_backward(cotangent, gate_lin, up_lin, weights):
    rows = cotangent.shape[0]
    part = ((rows, 512), lambda j: (0, j))
    whole = ((rows, 1024), lambda j: (0, 0))
    return kernel_call(
        feed_back_kernel,
        4,
        [whole, part, part] + FEED_WEIGHTS,
        [
            ((rows, 2048), jnp.bfloat16) + part,
            ((rows, 2048), jnp.bfloat16) + part,
            ((rows, 1024), jnp.float32) + whole,
        ],
        6 * rows * 1024 * 2048,
        (cotangent, gate_lin, up_lin, weights, weights, weights),
    )


def attend(query_t, slots, bias):
    keys, rows = bias.shape
    size = HEAD_WIDTH
    return kernel_call(
        attend_kernel,
        QUERY_HEADS,
        [((size, rows), lambda h: (h, 0))]
        + [((rows, 4 * size), lambda h: (0, 0))] * 8
        + [((keys, rows), lambda h: (0, 0))],
        [
            ((QUERY_HEADS * size, rows), jnp.bfloat16, (size, rows), lambda h: (h, 0)),
            ((QUERY_HEADS, 1, rows), jnp.float32, (1, 1, rows), lambda h: (h, 0, 0)),
            ((4, keys, size), jnp.bfloat16, (4, keys, size), lambda h: (0, 0, 0)),
            ((4 * size, keys), jnp.bfloat16, (4 * size, keys), lambda h: (0, 0)),
        ],
        4 * QUERY_HEADS * size * rows * keys * 4,
        (query_t, *slots, bias),
    )


def attend_back(query_t, query_heads, out_t, out_heads, kv_heads, kv_t, bias, totals):
    keys, rows = bias.shape
    size = HEAD_WIDTH
    return kernel_call(
        attend_back_kernel,
        QUERY_HEADS,
        [
            ((size, rows), lambda h: (h, 0)),
            ((1, rows, size), lambda h: (h, 0, 0)),
            ((size, rows), lambda h: (h, 0)),
            ((1, rows, size), lambda h: (h, 0, 0)),
            ((1, keys, size), lambda h: (h // 4, 0, 0)),
            ((1, keys, size), lambda h: (2 + h // 4, 0, 0)),
            ((size, keys), lambda h: (h // 4, 0)),
            ((keys, rows), lambda h: (0, 0)),
            ((1, 1, rows), lambda h: (h, 0, 0)),
        ],
        [
            ((QUERY_HEADS * size, rows), jnp.float32, (size, rows), lambda h: (h, 0)),
            (
                (KEY_VALUE_HEADS, keys, 2 * size),
                jnp.float32,
                (1, keys, 2 * size),
                lambda h: (h // 4, 0, 0),
            ),
        ],
        10 * QUERY_HEADS * size * rows * keys * 4,
        (query_t, query_heads, out_t, out_heads, kv_heads, kv_heads, kv_t, bias, totals),
    )


def pair_blocks(rows):
    return (
        ((rows, 2 * MP), lambda i: (0, i)),
        ((rows, rows), lambda i: (0, 0)),
        ((1, rows, 2), lambda i: (i, 0, 0)),
        ((1, 2, rows), lambda i: (i, 0, 0)),
    )


def within_block(inputs_low, inter, bias, columns, rows_of):
    rows = inter.shape[0]
    wide, square, column, row = pair_blocks(rows)
    return kernel_call(
        within_kernel,
        MH // 2,
        [wide, square, square, column, row],
        [((rows, MH * MP), jnp.float32) + wide],
        16 * MH * MP * rows * rows,
        (inputs_low, inter, bias, columns, rows_of),
    )[0]


def within_block_back(inputs_low, grad_low, inter_t, bias_t, columns, rows_of):
    rows = inter_t.shape[0]
    wide, square, column, row = pair_blocks(rows)
    return kernel_call(
        within_back_kernel,
        MH // 2,
        [wide, wide, square, square, column, row],
        [
            ((rows, MH * MP), jnp.float32) + wide,
            ((rows, rows), jnp.float32) + square,
            ((MH // 2, rows, 2), jnp.float32) + column,
            ((MH // 2, 2, rows), jnp.float32) + row,
        ],
        32 * MH * MP * rows * rows,
        (inputs_low, grad_low, inter_t, bias_t, columns, rows_of),
    )


def project(left, right):
    return jnp.dot(left, right, preferred_element_type=jnp.float32)


def input_grad(left, right):
    return jnp.einsum("rk,rj->kj", left, right, preferred_element_type=jnp.float32)


def back_through(grad_low, weight_full):
    return jnp.einsum("rj,kj->rk", grad_low, weight_full, preferred_element_type=jnp.float32)


def swiglu(gate_values, up_values):
    return jax.nn.silu(gate_values) * up_values


def gating(scan_values, gate_values):
    return scan_values * jax.nn.silu(gate_values)


def on_device(
    tokens,
    segments,
    cotangent,
    attention_gain,
    query_weight,
    key_matrix,
    value_matrix,
    attention_out,
    gate_weight,
    mixer_weight,
    step_weight,
    mixer_out,
    conv_weight,
    conv_bias,
    step_bias,
    decay_log,
    skip_gain,
    feed_gain,
    feed_gate,
    feed_up,
    feed_down,
):
    block_index = lax.axis_index("context")
    core = block_index % 2
    chip = block_index // 2
    both = ("dp", "context")
    step_padded = jnp.pad(step_weight, ((0, 0), (0, IN_WIDTH - IN_USED)))
    in_shard = jnp.concatenate(
        [query_weight, key_matrix, value_matrix, gate_weight, mixer_weight, step_padded], axis=1
    )
    in_full = lax.all_gather(
        lax.dynamic_slice_in_dim(in_shard, block_index * 8, 8, 0), both, axis=0, tiled=True
    )
    def hidden_order(block):
        return block.reshape(8, 16, 2, 64).transpose(0, 2, 1, 3).reshape(8, 2048)

    feed_shard = jnp.concatenate(
        [
            hidden_order(lax.dynamic_slice_in_dim(feed_gate, block_index * 8, 8, 0)),
            hidden_order(lax.dynamic_slice_in_dim(feed_up, block_index * 8, 8, 0)),
        ],
        axis=1,
    )
    out_rows_own = jnp.concatenate([attention_out, mixer_out, feed_down], axis=0)
    out_shard = [
        lax.dynamic_slice_in_dim(out_rows_own, group * 64 + block_index * 8, 8, 0)
        for group in range(4)
    ]
    late_full = lax.all_gather(
        jnp.concatenate([feed_shard] + out_shard, axis=1), both, axis=0, tiled=True
    )
    first_rows = late_full[:, 4096:5120].reshape(16, 64, 1024)
    second_rows = late_full[:, 5120:6144].reshape(16, 64, 1024)
    out_full = first_rows[:, :32].reshape(512, 1024)
    mixer_out_full = jnp.concatenate([first_rows[:, 32:], second_rows], axis=1).reshape(1536, 1024)
    count_of_rows = tokens.shape[0]
    tap_count = conv_weight.shape[0]
    inner_width = MH * MP
    width_of_keys = KEY_VALUE_HEADS * HEAD_WIDTH
    query_places = block_index * count_of_rows + jnp.arange(count_of_rows, dtype=jnp.int32)
    place_float = query_places.astype(jnp.float32)
    seg_float = segments.astype(jnp.float32)
    seg_low = segments.astype(jnp.bfloat16)
    seg_all = jnp.concatenate(from_everyone(seg_low))
    owners = jnp.concatenate(
        [(chip - jnp.arange(4)) % 4 * 2 + core, (chip - jnp.arange(4)) % 4 * 2 + 1 - core]
    )
    key_places = (
        owners[:, None] * count_of_rows + jnp.arange(count_of_rows, dtype=jnp.int32)[None, :]
    ).reshape(-1)
    attention_bias = jnp.where(
        (key_places[:, None] <= query_places[None, :]) & (seg_all[:, None] == seg_low[None, :]),
        0.0,
        masked_fill,
    ).astype(jnp.bfloat16)
    halo = 8
    tokens_before, seg_rows_before = from_behind(
        (tokens[count_of_rows - halo :], seg_float[count_of_rows - halo :]), "context", 1
    )
    prev_segs = seg_rows_before[halo - tap_count + 1 :]
    normed_before = rms_norm(tokens_before.astype(jnp.float32), attention_gain)
    hidden_in = tokens.astype(jnp.float32)
    normed, norm_one_back = jax.vjp(rms_norm, hidden_in, attention_gain)
    normed_low = normed.astype(jnp.bfloat16)
    every_lin = project(normed_low, in_full)
    query_lin = every_lin[:, :512]
    key_lin = every_lin[:, 512:640]
    value_lin = every_lin[:, 640:768]
    gate_lin = every_lin[:, 768:2304]
    mixer_lin = every_lin[:, 2304:4096]
    step_lin = every_lin[:, 4096:IN_USED]
    rotated_queries = rotary(query_lin, place_float, 1.0).astype(jnp.bfloat16)
    rotated_keys = rotary(key_lin, place_float, 1.0).astype(jnp.bfloat16)
    value_reduced = value_lin.astype(jnp.bfloat16)
    sent, mixer_lin, gate_lin, step_lin = lax.optimization_barrier(
        (
            jnp.concatenate([rotated_keys, value_reduced], axis=1),
            mixer_lin,
            gate_lin,
            step_lin,
        )
    )
    slots = from_everyone(sent)
    scale_factor = 1.0 / math.sqrt(HEAD_WIDTH)
    query_scaled = rotated_queries * jnp.asarray(scale_factor, jnp.bfloat16)
    query_t = query_scaled.T
    attended_t, totals, kv_heads, kv_t = attend(query_t, slots, attention_bias)
    attended_low = attended_t.T
    attention_branch = project(attended_low, out_full)
    prev_rows = project(normed_before.astype(jnp.bfloat16), in_full[:, 2304:4096])
    prev_rows = prev_rows[halo - tap_count + 1 :]
    extended = jnp.concatenate([prev_rows, mixer_lin], axis=0)
    seg_extended = jnp.concatenate([prev_segs, seg_float])
    seg_before = prev_segs[-1]

    def mixer_piece(ext_rows, conv_taps, conv_shift, step_raw, step_shift, decay_logs):
        return mixer_inputs(
            ext_rows,
            seg_extended,
            seg_float,
            conv_taps,
            conv_shift,
            step_raw,
            step_shift,
            decay_logs,
        )

    (activated, step_size, log_rate), mixer_back = jax.vjp(
        mixer_piece, extended, conv_weight, conv_bias, step_lin, step_bias, decay_log
    )
    mixer_x = activated[:, :inner_width]
    bees = activated[:, inner_width : inner_width + NS].astype(jnp.bfloat16)
    seas = activated[:, inner_width + NS :].astype(jnp.bfloat16)

    def decay_piece(rates):
        return decay_terms(rates, seg_float, seg_before)

    (running, entry, leaving, carried), decay_back = jax.vjp(decay_piece, log_rate)
    spread = heads_to_columns(jnp.concatenate([step_size, leaving, entry], axis=0))
    step_wide = spread[:count_of_rows]
    leaving_wide = spread[count_of_rows : 2 * count_of_rows]
    entry_wide = spread[2 * count_of_rows :]
    inputs_low = (mixer_x * step_wide).astype(jnp.bfloat16)
    weighted_low = (inputs_low.astype(jnp.float32) * leaving_wide).astype(jnp.bfloat16)
    local_state = input_grad(bees, weighted_low)
    decays = chip_decays(jnp.repeat(carried, MP))
    skip_wide = jnp.repeat(skip_gain, MP)[None, :]
    incoming_low = carried_in(decays, local_state, False)
    index_rows = jnp.arange(count_of_rows)
    block_allowed = (index_rows[:, None] >= index_rows[None, :]) & (
        seg_float[:, None] == seg_float[None, :]
    )
    block_bias = jnp.where(block_allowed, 0.0, masked_fill)
    running_rows = running.T.reshape(MH // 2, 2, count_of_rows)
    running_columns = running_rows.transpose(0, 2, 1)
    intersection = matmul(seas, bees, ((1,), (1,)))
    inner = within_block(inputs_low, intersection, block_bias, running_columns, running_rows)
    from_state = project(seas, incoming_low)
    scanned = inner + from_state * entry_wide + skip_wide * mixer_x
    gated, gating_back = jax.vjp(gating, scanned, gate_lin)
    gated_low = gated.astype(jnp.bfloat16)
    mixer_branch = project(gated_low, mixer_out_full)
    residual = hidden_in + attention_multiplier * attention_branch + mixer_multiplier * mixer_branch
    normed_two, norm_two_back = jax.vjp(rms_norm, residual, feed_gain)
    normed_two_low = normed_two.astype(jnp.bfloat16)
    ffn_gate_lin, ffn_up_lin, hidden_low, feed_out = feed_forward(normed_two_low, late_full)
    output = (residual + feed_out).astype(jnp.bfloat16)
    upstream = cotangent.astype(jnp.float32)
    d_ffn_gate, d_ffn_up, d_normed_two = feed_backward(
        cotangent, ffn_gate_lin, ffn_up_lin, late_full
    )
    d_feed_low = jnp.stack([d_ffn_gate, d_ffn_up])
    d_resid_norm, grad_feed_gain = norm_two_back(d_normed_two)
    d_residual = upstream + d_resid_norm
    d_attn_low = (attention_multiplier * d_residual).astype(jnp.bfloat16)
    d_mixer_low = (mixer_multiplier * d_residual).astype(jnp.bfloat16)

    feed_got = swap_cores(
        input_grad(normed_two_low, d_feed_low[1 - core]).astype(jnp.bfloat16)
    )
    feed_own = (
        input_grad(normed_two_low, d_feed_low[core]) + feed_got.astype(jnp.float32)
    ).astype(jnp.bfloat16)
    attended_gradient = back_through(d_attn_low, out_full).astype(jnp.bfloat16)
    d_gated = back_through(d_mixer_low, mixer_out_full)
    d_scan_flat, d_gate_lin = gating_back(d_gated)
    d_gate_low = d_gate_lin.astype(jnp.bfloat16)

    def out_grads(which):
        attn = input_grad(attended_low, half(d_attn_low, which, 1)).astype(jnp.bfloat16)
        mix = input_grad(gated_low, half(d_mixer_low, which, 1)).astype(jnp.bfloat16)
        down = input_grad(hidden_low, half(cotangent, which, 1)).astype(jnp.bfloat16)
        gate = input_grad(normed_low, half(d_gate_low, which, 1)).astype(jnp.bfloat16)
        return (attn, mix, down, gate)

    out_got = jax.tree.map(swap_cores, out_grads(1 - core))
    early = jax.tree.map(lambda a, b: a + b, out_grads(core), out_got)
    mix_rows = early[1].reshape(16, 96, 512)
    early_rows = jnp.concatenate(
        [
            feed_own,
            early[3],
            jnp.concatenate([early[0].reshape(16, 32, 512), mix_rows[:, :32]], axis=1).reshape(
                1024, 512
            ),
            mix_rows[:, 32:].reshape(1024, 512),
            early[2][:1024],
            early[2][1024:],
        ],
        axis=1,
    )
    d_scan_low = d_scan_flat.astype(jnp.bfloat16)
    d_scan = d_scan_low.astype(jnp.float32)
    d_from_low = (d_scan * entry_wide).astype(jnp.bfloat16)
    d_incoming = input_grad(seas, d_from_low)
    attended_gradient, early_rows, d_incoming = lax.optimization_barrier(
        (attended_gradient, early_rows, d_incoming)
    )
    early_shard = lax.psum_scatter(early_rows, "dp", scatter_dimension=0, tiled=True)
    d_state_low = carried_in(decays, d_incoming, True)
    d_query_t, d_kv = attend_back(
        query_t,
        query_scaled.reshape(count_of_rows, QUERY_HEADS, HEAD_WIDTH).transpose(1, 0, 2),
        attended_gradient.T,
        attended_gradient.reshape(count_of_rows, QUERY_HEADS, HEAD_WIDTH).transpose(1, 0, 2),
        kv_heads,
        kv_t,
        attention_bias,
        totals,
    )
    d_scan_low, d_kv = lax.optimization_barrier((d_scan_low, d_kv))
    d_query_rot = d_query_t.T * scale_factor
    slot_grads = d_kv.astype(jnp.bfloat16).reshape(KEY_VALUE_HEADS, 2, 4, count_of_rows, -1)
    chip_grads = slot_grads[:, 0].astype(jnp.float32) + swap_cores(slot_grads[:, 1]).astype(
        jnp.float32
    )
    chip_low = chip_grads.astype(jnp.bfloat16)
    own_grads = chip_grads[:, 0]
    for k in range(1, 4):
        own_grads = own_grads + shift_chips(chip_low[:, k], -k).astype(jnp.float32)
    key_grads = jnp.concatenate(
        [
            own_grads[0, :, :HEAD_WIDTH],
            own_grads[1, :, :HEAD_WIDTH],
            own_grads[0, :, HEAD_WIDTH:],
            own_grads[1, :, HEAD_WIDTH:],
        ],
        axis=1,
    )
    d_query_low = rotary(d_query_rot, place_float, -1.0).astype(jnp.bfloat16)
    d_key_low = rotary(key_grads[:, :width_of_keys], place_float, -1.0).astype(jnp.bfloat16)
    d_value_low = key_grads[:, width_of_keys:].astype(jnp.bfloat16)
    d_inputs, d_inter_t, d_columns, d_rows = within_block_back(
        inputs_low, d_scan_low, intersection.T, block_bias.T, running_columns, running_rows
    )
    d_running = (d_rows - d_columns.transpose(0, 2, 1)).reshape(MH, count_of_rows).T
    d_inter_low = d_inter_t.astype(jnp.bfloat16)
    d_seas = back_through(d_from_low, incoming_low) + input_grad(d_inter_low, bees)
    d_bees = project(d_inter_low, seas) + back_through(weighted_low, d_state_low)
    d_weighted = project(bees, d_state_low)
    d_inputs = d_inputs + d_weighted * leaving_wide
    d_mixer_x = skip_wide * d_scan + d_inputs * step_wide
    d_entry = columns_to_heads(d_scan * from_state)
    d_leaving = columns_to_heads(d_weighted * inputs_low.astype(jnp.float32))
    d_step = columns_to_heads(d_inputs * mixer_x)
    sums = columns_to_heads(
        jnp.concatenate(
            [
                jnp.sum(d_scan * mixer_x, axis=0, keepdims=True),
                jnp.sum(
                    d_state_low.astype(jnp.float32) * incoming_low.astype(jnp.float32),
                    axis=0,
                    keepdims=True,
                ),
            ],
            axis=0,
        )
    )
    grad_skip_gain, d_carried = sums[0], sums[1]
    (d_rate,) = decay_back((d_running, d_entry, d_leaving, d_carried))
    d_activated = jnp.concatenate([d_mixer_x, d_bees, d_seas], axis=1)
    d_activated, early_shard = lax.optimization_barrier((d_activated, early_shard))
    one, two, three = (shift_chips(early_shard, k).astype(jnp.float32) for k in range(1, 4))
    early_mine = ((early_shard.astype(jnp.float32) + two) + (one + three)).astype(jnp.bfloat16)
    early_other = swap_cores(early_mine)
    d_extended, grad_conv_weight, grad_conv_bias, d_step_lin, grad_step_bias, grad_decay_log = (
        mixer_back((d_activated, d_step, d_rate))
    )
    rim_back = from_behind(d_extended[: tap_count - 1], "context", -1)
    d_mixer_lin = d_extended[tap_count - 1 :] + jnp.pad(
        rim_back, ((count_of_rows - tap_count + 1, 0), (0, 0))
    )
    d_late_low = jnp.concatenate(
        [
            d_query_low,
            d_key_low,
            d_value_low,
            d_mixer_lin.astype(jnp.bfloat16),
            jnp.pad(d_step_lin, ((0, 0), (0, IN_WIDTH - IN_USED))).astype(jnp.bfloat16),
        ],
        axis=1,
    )

    def summed_over_all(grad_low):
        width = grad_low.shape[1] // 2
        got = swap_cores(input_grad(normed_low, half(grad_low, 1 - core, 1)).astype(jnp.bfloat16))
        own = input_grad(normed_low, half(grad_low, core, 1)) + got.astype(jnp.float32)
        parts = lax.all_to_all(
            own.astype(jnp.bfloat16).reshape(64, 16, width),
            both,
            0,
            0,
            axis_index_groups=CORE_GROUPS,
        )
        total = jnp.sum(parts.astype(jnp.float32), axis=0).astype(jnp.bfloat16)
        spread_all = copies_of(total).reshape(4, 2, 16, width).astype(jnp.float32)
        return spread_all.transpose(0, 2, 1, 3).reshape(64, 2 * width)

    late_all = summed_over_all(d_late_low)
    d_every_low = jnp.concatenate([d_late_low[:, :768], d_gate_low, d_late_low[:, 768:]], axis=1)
    early_low = jnp.where(core == 0, early_mine, early_other).astype(jnp.float32)
    early_high = jnp.where(core == 0, early_other, early_mine).astype(jnp.float32)

    def joined(start, width):
        return jnp.concatenate(
            [early_low[:, start : start + width], early_high[:, start : start + width]], axis=1
        )

    def hidden_back(block):
        return block.reshape(64, 2, 16, 64).transpose(0, 2, 1, 3).reshape(64, 2048)

    first_out = joined(2816, 512)
    d_normed = back_through(d_every_low, in_full)
    d_tokens_norm, grad_attention_gain = norm_one_back(d_normed)
    grad_tokens = d_residual + d_tokens_norm

    def flat(part):
        part = part.reshape(-1)
        return jnp.pad(part, (0, -part.size % 128))

    pieces = (
        grad_attention_gain,
        grad_conv_weight,
        grad_conv_bias,
        grad_step_bias,
        grad_decay_log,
        grad_skip_gain,
        grad_feed_gain,
    )
    packed = jnp.concatenate([flat(part) for part in pieces])
    packed = sum_everywhere(jnp.pad(packed, (0, -packed.size % 1024)).reshape(-1, 128)).reshape(-1)
    small, start = [], 0
    for part in pieces:
        small.append(packed[start : start + part.size].reshape(part.shape))
        start += part.size + -part.size % 128
    summed = (
        late_all[:, :512],
        late_all[:, 512:640],
        late_all[:, 640:768],
        first_out[:32],
        joined(2048, 768),
        late_all[:, 768:2560],
        late_all[:, 2560 : 2560 + MH],
        jnp.concatenate([first_out[32:], joined(3328, 512)], axis=0),
        hidden_back(early_low[:, :2048]),
        hidden_back(early_high[:, :2048]),
        jnp.concatenate([joined(3840, 512), joined(4352, 512)], axis=0),
    )
    return (
        output,
        grad_tokens,
        small[0],
        summed[0],
        summed[1],
        summed[2],
        summed[3],
        summed[4],
        summed[5],
        summed[6],
        summed[7],
        small[1],
        small[2],
        small[3],
        small[4],
        small[5],
        small[6],
        summed[8],
        summed[9],
        summed[10],
    )


def solution(mesh):
    return jax.shard_map(
        on_device,
        mesh=mesh,
        in_specs=(
            P(("dp", "context"), None),
            P(("dp", "context")),
            P(("dp", "context"), None),
            P(),
            P("dp", None),
            P("dp", None),
            P("dp", None),
            P("dp", None),
            P("dp", None),
            P("dp", None),
            P("dp", None),
            P("dp", None),
            P(),
            P(),
            P(),
            P(),
            P(),
            P(),
            P("dp", None),
            P("dp", None),
            P("dp", None),
        ),
        out_specs=(
            P(("dp", "context"), None),
            P(("dp", "context"), None),
            P(),
            P("dp", None),
            P("dp", None),
            P("dp", None),
            P("dp", None),
            P("dp", None),
            P("dp", None),
            P("dp", None),
            P("dp", None),
            P(),
            P(),
            P(),
            P(),
            P(),
            P(),
            P("dp", None),
            P("dp", None),
            P("dp", None),
        ),
        check_vma=False,
    )
```

```python
import math

import jax
import jax.numpy as jnp
from jax import lax
from jax.experimental import pallas as pl
from jax.experimental.pallas import tpu as pltpu
from jax.sharding import PartitionSpec as P

QUERY_HEADS = 8
KEY_VALUE_HEADS = 2
HEAD_WIDTH = 64
MH = 24
MP = 64
NS = 128


EPSILON = 1e-05
masked_fill = -1e30
attention_multiplier = 0.9375
mixer_multiplier = 0.2357
rotary_base = 100000000000.0
IN_USED = 4120
IN_WIDTH = 4352
CHIP_GROUPS = [[2 * z + c for z in range(4)] for c in range(2)]
CORE_GROUPS = [[8 * d + 2 * z + c for d in range(16) for z in range(4)] for c in range(2)]


def from_behind(block, axis, distance):
    devices = range(lax.axis_size(axis))
    route = [(i - distance, i) for i in devices if i - distance in devices]
    return lax.ppermute(block, axis, route)


def swap_cores(block):
    devices = range(lax.axis_size("context"))
    return lax.ppermute(block, "context", [(i, i ^ 1) for i in devices])


def shift_chips(block, distance):
    devices = lax.axis_size("context")
    return lax.ppermute(
        block, "context", [(i, (i + 2 * distance) % devices) for i in range(devices)]
    )


def shift_other(block, distance):
    devices = lax.axis_size("context")
    route = [(i, (i + 2 * distance) % devices ^ 1) for i in range(devices)]
    return lax.ppermute(block, "context", route)


def from_everyone(block):
    near = [block] + [shift_chips(block, k) for k in range(1, 4)]
    return near + [shift_other(block, k) for k in range(4)]


def shift_rows(block, distance, stride):
    route = []
    for i in range(16):
        place = i // stride % 4
        route.append((i, i + ((place + distance) % 4 - place) * stride))
    return lax.ppermute(block, "dp", route)


def sum_of_four(block, shift):
    one, two, three = shift(block, 1), shift(block, 2), shift(block, 3)
    return (block + two) + (one + three)


def sum_everywhere(block):
    block = block + swap_cores(block)
    block = sum_of_four(block, shift_chips)
    block = sum_of_four(block, lambda part, k: shift_rows(part, k, 1))
    return sum_of_four(block, lambda part, k: shift_rows(part, k, 4))


def half(block, which, axis):
    size = block.shape[axis] // 2
    return lax.dynamic_slice_in_dim(block, which * size, size, axis)


def copies_of(block):
    devices = lax.axis_size("context")
    return lax.all_to_all(
        jnp.broadcast_to(block[None], (devices,) + block.shape), "context", 0, 0
    )


def chip_decays(carried):
    mine = lax.axis_index("context")
    core = mine % 2
    own = half(carried, core, 0)
    got = half(swap_cores(carried), core, 0)
    whole = own * got
    return own, got, [whole] + [shift_chips(whole, k) for k in range(1, 4)]


def carried_in(decays, local, reverse):
    mine = lax.axis_index("context")
    core, chip = mine % 2, mine // 2
    is_first = (core == 1) if reverse else (core == 0)
    order = 3 - chip if reverse else chip
    way = -1 if reverse else 1
    own_decay, got_decay, shifted = decays
    own_part = half(local, core, 1)
    got_part = swap_cores(half(local, 1 - core, 1).astype(jnp.bfloat16)).astype(jnp.float32)
    first = jnp.where(is_first, own_part, got_part)
    second = jnp.where(is_first, got_part, own_part)
    first_decay = jnp.where(is_first, own_decay, got_decay)
    second_decay = jnp.where(is_first, got_decay, own_decay)
    chip_low = (first * second_decay[None, :] + second).astype(jnp.bfloat16)
    total = jnp.zeros_like(first)
    factor = jnp.ones_like(own_decay)
    for k in range(1, 4):
        part = shift_chips(chip_low, way * k).astype(jnp.float32)
        reach = jnp.where(order >= k, factor, 0.0)
        total = total + reach[None, :] * part
        if k < 3:
            factor = factor * shifted[way * k % 4]
    for_first = total
    for_second = total * first_decay[None, :] + first
    keep = jnp.where(is_first, for_first, for_second)
    give = jnp.where(is_first, for_second, for_first)
    got = swap_cores(give.astype(jnp.bfloat16))
    keep = keep.astype(jnp.bfloat16)
    return jnp.where(
        core == 0, jnp.concatenate([keep, got], axis=1), jnp.concatenate([got, keep], axis=1)
    )


def rms_norm(values, gain_vector):
    return (
        values
        * lax.rsqrt(jnp.mean(values * values, axis=-1, keepdims=True) + EPSILON)
        * gain_vector
    )


def rotary(values, places, direction):
    count_of_rows = values.shape[0]
    head_count = values.shape[1] // HEAD_WIDTH
    half_size = HEAD_WIDTH // 2
    frequency = rotary_base ** (-2.0 * jnp.arange(half_size, dtype=jnp.float32) / HEAD_WIDTH)
    angles = places[:, None] * frequency[None, :]
    cosine = jnp.cos(angles)[:, None, :]
    sine_part = direction * jnp.sin(angles)[:, None, :]
    per_head = values.reshape(count_of_rows, head_count, HEAD_WIDTH)
    front_half = per_head[:, :, :half_size]
    back_half = per_head[:, :, half_size:]
    turned = jnp.concatenate(
        [front_half * cosine - back_half * sine_part, back_half * cosine + front_half * sine_part],
        axis=-1,
    )
    return turned.reshape(count_of_rows, head_count * HEAD_WIDTH)


def mixer_inputs(
    extended, seg_extended, seg_own, conv_taps, conv_shift, step_raw, step_shift, decay_logs
):
    count_of_rows = seg_own.shape[0]
    mixed = conv_shift[None, :]
    for tap_index in range(conv_taps.shape[0]):
        same_doc = (seg_extended[tap_index : tap_index + count_of_rows] == seg_own).astype(
            jnp.float32
        )
        mixed = (
            mixed
            + conv_taps[tap_index][None, :]
            * extended[tap_index : tap_index + count_of_rows]
            * same_doc[:, None]
        )
    activated = jax.nn.silu(mixed)
    step_size = jax.nn.softplus(step_raw + step_shift[None, :])
    log_rate = step_size * (-jnp.exp(decay_logs))[None, :]
    return (activated, step_size, log_rate)


def decay_terms(log_rate, seg_own, seg_before):
    count_of_rows = log_rate.shape[0]
    index_rows = jnp.arange(count_of_rows)
    lower = (index_rows[:, None] >= index_rows[None, :]).astype(jnp.float32)
    running = jnp.dot(lower, log_rate, precision=lax.Precision.HIGHEST)
    entry = jnp.exp(running) * (seg_own == seg_before).astype(jnp.float32)[:, None]
    leaving = (
        jnp.exp(running[-1][None, :] - running)
        * (seg_own == seg_own[-1]).astype(jnp.float32)[:, None]
    )
    carried = jnp.exp(running[-1]) * (seg_own[-1] == seg_before).astype(jnp.float32)
    return (running, entry, leaving, carried)


def heads_to_columns(values):
    spread = jnp.repeat(jnp.eye(MH, dtype=jnp.float32), MP, axis=1)
    return jnp.dot(values, spread, precision=lax.Precision.HIGH)


def columns_to_heads(values):
    spread = jnp.repeat(jnp.eye(MH, dtype=jnp.float32), MP, axis=1)
    return jnp.einsum("ic,hc->ih", values, spread, precision=lax.Precision.HIGH)


def matmul(left, right, sides=((1,), (0,))):
    return lax.dot_general(left, right, (sides, ((), ())), preferred_element_type=jnp.float32)


def attend_kernel(*refs):
    query_ref, slots, bias_ref = refs[0], refs[1:9], refs[9]
    out_ref, total_ref, heads_ref, turned_ref = refs[10:]
    head = pl.program_id(0)
    rows = slots[0].shape[0]

    @pl.when(head == 0)
    def _():
        for place, slot in enumerate(slots):
            block = slot[...]
            span = slice(place * rows, (place + 1) * rows)
            for part in range(4):
                heads_ref[part, span, :] = block[:, part * HEAD_WIDTH : (part + 1) * HEAD_WIDTH]
            turned_ref[:, span] = block.astype(jnp.float32).T.astype(jnp.bfloat16)

    group = head // 4
    value_rows = pl.ds(pl.multiple_of((2 + group) * HEAD_WIDTH, HEAD_WIDTH), HEAD_WIDTH)
    scores = matmul(heads_ref[group], query_ref[...]) + bias_ref[...].astype(jnp.float32)
    top = jnp.max(scores, axis=0, keepdims=True)
    exponent = jnp.exp(scores - top)
    total = jnp.sum(exponent, axis=0, keepdims=True)
    probs = (exponent * (1.0 / total)).astype(jnp.bfloat16)
    out_ref[...] = matmul(turned_ref[value_rows, :], probs).astype(jnp.bfloat16)
    total_ref[0] = top + jnp.log(total)


def attend_back_kernel(
    query_t_ref,
    query_ref,
    out_t_ref,
    out_ref,
    key_ref,
    value_ref,
    key_t_ref,
    bias_ref,
    total_ref,
    d_query_ref,
    d_key_ref,
):
    scores = matmul(key_ref[0], query_t_ref[...]) + bias_ref[...].astype(jnp.float32)
    probs = jnp.exp(scores - total_ref[0])
    d_probs = matmul(value_ref[0], out_t_ref[...])
    delta = jnp.sum(probs * d_probs, axis=0, keepdims=True)
    d_scores = (probs * (d_probs - delta)).astype(jnp.bfloat16)
    d_query_ref[...] = matmul(key_t_ref[...], d_scores)
    d_key = matmul(d_scores, query_ref[0])
    d_value = matmul(probs.astype(jnp.bfloat16), out_ref[0])
    both = jnp.concatenate([d_key, d_value], axis=1)
    first = pl.program_id(0) % 4 == 0

    @pl.when(first)
    def _():
        d_key_ref[0] = both

    @pl.when(jnp.logical_not(first))
    def _():
        d_key_ref[0] += both


def within_kernel(inputs_ref, inter_ref, bias_ref, column_ref, row_ref, out_ref):
    parts = []
    for p in range(2):
        within = jnp.exp(column_ref[0, :, p : p + 1] - row_ref[0, p : p + 1, :] + bias_ref[...])
        mixing = (inter_ref[...] * within).astype(jnp.bfloat16)
        parts.append(matmul(mixing, inputs_ref[...]))
    lane = lax.broadcasted_iota(jnp.int32, parts[0].shape, 1)
    out_ref[...] = jnp.where(lane < MP, parts[0], parts[1])


def within_back_kernel(
    inputs_ref,
    grad_ref,
    inter_ref,
    bias_ref,
    column_ref,
    row_ref,
    d_inputs_ref,
    d_inter_ref,
    d_column_ref,
    d_row_ref,
):
    lane = lax.broadcasted_iota(jnp.int32, inputs_ref.shape, 1)
    parts, columns, rows, d_inter = [], [], [], None
    for p in range(2):
        within = jnp.exp(row_ref[0, p : p + 1, :] - column_ref[0, :, p : p + 1] + bias_ref[...])
        mixing = inter_ref[...] * within
        parts.append(matmul(mixing.astype(jnp.bfloat16), grad_ref[...]))
        own = (lane < MP) if p == 0 else (lane >= MP)
        own_inputs = jnp.where(own, inputs_ref[...].astype(jnp.float32), 0.0)
        d_mixing = matmul(own_inputs.astype(jnp.bfloat16), grad_ref[...], ((1,), (1,)))
        product = d_mixing * mixing
        rows.append(jnp.sum(product, axis=0, keepdims=True))
        columns.append(jnp.sum(product, axis=1, keepdims=True))
        term = d_mixing * within
        d_inter = term if d_inter is None else d_inter + term
    d_inputs_ref[...] = jnp.where(lane < MP, parts[0], parts[1])
    d_row_ref[0] = jnp.concatenate(rows, axis=0)
    d_column_ref[0] = jnp.concatenate(columns, axis=1)
    first = pl.program_id(0) == 0

    @pl.when(first)
    def _():
        d_inter_ref[...] = d_inter

    @pl.when(jnp.logical_not(first))
    def _():
        d_inter_ref[...] += d_inter


def kernel_call(kernel, steps, ins, outs, flops, args):
    out_shape = [jax.ShapeDtypeStruct(shape, kind) for shape, kind, _, _ in outs]
    return pl.pallas_call(
        kernel,
        grid=(steps,),
        in_specs=[pl.BlockSpec(block, where) for block, where in ins],
        out_specs=[pl.BlockSpec(block, where) for _, _, block, where in outs],
        out_shape=out_shape,
        compiler_params=pltpu.CompilerParams(vmem_limit_bytes=48 * 1024 * 1024),
        cost_estimate=pl.CostEstimate(flops=flops, bytes_accessed=4 << 20, transcendentals=4 << 20),
    )(*args)


def feed_kernel(normed_ref, gate_ref, up_ref, down_ref, gate_lin_ref, up_lin_ref, hidden_ref, out_ref):
    gate = matmul(normed_ref[...], gate_ref[...])
    up = matmul(normed_ref[...], up_ref[...])
    gate_lin_ref[...] = gate
    up_lin_ref[...] = up
    hidden = (jax.nn.silu(gate) * up).astype(jnp.bfloat16)
    hidden_ref[...] = hidden
    out = matmul(hidden, down_ref[...])
    first = pl.program_id(0) == 0

    @pl.when(first)
    def _():
        out_ref[...] = out

    @pl.when(jnp.logical_not(first))
    def _():
        out_ref[...] += out


def feed_back_kernel(
    cotangent_ref,
    gate_lin_ref,
    up_lin_ref,
    gate_ref,
    up_ref,
    down_ref,
    d_gate_ref,
    d_up_ref,
    d_normed_ref,
):
    d_hidden = matmul(cotangent_ref[...], down_ref[...], ((1,), (1,)))
    gate, up = gate_lin_ref[...], up_lin_ref[...]
    sigmoid = jax.nn.sigmoid(gate)
    d_gate = (d_hidden * up * sigmoid * (1.0 + gate * (1.0 - sigmoid))).astype(jnp.bfloat16)
    d_up = (d_hidden * gate * sigmoid).astype(jnp.bfloat16)
    d_gate_ref[...] = d_gate
    d_up_ref[...] = d_up
    back = matmul(d_gate, gate_ref[...], ((1,), (1,))) + matmul(d_up, up_ref[...], ((1,), (1,)))
    first = pl.program_id(0) == 0

    @pl.when(first)
    def _():
        d_normed_ref[...] = back

    @pl.when(jnp.logical_not(first))
    def _():
        d_normed_ref[...] += back


FEED_WEIGHTS = [
    ((1024, 512), lambda j: (0, j)),
    ((1024, 512), lambda j: (0, 4 + j)),
    ((512, 1024), lambda j: (j % 2, 6 + j // 2)),
]


def feed_forward(normed_low, weights):
    rows = normed_low.shape[0]
    part = ((rows, 512), lambda j: (0, j))
    whole = ((rows, 1024), lambda j: (0, 0))
    return kernel_call(
        feed_kernel,
        4,
        [whole] + FEED_WEIGHTS,
        [
            ((rows, 2048), jnp.float32) + part,
            ((rows, 2048), jnp.float32) + part,
            ((rows, 2048), jnp.bfloat16) + part,
            ((rows, 1024), jnp.float32) + whole,
        ],
        6 * rows * 1024 * 2048,
        (normed_low, weights, weights, weights),
    )


def feed_backward(cotangent, gate_lin, up_lin, weights):
    rows = cotangent.shape[0]
    part = ((rows, 512), lambda j: (0, j))
    whole = ((rows, 1024), lambda j: (0, 0))
    return kernel_call(
        feed_back_kernel,
        4,
        [whole, part, part] + FEED_WEIGHTS,
        [
            ((rows, 2048), jnp.bfloat16) + part,
            ((rows, 2048), jnp.bfloat16) + part,
            ((rows, 1024), jnp.float32) + whole,
        ],
        6 * rows * 1024 * 2048,
        (cotangent, gate_lin, up_lin, weights, weights, weights),
    )


def layout_kernel(low_ref, high_ref, gate_ref, up_ref, mix_gate_ref, attn_ref, mix_ref, down_ref):
    for side, source in enumerate((low_ref, high_ref)):
        block = source[...].astype(jnp.float32)
        target = up_ref if side else gate_ref
        for d in range(16):
            target[:, 128 * d : 128 * d + 128] = jnp.concatenate(
                [block[:, 64 * d : 64 * d + 64], block[:, 1024 + 64 * d : 1088 + 64 * d]], axis=1
            )
        mix_gate_ref[:, 768 * side : 768 * side + 768] = block[:, 2048:2816]
        span = slice(512 * side, 512 * side + 512)
        attn_ref[:, span] = block[:32, 2816:3328]
        mix_ref[:32, span] = block[32:, 2816:3328]
        mix_ref[32:, span] = block[:, 3328:3840]
        down_ref[:64, span] = block[:, 3840:4352]
        down_ref[64:, span] = block[:, 4352:4864]


def laid_out(low, high):
    shapes = [(64, 2048), (64, 2048), (64, 1536), (32, 1024), (96, 1024), (128, 1024)]

    def origin(_):
        return (0, 0)

    return kernel_call(
        layout_kernel,
        1,
        [(low.shape, origin), (high.shape, origin)],
        [(shape, jnp.float32, shape, origin) for shape in shapes],
        1 << 20,
        (low, high),
    )


def attend(query_t, slots, bias):
    keys, rows = bias.shape
    size = HEAD_WIDTH
    return kernel_call(
        attend_kernel,
        QUERY_HEADS,
        [((size, rows), lambda h: (h, 0))]
        + [((rows, 4 * size), lambda h: (0, 0))] * 8
        + [((keys, rows), lambda h: (0, 0))],
        [
            ((QUERY_HEADS * size, rows), jnp.bfloat16, (size, rows), lambda h: (h, 0)),
            ((QUERY_HEADS, 1, rows), jnp.float32, (1, 1, rows), lambda h: (h, 0, 0)),
            ((4, keys, size), jnp.bfloat16, (4, keys, size), lambda h: (0, 0, 0)),
            ((4 * size, keys), jnp.bfloat16, (4 * size, keys), lambda h: (0, 0)),
        ],
        4 * QUERY_HEADS * size * rows * keys * 4,
        (query_t, *slots, bias),
    )


def attend_back(query_t, query_heads, out_t, out_heads, kv_heads, kv_t, bias, totals):
    keys, rows = bias.shape
    size = HEAD_WIDTH
    return kernel_call(
        attend_back_kernel,
        QUERY_HEADS,
        [
            ((size, rows), lambda h: (h, 0)),
            ((1, rows, size), lambda h: (h, 0, 0)),
            ((size, rows), lambda h: (h, 0)),
            ((1, rows, size), lambda h: (h, 0, 0)),
            ((1, keys, size), lambda h: (h // 4, 0, 0)),
            ((1, keys, size), lambda h: (2 + h // 4, 0, 0)),
            ((size, keys), lambda h: (h // 4, 0)),
            ((keys, rows), lambda h: (0, 0)),
            ((1, 1, rows), lambda h: (h, 0, 0)),
        ],
        [
            ((QUERY_HEADS * size, rows), jnp.float32, (size, rows), lambda h: (h, 0)),
            (
                (KEY_VALUE_HEADS, keys, 2 * size),
                jnp.float32,
                (1, keys, 2 * size),
                lambda h: (h // 4, 0, 0),
            ),
        ],
        10 * QUERY_HEADS * size * rows * keys * 4,
        (query_t, query_heads, out_t, out_heads, kv_heads, kv_heads, kv_t, bias, totals),
    )


def pair_blocks(rows):
    return (
        ((rows, 2 * MP), lambda i: (0, i)),
        ((rows, rows), lambda i: (0, 0)),
        ((1, rows, 2), lambda i: (i, 0, 0)),
        ((1, 2, rows), lambda i: (i, 0, 0)),
    )


def within_block(inputs_low, inter, bias, columns, rows_of):
    rows = inter.shape[0]
    wide, square, column, row = pair_blocks(rows)
    return kernel_call(
        within_kernel,
        MH // 2,
        [wide, square, square, column, row],
        [((rows, MH * MP), jnp.float32) + wide],
        16 * MH * MP * rows * rows,
        (inputs_low, inter, bias, columns, rows_of),
    )[0]


def within_block_back(inputs_low, grad_low, inter_t, bias_t, columns, rows_of):
    rows = inter_t.shape[0]
    wide, square, column, row = pair_blocks(rows)
    return kernel_call(
        within_back_kernel,
        MH // 2,
        [wide, wide, square, square, column, row],
        [
            ((rows, MH * MP), jnp.float32) + wide,
            ((rows, rows), jnp.float32) + square,
            ((MH // 2, rows, 2), jnp.float32) + column,
            ((MH // 2, 2, rows), jnp.float32) + row,
        ],
        32 * MH * MP * rows * rows,
        (inputs_low, grad_low, inter_t, bias_t, columns, rows_of),
    )


def project(left, right):
    return jnp.dot(left, right, preferred_element_type=jnp.float32)


def input_grad(left, right):
    return jnp.einsum("rk,rj->kj", left, right, preferred_element_type=jnp.float32)


def back_through(grad_low, weight_full):
    return jnp.einsum("rj,kj->rk", grad_low, weight_full, preferred_element_type=jnp.float32)


def swiglu(gate_values, up_values):
    return jax.nn.silu(gate_values) * up_values


def gating(scan_values, gate_values):
    return scan_values * jax.nn.silu(gate_values)


def on_device(
    tokens,
    segments,
    cotangent,
    attention_gain,
    query_weight,
    key_matrix,
    value_matrix,
    attention_out,
    gate_weight,
    mixer_weight,
    step_weight,
    mixer_out,
    conv_weight,
    conv_bias,
    step_bias,
    decay_log,
    skip_gain,
    feed_gain,
    feed_gate,
    feed_up,
    feed_down,
):
    block_index = lax.axis_index("context")
    core = block_index % 2
    chip = block_index // 2
    both = ("dp", "context")
    step_padded = jnp.pad(step_weight, ((0, 0), (0, IN_WIDTH - IN_USED)))
    in_shard = jnp.concatenate(
        [query_weight, key_matrix, value_matrix, gate_weight, mixer_weight, step_padded], axis=1
    )
    in_full = lax.all_gather(
        lax.dynamic_slice_in_dim(in_shard, block_index * 8, 8, 0), both, axis=0, tiled=True
    )
    def hidden_order(block):
        return block.reshape(8, 16, 2, 64).transpose(0, 2, 1, 3).reshape(8, 2048)

    feed_shard = jnp.concatenate(
        [
            hidden_order(lax.dynamic_slice_in_dim(feed_gate, block_index * 8, 8, 0)),
            hidden_order(lax.dynamic_slice_in_dim(feed_up, block_index * 8, 8, 0)),
        ],
        axis=1,
    )
    out_rows_own = jnp.concatenate([attention_out, mixer_out, feed_down], axis=0)
    out_shard = [
        lax.dynamic_slice_in_dim(out_rows_own, group * 64 + block_index * 8, 8, 0)
        for group in range(4)
    ]
    late_full = lax.all_gather(
        jnp.concatenate([feed_shard] + out_shard, axis=1), both, axis=0, tiled=True
    )
    first_rows = late_full[:, 4096:5120].reshape(16, 64, 1024)
    second_rows = late_full[:, 5120:6144].reshape(16, 64, 1024)
    out_full = first_rows[:, :32].reshape(512, 1024)
    mixer_out_full = jnp.concatenate([first_rows[:, 32:], second_rows], axis=1).reshape(1536, 1024)
    count_of_rows = tokens.shape[0]
    tap_count = conv_weight.shape[0]
    inner_width = MH * MP
    width_of_keys = KEY_VALUE_HEADS * HEAD_WIDTH
    query_places = block_index * count_of_rows + jnp.arange(count_of_rows, dtype=jnp.int32)
    place_float = query_places.astype(jnp.float32)
    seg_float = segments.astype(jnp.float32)
    seg_low = segments.astype(jnp.bfloat16)
    seg_all = jnp.concatenate(from_everyone(seg_low))
    owners = jnp.concatenate(
        [(chip - jnp.arange(4)) % 4 * 2 + core, (chip - jnp.arange(4)) % 4 * 2 + 1 - core]
    )
    key_places = (
        owners[:, None] * count_of_rows + jnp.arange(count_of_rows, dtype=jnp.int32)[None, :]
    ).reshape(-1)
    attention_bias = jnp.where(
        (key_places[:, None] <= query_places[None, :]) & (seg_all[:, None] == seg_low[None, :]),
        0.0,
        masked_fill,
    ).astype(jnp.bfloat16)
    halo = 8
    tokens_before, seg_rows_before = from_behind(
        (tokens[count_of_rows - halo :], seg_float[count_of_rows - halo :]), "context", 1
    )
    prev_segs = seg_rows_before[halo - tap_count + 1 :]
    normed_before = rms_norm(tokens_before.astype(jnp.float32), attention_gain)
    hidden_in = tokens.astype(jnp.float32)
    normed, norm_one_back = jax.vjp(rms_norm, hidden_in, attention_gain)
    normed_low = normed.astype(jnp.bfloat16)
    every_lin = project(normed_low, in_full)
    query_lin = every_lin[:, :512]
    key_lin = every_lin[:, 512:640]
    value_lin = every_lin[:, 640:768]
    gate_lin = every_lin[:, 768:2304]
    mixer_lin = every_lin[:, 2304:4096]
    step_lin = every_lin[:, 4096:IN_USED]
    rotated_queries = rotary(query_lin, place_float, 1.0).astype(jnp.bfloat16)
    rotated_keys = rotary(key_lin, place_float, 1.0).astype(jnp.bfloat16)
    value_reduced = value_lin.astype(jnp.bfloat16)
    sent, mixer_lin, gate_lin, step_lin = lax.optimization_barrier(
        (
            jnp.concatenate([rotated_keys, value_reduced], axis=1),
            mixer_lin,
            gate_lin,
            step_lin,
        )
    )
    slots = from_everyone(sent)
    scale_factor = 1.0 / math.sqrt(HEAD_WIDTH)
    query_scaled = rotated_queries * jnp.asarray(scale_factor, jnp.bfloat16)
    query_t = query_scaled.T
    attended_t, totals, kv_heads, kv_t = attend(query_t, slots, attention_bias)
    attended_low = attended_t.T
    attention_branch = project(attended_low, out_full)
    prev_rows = project(normed_before.astype(jnp.bfloat16), in_full[:, 2304:4096])
    prev_rows = prev_rows[halo - tap_count + 1 :]
    extended = jnp.concatenate([prev_rows, mixer_lin], axis=0)
    seg_extended = jnp.concatenate([prev_segs, seg_float])
    seg_before = prev_segs[-1]

    def mixer_piece(ext_rows, conv_taps, conv_shift, step_raw, step_shift, decay_logs):
        return mixer_inputs(
            ext_rows,
            seg_extended,
            seg_float,
            conv_taps,
            conv_shift,
            step_raw,
            step_shift,
            decay_logs,
        )

    (activated, step_size, log_rate), mixer_back = jax.vjp(
        mixer_piece, extended, conv_weight, conv_bias, step_lin, step_bias, decay_log
    )
    mixer_x = activated[:, :inner_width]
    bees = activated[:, inner_width : inner_width + NS].astype(jnp.bfloat16)
    seas = activated[:, inner_width + NS :].astype(jnp.bfloat16)

    def decay_piece(rates):
        return decay_terms(rates, seg_float, seg_before)

    (running, entry, leaving, carried), decay_back = jax.vjp(decay_piece, log_rate)
    spread = heads_to_columns(jnp.concatenate([step_size, leaving, entry], axis=0))
    step_wide = spread[:count_of_rows]
    leaving_wide = spread[count_of_rows : 2 * count_of_rows]
    entry_wide = spread[2 * count_of_rows :]
    inputs_low = (mixer_x * step_wide).astype(jnp.bfloat16)
    inputs_low, slots = lax.optimization_barrier((inputs_low, slots))
    weighted_low = (inputs_low.astype(jnp.float32) * leaving_wide).astype(jnp.bfloat16)
    local_state = input_grad(bees, weighted_low)
    decays = chip_decays(jnp.repeat(carried, MP))
    skip_wide = jnp.repeat(skip_gain, MP)[None, :]
    incoming_low = carried_in(decays, local_state, False)
    index_rows = jnp.arange(count_of_rows)
    block_allowed = (index_rows[:, None] >= index_rows[None, :]) & (
        seg_float[:, None] == seg_float[None, :]
    )
    block_bias = jnp.where(block_allowed, 0.0, masked_fill)
    running_rows = running.T.reshape(MH // 2, 2, count_of_rows)
    running_columns = running_rows.transpose(0, 2, 1)
    intersection = matmul(seas, bees, ((1,), (1,)))
    inner = within_block(inputs_low, intersection, block_bias, running_columns, running_rows)
    from_state = project(seas, incoming_low)
    scanned = inner + from_state * entry_wide + skip_wide * mixer_x
    gated, gating_back = jax.vjp(gating, scanned, gate_lin)
    gated_low = gated.astype(jnp.bfloat16)
    mixer_branch = project(gated_low, mixer_out_full)
    residual = hidden_in + attention_multiplier * attention_branch + mixer_multiplier * mixer_branch
    normed_two, norm_two_back = jax.vjp(rms_norm, residual, feed_gain)
    normed_two_low = normed_two.astype(jnp.bfloat16)
    ffn_gate_lin, ffn_up_lin, hidden_low, feed_out = feed_forward(normed_two_low, late_full)
    output = (residual + feed_out).astype(jnp.bfloat16)
    upstream = cotangent.astype(jnp.float32)
    d_ffn_gate, d_ffn_up, d_normed_two = feed_backward(
        cotangent, ffn_gate_lin, ffn_up_lin, late_full
    )
    d_feed_low = jnp.stack([d_ffn_gate, d_ffn_up])
    d_resid_norm, grad_feed_gain = norm_two_back(d_normed_two)
    d_residual = upstream + d_resid_norm
    d_attn_low = (attention_multiplier * d_residual).astype(jnp.bfloat16)
    d_mixer_low = (mixer_multiplier * d_residual).astype(jnp.bfloat16)

    feed_got = swap_cores(
        input_grad(normed_two_low, d_feed_low[1 - core]).astype(jnp.bfloat16)
    )
    feed_own = (
        input_grad(normed_two_low, d_feed_low[core]) + feed_got.astype(jnp.float32)
    ).astype(jnp.bfloat16)
    attended_gradient = back_through(d_attn_low, out_full).astype(jnp.bfloat16)
    d_gated = back_through(d_mixer_low, mixer_out_full)
    d_scan_flat, d_gate_lin = gating_back(d_gated)
    d_gate_low = d_gate_lin.astype(jnp.bfloat16)

    def out_grads(which):
        attn = input_grad(attended_low, half(d_attn_low, which, 1)).astype(jnp.bfloat16)
        mix = input_grad(gated_low, half(d_mixer_low, which, 1)).astype(jnp.bfloat16)
        down = input_grad(hidden_low, half(cotangent, which, 1)).astype(jnp.bfloat16)
        gate = input_grad(normed_low, half(d_gate_low, which, 1)).astype(jnp.bfloat16)
        return (attn, mix, down, gate)

    out_got = jax.tree.map(swap_cores, out_grads(1 - core))
    early = jax.tree.map(lambda a, b: a + b, out_grads(core), out_got)
    mix_rows = early[1].reshape(16, 96, 512)
    early_rows = jnp.concatenate(
        [
            feed_own,
            early[3],
            jnp.concatenate([early[0].reshape(16, 32, 512), mix_rows[:, :32]], axis=1).reshape(
                1024, 512
            ),
            mix_rows[:, 32:].reshape(1024, 512),
            early[2][:1024],
            early[2][1024:],
        ],
        axis=1,
    )
    d_scan_low = d_scan_flat.astype(jnp.bfloat16)
    d_scan = d_scan_low.astype(jnp.float32)
    d_from_low = (d_scan * entry_wide).astype(jnp.bfloat16)
    d_incoming = input_grad(seas, d_from_low)
    attended_gradient, early_rows, d_incoming = lax.optimization_barrier(
        (attended_gradient, early_rows, d_incoming)
    )
    early_shard = lax.psum_scatter(early_rows, "dp", scatter_dimension=0, tiled=True)
    d_state_low = carried_in(decays, d_incoming, True)
    d_query_t, d_kv = attend_back(
        query_t,
        query_scaled.reshape(count_of_rows, QUERY_HEADS, HEAD_WIDTH).transpose(1, 0, 2),
        attended_gradient.T,
        attended_gradient.reshape(count_of_rows, QUERY_HEADS, HEAD_WIDTH).transpose(1, 0, 2),
        kv_heads,
        kv_t,
        attention_bias,
        totals,
    )
    d_scan_low, d_kv, d_state_low = lax.optimization_barrier((d_scan_low, d_kv, d_state_low))
    d_query_rot = d_query_t.T * scale_factor
    slot_grads = d_kv.astype(jnp.bfloat16).reshape(KEY_VALUE_HEADS, 2, 4, count_of_rows, -1)
    chip_grads = slot_grads[:, 0].astype(jnp.float32) + swap_cores(slot_grads[:, 1]).astype(
        jnp.float32
    )
    chip_low = chip_grads.astype(jnp.bfloat16)
    own_grads = chip_grads[:, 0]
    for k in range(1, 4):
        own_grads = own_grads + shift_chips(chip_low[:, k], -k).astype(jnp.float32)
    key_grads = jnp.concatenate(
        [
            own_grads[0, :, :HEAD_WIDTH],
            own_grads[1, :, :HEAD_WIDTH],
            own_grads[0, :, HEAD_WIDTH:],
            own_grads[1, :, HEAD_WIDTH:],
        ],
        axis=1,
    )
    d_query_low = rotary(d_query_rot, place_float, -1.0).astype(jnp.bfloat16)
    d_key_low = rotary(key_grads[:, :width_of_keys], place_float, -1.0).astype(jnp.bfloat16)
    d_value_low = key_grads[:, width_of_keys:].astype(jnp.bfloat16)
    d_inputs, d_inter_t, d_columns, d_rows = within_block_back(
        inputs_low, d_scan_low, intersection.T, block_bias.T, running_columns, running_rows
    )
    d_running = (d_rows - d_columns.transpose(0, 2, 1)).reshape(MH, count_of_rows).T
    d_inter_low = d_inter_t.astype(jnp.bfloat16)
    d_seas = back_through(d_from_low, incoming_low) + input_grad(d_inter_low, bees)
    d_bees = project(d_inter_low, seas) + back_through(weighted_low, d_state_low)
    d_weighted = project(bees, d_state_low)
    d_inputs = d_inputs + d_weighted * leaving_wide
    d_mixer_x = skip_wide * d_scan + d_inputs * step_wide
    d_entry = columns_to_heads(d_scan * from_state)
    d_leaving = columns_to_heads(d_weighted * inputs_low.astype(jnp.float32))
    d_step = columns_to_heads(d_inputs * mixer_x)
    sums = columns_to_heads(
        jnp.concatenate(
            [
                jnp.sum(d_scan * mixer_x, axis=0, keepdims=True),
                jnp.sum(
                    d_state_low.astype(jnp.float32) * incoming_low.astype(jnp.float32),
                    axis=0,
                    keepdims=True,
                ),
            ],
            axis=0,
        )
    )
    grad_skip_gain, d_carried = sums[0], sums[1]
    (d_rate,) = decay_back((d_running, d_entry, d_leaving, d_carried))
    d_activated = jnp.concatenate([d_mixer_x, d_bees, d_seas], axis=1)
    d_activated, early_shard = lax.optimization_barrier((d_activated, early_shard))
    one, two, three = (shift_chips(early_shard, k).astype(jnp.float32) for k in range(1, 4))
    early_mine = ((early_shard.astype(jnp.float32) + two) + (one + three)).astype(jnp.bfloat16)
    early_other = swap_cores(early_mine)
    d_extended, grad_conv_weight, grad_conv_bias, d_step_lin, grad_step_bias, grad_decay_log = (
        mixer_back((d_activated, d_step, d_rate))
    )
    rim_back = from_behind(d_extended[: tap_count - 1], "context", -1)
    d_mixer_lin = d_extended[tap_count - 1 :] + jnp.pad(
        rim_back, ((count_of_rows - tap_count + 1, 0), (0, 0))
    )
    d_late_low = jnp.concatenate(
        [
            d_query_low,
            d_key_low,
            d_value_low,
            d_mixer_lin.astype(jnp.bfloat16),
            jnp.pad(d_step_lin, ((0, 0), (0, IN_WIDTH - IN_USED))).astype(jnp.bfloat16),
        ],
        axis=1,
    )

    width = IN_WIDTH // 2 - 768
    late_got = swap_cores(
        input_grad(normed_low, half(d_late_low, 1 - core, 1)).astype(jnp.bfloat16)
    )
    late_own = input_grad(normed_low, half(d_late_low, core, 1)) + late_got.astype(jnp.float32)
    late_own = late_own.astype(jnp.bfloat16)
    d_every_low = jnp.concatenate([d_late_low[:, :768], d_gate_low, d_late_low[:, 768:]], axis=1)
    d_normed = back_through(d_every_low, in_full)
    d_tokens_norm, grad_attention_gain = norm_one_back(d_normed)
    grad_tokens = d_residual + d_tokens_norm

    def flat(part):
        part = part.reshape(-1)
        return jnp.pad(part, (0, -part.size % 128))

    pieces = (
        grad_attention_gain,
        grad_conv_weight,
        grad_conv_bias,
        grad_step_bias,
        grad_decay_log,
        grad_skip_gain,
        grad_feed_gain,
    )
    packed = jnp.concatenate([flat(part) for part in pieces])
    packed = jnp.pad(packed, (0, -packed.size % 1024)).reshape(-1, 128)
    late_own, packed = lax.optimization_barrier((late_own, packed))
    late_parts = lax.all_to_all(
        late_own.reshape(64, 16, width), both, 0, 0, axis_index_groups=CORE_GROUPS
    )
    packed = sum_everywhere(packed).reshape(-1)
    late_total = jnp.sum(late_parts.astype(jnp.float32), axis=0).astype(jnp.bfloat16)
    early_low = jnp.where(core == 0, early_mine, early_other)
    early_high = jnp.where(core == 0, early_other, early_mine)
    late_total, early_low, early_high = lax.optimization_barrier(
        (late_total, early_low, early_high)
    )
    late_all = copies_of(late_total).reshape(4, 2, 16, width).astype(jnp.float32)
    late_all = late_all.transpose(0, 2, 1, 3).reshape(64, 2 * width)
    grad_feed_gate, grad_feed_up, grad_gate_weight, grad_attn, grad_mix, grad_down = laid_out(
        early_low, early_high
    )
    small, start = [], 0
    for part in pieces:
        small.append(packed[start : start + part.size].reshape(part.shape))
        start += part.size + -part.size % 128
    summed = (
        late_all[:, :512],
        late_all[:, 512:640],
        late_all[:, 640:768],
        grad_attn,
        grad_gate_weight,
        late_all[:, 768:2560],
        late_all[:, 2560 : 2560 + MH],
        grad_mix,
        grad_feed_gate,
        grad_feed_up,
        grad_down,
    )
    return (
        output,
        grad_tokens,
        small[0],
        summed[0],
        summed[1],
        summed[2],
        summed[3],
        summed[4],
        summed[5],
        summed[6],
        summed[7],
        small[1],
        small[2],
        small[3],
        small[4],
        small[5],
        small[6],
        summed[8],
        summed[9],
        summed[10],
    )


def solution(mesh):
    return jax.shard_map(
        on_device,
        mesh=mesh,
        in_specs=(
            P(("dp", "context"), None),
            P(("dp", "context")),
            P(("dp", "context"), None),
            P(),
            P("dp", None),
            P("dp", None),
            P("dp", None),
            P("dp", None),
            P("dp", None),
            P("dp", None),
            P("dp", None),
            P("dp", None),
            P(),
            P(),
            P(),
            P(),
            P(),
            P(),
            P("dp", None),
            P("dp", None),
            P("dp", None),
        ),
        out_specs=(
            P(("dp", "context"), None),
            P(("dp", "context"), None),
            P(),
            P("dp", None),
            P("dp", None),
            P("dp", None),
            P("dp", None),
            P("dp", None),
            P("dp", None),
            P("dp", None),
            P("dp", None),
            P(),
            P(),
            P(),
            P(),
            P(),
            P(),
            P("dp", None),
            P("dp", None),
            P("dp", None),
        ),
        check_vma=False,
    )
```

```python
import math

import jax
import jax.numpy as jnp
from jax import lax
from jax.experimental import pallas as pl
from jax.experimental.pallas import tpu as pltpu
from jax.sharding import PartitionSpec as P

QUERY_HEADS = 8
KEY_VALUE_HEADS = 2
HEAD_WIDTH = 64
MH = 24
MP = 64
NS = 128


EPSILON = 1e-05
masked_fill = -1e30
attention_multiplier = 0.9375
mixer_multiplier = 0.2357
rotary_base = 100000000000.0
IN_USED = 4120
IN_WIDTH = 4352
CHIP_GROUPS = [[2 * z + c for z in range(4)] for c in range(2)]
CORE_GROUPS = [[8 * d + 2 * z + c for d in range(16) for z in range(4)] for c in range(2)]


def from_behind(block, axis, distance):
    devices = range(lax.axis_size(axis))
    route = [(i - distance, i) for i in devices if i - distance in devices]
    return lax.ppermute(block, axis, route)


def swap_cores(block):
    devices = range(lax.axis_size("context"))
    return lax.ppermute(block, "context", [(i, i ^ 1) for i in devices])


def shift_chips(block, distance):
    devices = lax.axis_size("context")
    return lax.ppermute(
        block, "context", [(i, (i + 2 * distance) % devices) for i in range(devices)]
    )


def shift_other(block, distance):
    devices = lax.axis_size("context")
    route = [(i, (i + 2 * distance) % devices ^ 1) for i in range(devices)]
    return lax.ppermute(block, "context", route)


def from_everyone(block):
    near = [block] + [shift_chips(block, k) for k in range(1, 4)]
    return near + [shift_other(block, k) for k in range(4)]


def shift_rows(block, distance, stride):
    route = []
    for i in range(16):
        place = i // stride % 4
        route.append((i, i + ((place + distance) % 4 - place) * stride))
    return lax.ppermute(block, "dp", route)


def sum_of_four(block, shift):
    one, two, three = shift(block, 1), shift(block, 2), shift(block, 3)
    return (block + two) + (one + three)


def sum_near(block):
    block = block + swap_cores(block)
    block = sum_of_four(block, shift_chips)
    return sum_of_four(block, lambda part, k: shift_rows(part, k, 1))


def half(block, which, axis):
    size = block.shape[axis] // 2
    return lax.dynamic_slice_in_dim(block, which * size, size, axis)


def copies_of(block):
    devices = lax.axis_size("context")
    return lax.all_to_all(
        jnp.broadcast_to(block[None], (devices,) + block.shape), "context", 0, 0
    )


def chip_decays(carried):
    mine = lax.axis_index("context")
    core = mine % 2
    own = half(carried, core, 0)
    got = half(swap_cores(carried), core, 0)
    whole = own * got
    return own, got, [whole] + [shift_chips(whole, k) for k in range(1, 4)]


def chip_part(decays, local, reverse):
    core = lax.axis_index("context") % 2
    is_first = (core == 1) if reverse else (core == 0)
    own_decay, got_decay, _ = decays
    own_part = half(local, core, 1)
    got_part = swap_cores(half(local, 1 - core, 1).astype(jnp.bfloat16)).astype(jnp.float32)
    first = jnp.where(is_first, own_part, got_part)
    second = jnp.where(is_first, got_part, own_part)
    second_decay = jnp.where(is_first, got_decay, own_decay)
    return first, (first * second_decay[None, :] + second).astype(jnp.bfloat16)


def from_chips(chip_low, reverse, beside):
    way = -1 if reverse else 1
    parts = [shift_chips(chip_low, way * k) for k in range(1, 4)]
    return lax.optimization_barrier((parts, beside))


def carried_in(decays, first, parts, reverse):
    mine = lax.axis_index("context")
    core, chip = mine % 2, mine // 2
    is_first = (core == 1) if reverse else (core == 0)
    order = 3 - chip if reverse else chip
    way = -1 if reverse else 1
    own_decay, got_decay, shifted = decays
    first_decay = jnp.where(is_first, own_decay, got_decay)
    total = jnp.zeros_like(first)
    factor = jnp.ones_like(own_decay)
    for k in range(1, 4):
        reach = jnp.where(order >= k, factor, 0.0)
        total = total + reach[None, :] * parts[k - 1].astype(jnp.float32)
        if k < 3:
            factor = factor * shifted[way * k % 4]
    for_first = total
    for_second = total * first_decay[None, :] + first
    keep = jnp.where(is_first, for_first, for_second)
    give = jnp.where(is_first, for_second, for_first)
    got = swap_cores(give.astype(jnp.bfloat16))
    keep = keep.astype(jnp.bfloat16)
    return jnp.where(
        core == 0, jnp.concatenate([keep, got], axis=1), jnp.concatenate([got, keep], axis=1)
    )


def rms_norm(values, gain_vector):
    return (
        values
        * lax.rsqrt(jnp.mean(values * values, axis=-1, keepdims=True) + EPSILON)
        * gain_vector
    )


def rotary(values, places, direction):
    count_of_rows = values.shape[0]
    head_count = values.shape[1] // HEAD_WIDTH
    half_size = HEAD_WIDTH // 2
    frequency = rotary_base ** (-2.0 * jnp.arange(half_size, dtype=jnp.float32) / HEAD_WIDTH)
    angles = places[:, None] * frequency[None, :]
    cosine = jnp.cos(angles)[:, None, :]
    sine_part = direction * jnp.sin(angles)[:, None, :]
    per_head = values.reshape(count_of_rows, head_count, HEAD_WIDTH)
    front_half = per_head[:, :, :half_size]
    back_half = per_head[:, :, half_size:]
    turned = jnp.concatenate(
        [front_half * cosine - back_half * sine_part, back_half * cosine + front_half * sine_part],
        axis=-1,
    )
    return turned.reshape(count_of_rows, head_count * HEAD_WIDTH)


def mixer_inputs(
    extended, seg_extended, seg_own, conv_taps, conv_shift, step_raw, step_shift, decay_logs
):
    count_of_rows = seg_own.shape[0]
    mixed = conv_shift[None, :]
    for tap_index in range(conv_taps.shape[0]):
        same_doc = (seg_extended[tap_index : tap_index + count_of_rows] == seg_own).astype(
            jnp.float32
        )
        mixed = (
            mixed
            + conv_taps[tap_index][None, :]
            * extended[tap_index : tap_index + count_of_rows]
            * same_doc[:, None]
        )
    activated = jax.nn.silu(mixed)
    step_size = jax.nn.softplus(step_raw + step_shift[None, :])
    log_rate = step_size * (-jnp.exp(decay_logs))[None, :]
    return (activated, step_size, log_rate)


def decay_terms(log_rate, seg_own, seg_before):
    count_of_rows = log_rate.shape[0]
    index_rows = jnp.arange(count_of_rows)
    lower = (index_rows[:, None] >= index_rows[None, :]).astype(jnp.float32)
    running = jnp.dot(lower, log_rate, precision=lax.Precision.HIGHEST)
    entry = jnp.exp(running) * (seg_own == seg_before).astype(jnp.float32)[:, None]
    leaving = (
        jnp.exp(running[-1][None, :] - running)
        * (seg_own == seg_own[-1]).astype(jnp.float32)[:, None]
    )
    carried = jnp.exp(running[-1]) * (seg_own[-1] == seg_before).astype(jnp.float32)
    return (running, entry, leaving, carried)


def heads_to_columns(values):
    spread = jnp.repeat(jnp.eye(MH, dtype=jnp.float32), MP, axis=1)
    return jnp.dot(values, spread, precision=lax.Precision.HIGH)


def columns_to_heads(values):
    spread = jnp.repeat(jnp.eye(MH, dtype=jnp.float32), MP, axis=1)
    return jnp.einsum("ic,hc->ih", values, spread, precision=lax.Precision.HIGH)


def matmul(left, right, sides=((1,), (0,))):
    return lax.dot_general(left, right, (sides, ((), ())), preferred_element_type=jnp.float32)


def attend_kernel(*refs):
    query_ref, slots, bias_ref = refs[0], refs[1:9], refs[9]
    out_ref, total_ref, heads_ref, turned_ref = refs[10:]
    head = pl.program_id(0)
    rows = slots[0].shape[0]

    @pl.when(head == 0)
    def _():
        for place, slot in enumerate(slots):
            block = slot[...]
            span = slice(place * rows, (place + 1) * rows)
            for part in range(4):
                heads_ref[part, span, :] = block[:, part * HEAD_WIDTH : (part + 1) * HEAD_WIDTH]
            turned_ref[:, span] = block.astype(jnp.float32).T.astype(jnp.bfloat16)

    group = head // 4
    value_rows = pl.ds(pl.multiple_of((2 + group) * HEAD_WIDTH, HEAD_WIDTH), HEAD_WIDTH)
    scores = matmul(heads_ref[group], query_ref[...]) + bias_ref[...].astype(jnp.float32)
    top = jnp.max(scores, axis=0, keepdims=True)
    exponent = jnp.exp(scores - top)
    total = jnp.sum(exponent, axis=0, keepdims=True)
    probs = (exponent * (1.0 / total)).astype(jnp.bfloat16)
    out_ref[...] = matmul(turned_ref[value_rows, :], probs).astype(jnp.bfloat16)
    total_ref[0] = top + jnp.log(total)


def attend_back_kernel(
    query_t_ref,
    query_ref,
    out_t_ref,
    out_ref,
    key_ref,
    value_ref,
    key_t_ref,
    bias_ref,
    total_ref,
    d_query_ref,
    d_key_ref,
):
    scores = matmul(key_ref[0], query_t_ref[...]) + bias_ref[...].astype(jnp.float32)
    probs = jnp.exp(scores - total_ref[0])
    d_probs = matmul(value_ref[0], out_t_ref[...])
    delta = jnp.sum(probs * d_probs, axis=0, keepdims=True)
    d_scores = (probs * (d_probs - delta)).astype(jnp.bfloat16)
    d_query_ref[...] = matmul(key_t_ref[...], d_scores)
    d_key = matmul(d_scores, query_ref[0])
    d_value = matmul(probs.astype(jnp.bfloat16), out_ref[0])
    both = jnp.concatenate([d_key, d_value], axis=1)
    first = pl.program_id(0) % 4 == 0

    @pl.when(first)
    def _():
        d_key_ref[0] = both

    @pl.when(jnp.logical_not(first))
    def _():
        d_key_ref[0] += both


def within_kernel(inputs_ref, inter_ref, bias_ref, column_ref, row_ref, out_ref):
    parts = []
    for p in range(2):
        within = jnp.exp(column_ref[0, :, p : p + 1] - row_ref[0, p : p + 1, :] + bias_ref[...])
        mixing = (inter_ref[...] * within).astype(jnp.bfloat16)
        parts.append(matmul(mixing, inputs_ref[...]))
    lane = lax.broadcasted_iota(jnp.int32, parts[0].shape, 1)
    out_ref[...] = jnp.where(lane < MP, parts[0], parts[1])


def within_back_kernel(
    inputs_ref,
    grad_ref,
    inter_ref,
    bias_ref,
    column_ref,
    row_ref,
    d_inputs_ref,
    d_inter_ref,
    d_column_ref,
    d_row_ref,
):
    lane = lax.broadcasted_iota(jnp.int32, inputs_ref.shape, 1)
    parts, columns, rows, d_inter = [], [], [], None
    for p in range(2):
        within = jnp.exp(row_ref[0, p : p + 1, :] - column_ref[0, :, p : p + 1] + bias_ref[...])
        mixing = inter_ref[...] * within
        parts.append(matmul(mixing.astype(jnp.bfloat16), grad_ref[...]))
        own = (lane < MP) if p == 0 else (lane >= MP)
        own_inputs = jnp.where(own, inputs_ref[...].astype(jnp.float32), 0.0)
        d_mixing = matmul(own_inputs.astype(jnp.bfloat16), grad_ref[...], ((1,), (1,)))
        product = d_mixing * mixing
        rows.append(jnp.sum(product, axis=0, keepdims=True))
        columns.append(jnp.sum(product, axis=1, keepdims=True))
        term = d_mixing * within
        d_inter = term if d_inter is None else d_inter + term
    d_inputs_ref[...] = jnp.where(lane < MP, parts[0], parts[1])
    d_row_ref[0] = jnp.concatenate(rows, axis=0)
    d_column_ref[0] = jnp.concatenate(columns, axis=1)
    first = pl.program_id(0) == 0

    @pl.when(first)
    def _():
        d_inter_ref[...] = d_inter

    @pl.when(jnp.logical_not(first))
    def _():
        d_inter_ref[...] += d_inter


def kernel_call(kernel, steps, ins, outs, flops, args):
    out_shape = [jax.ShapeDtypeStruct(shape, kind) for shape, kind, _, _ in outs]
    return pl.pallas_call(
        kernel,
        grid=(steps,),
        in_specs=[pl.BlockSpec(block, where) for block, where in ins],
        out_specs=[pl.BlockSpec(block, where) for _, _, block, where in outs],
        out_shape=out_shape,
        compiler_params=pltpu.CompilerParams(vmem_limit_bytes=48 * 1024 * 1024),
        cost_estimate=pl.CostEstimate(flops=flops, bytes_accessed=4 << 20, transcendentals=4 << 20),
    )(*args)


def feed_kernel(normed_ref, gate_ref, up_ref, down_ref, gate_lin_ref, up_lin_ref, hidden_ref, out_ref):
    gate = matmul(normed_ref[...], gate_ref[...])
    up = matmul(normed_ref[...], up_ref[...])
    gate_lin_ref[...] = gate
    up_lin_ref[...] = up
    hidden = (jax.nn.silu(gate) * up).astype(jnp.bfloat16)
    hidden_ref[...] = hidden
    out = matmul(hidden, down_ref[...])
    first = pl.program_id(0) == 0

    @pl.when(first)
    def _():
        out_ref[...] = out

    @pl.when(jnp.logical_not(first))
    def _():
        out_ref[...] += out


def feed_back_kernel(
    cotangent_ref,
    gate_lin_ref,
    up_lin_ref,
    gate_ref,
    up_ref,
    down_ref,
    d_gate_ref,
    d_up_ref,
    d_normed_ref,
):
    d_hidden = matmul(cotangent_ref[...], down_ref[...], ((1,), (1,)))
    gate, up = gate_lin_ref[...], up_lin_ref[...]
    sigmoid = jax.nn.sigmoid(gate)
    d_gate = (d_hidden * up * sigmoid * (1.0 + gate * (1.0 - sigmoid))).astype(jnp.bfloat16)
    d_up = (d_hidden * gate * sigmoid).astype(jnp.bfloat16)
    d_gate_ref[...] = d_gate
    d_up_ref[...] = d_up
    back = matmul(d_gate, gate_ref[...], ((1,), (1,))) + matmul(d_up, up_ref[...], ((1,), (1,)))
    first = pl.program_id(0) == 0

    @pl.when(first)
    def _():
        d_normed_ref[...] = back

    @pl.when(jnp.logical_not(first))
    def _():
        d_normed_ref[...] += back


FEED_WEIGHTS = [
    ((1024, 512), lambda j: (0, j)),
    ((1024, 512), lambda j: (0, 4 + j)),
    ((512, 1024), lambda j: (j % 2, 6 + j // 2)),
]


def feed_forward(normed_low, weights):
    rows = normed_low.shape[0]
    part = ((rows, 512), lambda j: (0, j))
    whole = ((rows, 1024), lambda j: (0, 0))
    return kernel_call(
        feed_kernel,
        4,
        [whole] + FEED_WEIGHTS,
        [
            ((rows, 2048), jnp.float32) + part,
            ((rows, 2048), jnp.float32) + part,
            ((rows, 2048), jnp.bfloat16) + part,
            ((rows, 1024), jnp.float32) + whole,
        ],
        6 * rows * 1024 * 2048,
        (normed_low, weights, weights, weights),
    )


def feed_backward(cotangent, gate_lin, up_lin, weights):
    rows = cotangent.shape[0]
    part = ((rows, 512), lambda j: (0, j))
    whole = ((rows, 1024), lambda j: (0, 0))
    return kernel_call(
        feed_back_kernel,
        4,
        [whole, part, part] + FEED_WEIGHTS,
        [
            ((rows, 2048), jnp.bfloat16) + part,
            ((rows, 2048), jnp.bfloat16) + part,
            ((rows, 1024), jnp.float32) + whole,
        ],
        6 * rows * 1024 * 2048,
        (cotangent, gate_lin, up_lin, weights, weights, weights),
    )


def layout_kernel(low_ref, high_ref, gate_ref, up_ref, mix_gate_ref, attn_ref, mix_ref, down_ref):
    for side, source in enumerate((low_ref, high_ref)):
        block = source[...].astype(jnp.float32)
        target = up_ref if side else gate_ref
        for d in range(16):
            target[:, 128 * d : 128 * d + 128] = jnp.concatenate(
                [block[:, 64 * d : 64 * d + 64], block[:, 1024 + 64 * d : 1088 + 64 * d]], axis=1
            )
        mix_gate_ref[:, 768 * side : 768 * side + 768] = block[:, 2048:2816]
        span = slice(512 * side, 512 * side + 512)
        attn_ref[:, span] = block[:32, 2816:3328]
        mix_ref[:32, span] = block[32:, 2816:3328]
        mix_ref[32:, span] = block[:, 3328:3840]
        down_ref[:64, span] = block[:, 3840:4352]
        down_ref[64:, span] = block[:, 4352:4864]


def laid_out(low, high):
    shapes = [(64, 2048), (64, 2048), (64, 1536), (32, 1024), (96, 1024), (128, 1024)]

    def origin(_):
        return (0, 0)

    return kernel_call(
        layout_kernel,
        1,
        [(low.shape, origin), (high.shape, origin)],
        [(shape, jnp.float32, shape, origin) for shape in shapes],
        1 << 20,
        (low, high),
    )


def attend(query_t, slots, bias):
    keys, rows = bias.shape
    size = HEAD_WIDTH
    return kernel_call(
        attend_kernel,
        QUERY_HEADS,
        [((size, rows), lambda h: (h, 0))]
        + [((rows, 4 * size), lambda h: (0, 0))] * 8
        + [((keys, rows), lambda h: (0, 0))],
        [
            ((QUERY_HEADS * size, rows), jnp.bfloat16, (size, rows), lambda h: (h, 0)),
            ((QUERY_HEADS, 1, rows), jnp.float32, (1, 1, rows), lambda h: (h, 0, 0)),
            ((4, keys, size), jnp.bfloat16, (4, keys, size), lambda h: (0, 0, 0)),
            ((4 * size, keys), jnp.bfloat16, (4 * size, keys), lambda h: (0, 0)),
        ],
        4 * QUERY_HEADS * size * rows * keys * 4,
        (query_t, *slots, bias),
    )


def attend_back(query_t, query_heads, out_t, out_heads, kv_heads, kv_t, bias, totals):
    keys, rows = bias.shape
    size = HEAD_WIDTH
    return kernel_call(
        attend_back_kernel,
        QUERY_HEADS,
        [
            ((size, rows), lambda h: (h, 0)),
            ((1, rows, size), lambda h: (h, 0, 0)),
            ((size, rows), lambda h: (h, 0)),
            ((1, rows, size), lambda h: (h, 0, 0)),
            ((1, keys, size), lambda h: (h // 4, 0, 0)),
            ((1, keys, size), lambda h: (2 + h // 4, 0, 0)),
            ((size, keys), lambda h: (h // 4, 0)),
            ((keys, rows), lambda h: (0, 0)),
            ((1, 1, rows), lambda h: (h, 0, 0)),
        ],
        [
            ((QUERY_HEADS * size, rows), jnp.float32, (size, rows), lambda h: (h, 0)),
            (
                (KEY_VALUE_HEADS, keys, 2 * size),
                jnp.float32,
                (1, keys, 2 * size),
                lambda h: (h // 4, 0, 0),
            ),
        ],
        10 * QUERY_HEADS * size * rows * keys * 4,
        (query_t, query_heads, out_t, out_heads, kv_heads, kv_heads, kv_t, bias, totals),
    )


def pair_blocks(rows):
    return (
        ((rows, 2 * MP), lambda i: (0, i)),
        ((rows, rows), lambda i: (0, 0)),
        ((1, rows, 2), lambda i: (i, 0, 0)),
        ((1, 2, rows), lambda i: (i, 0, 0)),
    )


def within_block(inputs_low, inter, bias, columns, rows_of):
    rows = inter.shape[0]
    wide, square, column, row = pair_blocks(rows)
    return kernel_call(
        within_kernel,
        MH // 2,
        [wide, square, square, column, row],
        [((rows, MH * MP), jnp.float32) + wide],
        16 * MH * MP * rows * rows,
        (inputs_low, inter, bias, columns, rows_of),
    )[0]


def within_block_back(inputs_low, grad_low, inter_t, bias_t, columns, rows_of):
    rows = inter_t.shape[0]
    wide, square, column, row = pair_blocks(rows)
    return kernel_call(
        within_back_kernel,
        MH // 2,
        [wide, wide, square, square, column, row],
        [
            ((rows, MH * MP), jnp.float32) + wide,
            ((rows, rows), jnp.float32) + square,
            ((MH // 2, rows, 2), jnp.float32) + column,
            ((MH // 2, 2, rows), jnp.float32) + row,
        ],
        32 * MH * MP * rows * rows,
        (inputs_low, grad_low, inter_t, bias_t, columns, rows_of),
    )


def project(left, right):
    return jnp.dot(left, right, preferred_element_type=jnp.float32)


def input_grad(left, right):
    return jnp.einsum("rk,rj->kj", left, right, preferred_element_type=jnp.float32)


def back_through(grad_low, weight_full):
    return jnp.einsum("rj,kj->rk", grad_low, weight_full, preferred_element_type=jnp.float32)


def swiglu(gate_values, up_values):
    return jax.nn.silu(gate_values) * up_values


def gating(scan_values, gate_values):
    return scan_values * jax.nn.silu(gate_values)


def on_device(
    tokens,
    segments,
    cotangent,
    attention_gain,
    query_weight,
    key_matrix,
    value_matrix,
    attention_out,
    gate_weight,
    mixer_weight,
    step_weight,
    mixer_out,
    conv_weight,
    conv_bias,
    step_bias,
    decay_log,
    skip_gain,
    feed_gain,
    feed_gate,
    feed_up,
    feed_down,
):
    block_index = lax.axis_index("context")
    core = block_index % 2
    chip = block_index // 2
    both = ("dp", "context")
    step_padded = jnp.pad(step_weight, ((0, 0), (0, IN_WIDTH - IN_USED)))
    in_shard = jnp.concatenate(
        [query_weight, key_matrix, value_matrix, gate_weight, mixer_weight, step_padded], axis=1
    )
    in_full = lax.all_gather(
        lax.dynamic_slice_in_dim(in_shard, block_index * 8, 8, 0), both, axis=0, tiled=True
    )
    def hidden_order(block):
        return block.reshape(8, 16, 2, 64).transpose(0, 2, 1, 3).reshape(8, 2048)

    feed_shard = jnp.concatenate(
        [
            hidden_order(lax.dynamic_slice_in_dim(feed_gate, block_index * 8, 8, 0)),
            hidden_order(lax.dynamic_slice_in_dim(feed_up, block_index * 8, 8, 0)),
        ],
        axis=1,
    )
    out_rows_own = jnp.concatenate([attention_out, mixer_out, feed_down], axis=0)
    out_shard = [
        lax.dynamic_slice_in_dim(out_rows_own, group * 64 + block_index * 8, 8, 0)
        for group in range(4)
    ]
    late_full = lax.all_gather(
        jnp.concatenate([feed_shard] + out_shard, axis=1), both, axis=0, tiled=True
    )
    first_rows = late_full[:, 4096:5120].reshape(16, 64, 1024)
    second_rows = late_full[:, 5120:6144].reshape(16, 64, 1024)
    out_full = first_rows[:, :32].reshape(512, 1024)
    mixer_out_full = jnp.concatenate([first_rows[:, 32:], second_rows], axis=1).reshape(1536, 1024)
    count_of_rows = tokens.shape[0]
    tap_count = conv_weight.shape[0]
    inner_width = MH * MP
    width_of_keys = KEY_VALUE_HEADS * HEAD_WIDTH
    query_places = block_index * count_of_rows + jnp.arange(count_of_rows, dtype=jnp.int32)
    place_float = query_places.astype(jnp.float32)
    seg_float = segments.astype(jnp.float32)
    seg_low = segments.astype(jnp.bfloat16)
    seg_all = jnp.concatenate(from_everyone(seg_low))
    owners = jnp.concatenate(
        [(chip - jnp.arange(4)) % 4 * 2 + core, (chip - jnp.arange(4)) % 4 * 2 + 1 - core]
    )
    key_places = (
        owners[:, None] * count_of_rows + jnp.arange(count_of_rows, dtype=jnp.int32)[None, :]
    ).reshape(-1)
    attention_bias = jnp.where(
        (key_places[:, None] <= query_places[None, :]) & (seg_all[:, None] == seg_low[None, :]),
        0.0,
        masked_fill,
    ).astype(jnp.bfloat16)
    halo = 8
    tokens_before, seg_rows_before = from_behind(
        (tokens[count_of_rows - halo :], seg_float[count_of_rows - halo :]), "context", 1
    )
    prev_segs = seg_rows_before[halo - tap_count + 1 :]
    normed_before = rms_norm(tokens_before.astype(jnp.float32), attention_gain)
    hidden_in = tokens.astype(jnp.float32)
    normed, norm_one_back = jax.vjp(rms_norm, hidden_in, attention_gain)
    normed_low = normed.astype(jnp.bfloat16)
    every_lin = project(normed_low, in_full)
    query_lin = every_lin[:, :512]
    key_lin = every_lin[:, 512:640]
    value_lin = every_lin[:, 640:768]
    gate_lin = every_lin[:, 768:2304]
    mixer_lin = every_lin[:, 2304:4096]
    step_lin = every_lin[:, 4096:IN_USED]
    rotated_queries = rotary(query_lin, place_float, 1.0).astype(jnp.bfloat16)
    rotated_keys = rotary(key_lin, place_float, 1.0).astype(jnp.bfloat16)
    value_reduced = value_lin.astype(jnp.bfloat16)
    sent, mixer_lin, gate_lin, step_lin = lax.optimization_barrier(
        (
            jnp.concatenate([rotated_keys, value_reduced], axis=1),
            mixer_lin,
            gate_lin,
            step_lin,
        )
    )
    slots = from_everyone(sent)
    scale_factor = 1.0 / math.sqrt(HEAD_WIDTH)
    query_scaled = rotated_queries * jnp.asarray(scale_factor, jnp.bfloat16)
    prev_rows = project(normed_before.astype(jnp.bfloat16), in_full[:, 2304:4096])
    prev_rows = prev_rows[halo - tap_count + 1 :]
    extended = jnp.concatenate([prev_rows, mixer_lin], axis=0)
    seg_extended = jnp.concatenate([prev_segs, seg_float])
    seg_before = prev_segs[-1]

    def mixer_piece(ext_rows, conv_taps, conv_shift, step_raw, step_shift, decay_logs):
        return mixer_inputs(
            ext_rows,
            seg_extended,
            seg_float,
            conv_taps,
            conv_shift,
            step_raw,
            step_shift,
            decay_logs,
        )

    (activated, step_size, log_rate), mixer_back = jax.vjp(
        mixer_piece, extended, conv_weight, conv_bias, step_lin, step_bias, decay_log
    )
    mixer_x = activated[:, :inner_width]
    bees = activated[:, inner_width : inner_width + NS].astype(jnp.bfloat16)
    seas = activated[:, inner_width + NS :].astype(jnp.bfloat16)

    def decay_piece(rates):
        return decay_terms(rates, seg_float, seg_before)

    (running, entry, leaving, carried), decay_back = jax.vjp(decay_piece, log_rate)
    spread = heads_to_columns(jnp.concatenate([step_size, leaving, entry], axis=0))
    step_wide = spread[:count_of_rows]
    leaving_wide = spread[count_of_rows : 2 * count_of_rows]
    entry_wide = spread[2 * count_of_rows :]
    inputs_low = (mixer_x * step_wide).astype(jnp.bfloat16)
    inputs_low, slots = lax.optimization_barrier((inputs_low, slots))
    weighted_low = (inputs_low.astype(jnp.float32) * leaving_wide).astype(jnp.bfloat16)
    local_state = input_grad(bees, weighted_low)
    decays = chip_decays(jnp.repeat(carried, MP))
    skip_wide = jnp.repeat(skip_gain, MP)[None, :]
    chip_first, chip_low = chip_part(decays, local_state, False)
    query_t, chip_low = lax.optimization_barrier((query_scaled.T, chip_low))
    attended_t, totals, kv_heads, kv_t = attend(query_t, slots, attention_bias)
    parts, attended_t = from_chips(chip_low, False, attended_t)
    incoming_low = carried_in(decays, chip_first, parts, False)
    attended_low = attended_t.T
    attention_branch = project(attended_low, out_full)
    index_rows = jnp.arange(count_of_rows)
    block_allowed = (index_rows[:, None] >= index_rows[None, :]) & (
        seg_float[:, None] == seg_float[None, :]
    )
    block_bias = jnp.where(block_allowed, 0.0, masked_fill)
    running_rows = running.T.reshape(MH // 2, 2, count_of_rows)
    running_columns = running_rows.transpose(0, 2, 1)
    intersection = matmul(seas, bees, ((1,), (1,)))
    inner = within_block(inputs_low, intersection, block_bias, running_columns, running_rows)
    from_state = project(seas, incoming_low)
    scanned = inner + from_state * entry_wide + skip_wide * mixer_x
    gated, gating_back = jax.vjp(gating, scanned, gate_lin)
    gated_low = gated.astype(jnp.bfloat16)
    mixer_branch = project(gated_low, mixer_out_full)
    residual = hidden_in + attention_multiplier * attention_branch + mixer_multiplier * mixer_branch
    normed_two, norm_two_back = jax.vjp(rms_norm, residual, feed_gain)
    normed_two_low = normed_two.astype(jnp.bfloat16)
    ffn_gate_lin, ffn_up_lin, hidden_low, feed_out = feed_forward(normed_two_low, late_full)
    output = (residual + feed_out).astype(jnp.bfloat16)
    upstream = cotangent.astype(jnp.float32)
    d_ffn_gate, d_ffn_up, d_normed_two = feed_backward(
        cotangent, ffn_gate_lin, ffn_up_lin, late_full
    )
    d_feed_low = jnp.stack([d_ffn_gate, d_ffn_up])
    d_resid_norm, grad_feed_gain = norm_two_back(d_normed_two)
    d_residual = upstream + d_resid_norm
    d_attn_low = (attention_multiplier * d_residual).astype(jnp.bfloat16)
    d_mixer_low = (mixer_multiplier * d_residual).astype(jnp.bfloat16)

    feed_got = swap_cores(
        input_grad(normed_two_low, d_feed_low[1 - core]).astype(jnp.bfloat16)
    )
    feed_own = (
        input_grad(normed_two_low, d_feed_low[core]) + feed_got.astype(jnp.float32)
    ).astype(jnp.bfloat16)
    attended_gradient = back_through(d_attn_low, out_full).astype(jnp.bfloat16)
    d_gated = back_through(d_mixer_low, mixer_out_full)
    d_scan_flat, d_gate_lin = gating_back(d_gated)
    d_gate_low = d_gate_lin.astype(jnp.bfloat16)

    def out_grads(which):
        attn = input_grad(attended_low, half(d_attn_low, which, 1)).astype(jnp.bfloat16)
        mix = input_grad(gated_low, half(d_mixer_low, which, 1)).astype(jnp.bfloat16)
        down = input_grad(hidden_low, half(cotangent, which, 1)).astype(jnp.bfloat16)
        gate = input_grad(normed_low, half(d_gate_low, which, 1)).astype(jnp.bfloat16)
        return (attn, mix, down, gate)

    out_got = jax.tree.map(swap_cores, out_grads(1 - core))
    early = jax.tree.map(lambda a, b: a + b, out_grads(core), out_got)
    mix_rows = early[1].reshape(16, 96, 512)
    early_rows = jnp.concatenate(
        [
            feed_own,
            early[3],
            jnp.concatenate([early[0].reshape(16, 32, 512), mix_rows[:, :32]], axis=1).reshape(
                1024, 512
            ),
            mix_rows[:, 32:].reshape(1024, 512),
            early[2][:1024],
            early[2][1024:],
        ],
        axis=1,
    )
    d_scan_low = d_scan_flat.astype(jnp.bfloat16)
    d_scan = d_scan_low.astype(jnp.float32)
    d_from_low = (d_scan * entry_wide).astype(jnp.bfloat16)
    d_incoming = input_grad(seas, d_from_low)
    chip_last, chip_low_back = chip_part(decays, d_incoming, True)
    attended_gradient, early_rows, chip_low_back = lax.optimization_barrier(
        (attended_gradient, early_rows, chip_low_back)
    )
    early_shard = lax.psum_scatter(early_rows, "dp", scatter_dimension=0, tiled=True)
    d_query_t, d_kv = attend_back(
        query_t,
        query_scaled.reshape(count_of_rows, QUERY_HEADS, HEAD_WIDTH).transpose(1, 0, 2),
        attended_gradient.T,
        attended_gradient.reshape(count_of_rows, QUERY_HEADS, HEAD_WIDTH).transpose(1, 0, 2),
        kv_heads,
        kv_t,
        attention_bias,
        totals,
    )
    parts, d_kv = from_chips(chip_low_back, True, d_kv)
    d_state_low = carried_in(decays, chip_last, parts, True)
    d_scan_low, d_kv, d_state_low = lax.optimization_barrier((d_scan_low, d_kv, d_state_low))
    d_query_rot = d_query_t.T * scale_factor
    slot_grads = d_kv.astype(jnp.bfloat16).reshape(KEY_VALUE_HEADS, 2, 4, count_of_rows, -1)
    chip_grads = slot_grads[:, 0].astype(jnp.float32) + swap_cores(slot_grads[:, 1]).astype(
        jnp.float32
    )
    chip_low = chip_grads.astype(jnp.bfloat16)
    own_grads = chip_grads[:, 0]
    for k in range(1, 4):
        own_grads = own_grads + shift_chips(chip_low[:, k], -k).astype(jnp.float32)
    key_grads = jnp.concatenate(
        [
            own_grads[0, :, :HEAD_WIDTH],
            own_grads[1, :, :HEAD_WIDTH],
            own_grads[0, :, HEAD_WIDTH:],
            own_grads[1, :, HEAD_WIDTH:],
        ],
        axis=1,
    )
    d_query_low = rotary(d_query_rot, place_float, -1.0).astype(jnp.bfloat16)
    d_key_low = rotary(key_grads[:, :width_of_keys], place_float, -1.0).astype(jnp.bfloat16)
    d_value_low = key_grads[:, width_of_keys:].astype(jnp.bfloat16)
    d_inputs, d_inter_t, d_columns, d_rows = within_block_back(
        inputs_low, d_scan_low, intersection.T, block_bias.T, running_columns, running_rows
    )
    d_running = (d_rows - d_columns.transpose(0, 2, 1)).reshape(MH, count_of_rows).T
    d_inter_low = d_inter_t.astype(jnp.bfloat16)
    d_seas = back_through(d_from_low, incoming_low) + input_grad(d_inter_low, bees)
    d_bees = project(d_inter_low, seas) + back_through(weighted_low, d_state_low)
    d_weighted = project(bees, d_state_low)
    d_inputs = d_inputs + d_weighted * leaving_wide
    d_mixer_x = skip_wide * d_scan + d_inputs * step_wide
    d_entry = columns_to_heads(d_scan * from_state)
    d_leaving = columns_to_heads(d_weighted * inputs_low.astype(jnp.float32))
    d_step = columns_to_heads(d_inputs * mixer_x)
    sums = columns_to_heads(
        jnp.concatenate(
            [
                jnp.sum(d_scan * mixer_x, axis=0, keepdims=True),
                jnp.sum(
                    d_state_low.astype(jnp.float32) * incoming_low.astype(jnp.float32),
                    axis=0,
                    keepdims=True,
                ),
            ],
            axis=0,
        )
    )
    grad_skip_gain, d_carried = sums[0], sums[1]
    (d_rate,) = decay_back((d_running, d_entry, d_leaving, d_carried))
    d_activated = jnp.concatenate([d_mixer_x, d_bees, d_seas], axis=1)
    d_activated, early_shard = lax.optimization_barrier((d_activated, early_shard))
    one, two, three = (shift_chips(early_shard, k).astype(jnp.float32) for k in range(1, 4))
    early_mine = ((early_shard.astype(jnp.float32) + two) + (one + three)).astype(jnp.bfloat16)
    d_extended, grad_conv_weight, grad_conv_bias, d_step_lin, grad_step_bias, grad_decay_log = (
        mixer_back((d_activated, d_step, d_rate))
    )
    rim_back = from_behind(d_extended[: tap_count - 1], "context", -1)
    d_mixer_lin = d_extended[tap_count - 1 :] + jnp.pad(
        rim_back, ((count_of_rows - tap_count + 1, 0), (0, 0))
    )
    d_late_low = jnp.concatenate(
        [
            d_query_low,
            d_key_low,
            d_value_low,
            d_mixer_lin.astype(jnp.bfloat16),
            jnp.pad(d_step_lin, ((0, 0), (0, IN_WIDTH - IN_USED))).astype(jnp.bfloat16),
        ],
        axis=1,
    )

    d_late_low, early_mine = lax.optimization_barrier((d_late_low, early_mine))
    early_other = swap_cores(early_mine)
    width = IN_WIDTH // 2 - 768
    late_got = swap_cores(
        input_grad(normed_low, half(d_late_low, 1 - core, 1)).astype(jnp.bfloat16)
    )
    late_own = input_grad(normed_low, half(d_late_low, core, 1)) + late_got.astype(jnp.float32)
    late_own = late_own.astype(jnp.bfloat16)
    late_own, d_late_low = lax.optimization_barrier((late_own, d_late_low))
    d_every_low = jnp.concatenate([d_late_low[:, :768], d_gate_low, d_late_low[:, 768:]], axis=1)
    d_normed = back_through(d_every_low, in_full)
    d_tokens_norm, grad_attention_gain = norm_one_back(d_normed)
    grad_tokens = d_residual + d_tokens_norm

    def flat(part):
        part = part.reshape(-1)
        return jnp.pad(part, (0, -part.size % 128))

    pieces = (
        grad_attention_gain,
        grad_conv_weight,
        grad_conv_bias,
        grad_step_bias,
        grad_decay_log,
        grad_skip_gain,
        grad_feed_gain,
    )
    packed = jnp.concatenate([flat(part) for part in pieces])
    packed = jnp.pad(packed, (0, -packed.size % 1024)).reshape(-1, 128)
    late_parts = lax.all_to_all(
        late_own.reshape(64, 16, width), both, 0, 0, axis_index_groups=CORE_GROUPS
    )
    packed = sum_near(packed)
    late_total = jnp.sum(late_parts.astype(jnp.float32), axis=0).astype(jnp.bfloat16)
    early_low = jnp.where(core == 0, early_mine, early_other)
    early_high = jnp.where(core == 0, early_other, early_mine)
    late_total, early_low, early_high, packed = lax.optimization_barrier(
        (late_total, early_low, early_high, packed)
    )
    packed = sum_of_four(packed, lambda part, k: shift_rows(part, k, 4)).reshape(-1)
    late_all = copies_of(late_total).reshape(4, 2, 16, width).astype(jnp.float32)
    late_all = late_all.transpose(0, 2, 1, 3).reshape(64, 2 * width)
    grad_feed_gate, grad_feed_up, grad_gate_weight, grad_attn, grad_mix, grad_down = laid_out(
        early_low, early_high
    )
    small, start = [], 0
    for part in pieces:
        small.append(packed[start : start + part.size].reshape(part.shape))
        start += part.size + -part.size % 128
    summed = (
        late_all[:, :512],
        late_all[:, 512:640],
        late_all[:, 640:768],
        grad_attn,
        grad_gate_weight,
        late_all[:, 768:2560],
        late_all[:, 2560 : 2560 + MH],
        grad_mix,
        grad_feed_gate,
        grad_feed_up,
        grad_down,
    )
    return (
        output,
        grad_tokens,
        small[0],
        summed[0],
        summed[1],
        summed[2],
        summed[3],
        summed[4],
        summed[5],
        summed[6],
        summed[7],
        small[1],
        small[2],
        small[3],
        small[4],
        small[5],
        small[6],
        summed[8],
        summed[9],
        summed[10],
    )


def solution(mesh):
    return jax.shard_map(
        on_device,
        mesh=mesh,
        in_specs=(
            P(("dp", "context"), None),
            P(("dp", "context")),
            P(("dp", "context"), None),
            P(),
            P("dp", None),
            P("dp", None),
            P("dp", None),
            P("dp", None),
            P("dp", None),
            P("dp", None),
            P("dp", None),
            P("dp", None),
            P(),
            P(),
            P(),
            P(),
            P(),
            P(),
            P("dp", None),
            P("dp", None),
            P("dp", None),
        ),
        out_specs=(
            P(("dp", "context"), None),
            P(("dp", "context"), None),
            P(),
            P("dp", None),
            P("dp", None),
            P("dp", None),
            P("dp", None),
            P("dp", None),
            P("dp", None),
            P("dp", None),
            P("dp", None),
            P(),
            P(),
            P(),
            P(),
            P(),
            P(),
            P("dp", None),
            P("dp", None),
            P("dp", None),
        ),
        check_vma=False,
    )
```

```python
import math

import jax
import jax.numpy as jnp
from jax import lax
from jax.experimental import pallas as pl
from jax.experimental.pallas import tpu as pltpu
from jax.sharding import PartitionSpec as P

QUERY_HEADS = 8
KEY_VALUE_HEADS = 2
HEAD_WIDTH = 64
MH = 24
MP = 64
NS = 128


EPSILON = 1e-05
masked_fill = -1e30
attention_multiplier = 0.9375
mixer_multiplier = 0.2357
rotary_base = 100000000000.0
IN_USED = 4120
IN_WIDTH = 4352
CHIP_GROUPS = [[2 * z + c for z in range(4)] for c in range(2)]
CORE_GROUPS = [[8 * d + 2 * z + c for d in range(16) for z in range(4)] for c in range(2)]


def from_behind(block, axis, distance):
    devices = range(lax.axis_size(axis))
    route = [(i - distance, i) for i in devices if i - distance in devices]
    return lax.ppermute(block, axis, route)


def swap_cores(block):
    devices = range(lax.axis_size("context"))
    return lax.ppermute(block, "context", [(i, i ^ 1) for i in devices])


def shift_chips(block, distance):
    devices = lax.axis_size("context")
    return lax.ppermute(
        block, "context", [(i, (i + 2 * distance) % devices) for i in range(devices)]
    )


def shift_other(block, distance):
    devices = lax.axis_size("context")
    route = [(i, (i + 2 * distance) % devices ^ 1) for i in range(devices)]
    return lax.ppermute(block, "context", route)


def from_everyone(block):
    near = [block] + [shift_chips(block, k) for k in range(1, 4)]
    return near + [shift_other(block, k) for k in range(4)]


def shift_rows(block, distance, stride):
    route = []
    for i in range(16):
        place = i // stride % 4
        route.append((i, i + ((place + distance) % 4 - place) * stride))
    return lax.ppermute(block, "dp", route)


def sum_of_four(block, shift):
    one, two, three = shift(block, 1), shift(block, 2), shift(block, 3)
    return (block + two) + (one + three)


def sum_near(block):
    block = block + swap_cores(block)
    block = sum_of_four(block, shift_chips)
    return sum_of_four(block, lambda part, k: shift_rows(part, k, 1))


def half(block, which, axis):
    size = block.shape[axis] // 2
    return lax.dynamic_slice_in_dim(block, which * size, size, axis)


def copies_of(block):
    devices = lax.axis_size("context")
    return lax.all_to_all(
        jnp.broadcast_to(block[None], (devices,) + block.shape), "context", 0, 0
    )


def chip_decays(carried):
    mine = lax.axis_index("context")
    core = mine % 2
    own = half(carried, core, 0)
    got = half(swap_cores(carried), core, 0)
    whole = own * got
    return own, got, [whole] + [shift_chips(whole, k) for k in range(1, 4)]


def chip_part(decays, local, reverse):
    core = lax.axis_index("context") % 2
    is_first = (core == 1) if reverse else (core == 0)
    own_decay, got_decay, _ = decays
    own_part = half(local, core, 1)
    got_part = swap_cores(half(local, 1 - core, 1).astype(jnp.bfloat16)).astype(jnp.float32)
    first = jnp.where(is_first, own_part, got_part)
    second = jnp.where(is_first, got_part, own_part)
    second_decay = jnp.where(is_first, got_decay, own_decay)
    return first, (first * second_decay[None, :] + second).astype(jnp.bfloat16)


def from_chips(chip_low, reverse, beside):
    way = -1 if reverse else 1
    parts = [shift_chips(chip_low, way * k) for k in range(1, 4)]
    return lax.optimization_barrier((parts, beside))


def carried_in(decays, first, parts, reverse):
    mine = lax.axis_index("context")
    core, chip = mine % 2, mine // 2
    is_first = (core == 1) if reverse else (core == 0)
    order = 3 - chip if reverse else chip
    way = -1 if reverse else 1
    own_decay, got_decay, shifted = decays
    first_decay = jnp.where(is_first, own_decay, got_decay)
    total = jnp.zeros_like(first)
    factor = jnp.ones_like(own_decay)
    for k in range(1, 4):
        reach = jnp.where(order >= k, factor, 0.0)
        total = total + reach[None, :] * parts[k - 1].astype(jnp.float32)
        if k < 3:
            factor = factor * shifted[way * k % 4]
    for_first = total
    for_second = total * first_decay[None, :] + first
    keep = jnp.where(is_first, for_first, for_second)
    give = jnp.where(is_first, for_second, for_first)
    got = swap_cores(give.astype(jnp.bfloat16))
    keep = keep.astype(jnp.bfloat16)
    return jnp.where(
        core == 0, jnp.concatenate([keep, got], axis=1), jnp.concatenate([got, keep], axis=1)
    )


def rms_norm(values, gain_vector):
    return (
        values
        * lax.rsqrt(jnp.mean(values * values, axis=-1, keepdims=True) + EPSILON)
        * gain_vector
    )


def rotary(values, places, direction):
    count_of_rows = values.shape[0]
    head_count = values.shape[1] // HEAD_WIDTH
    half_size = HEAD_WIDTH // 2
    frequency = rotary_base ** (-2.0 * jnp.arange(half_size, dtype=jnp.float32) / HEAD_WIDTH)
    angles = places[:, None] * frequency[None, :]
    cosine = jnp.cos(angles)[:, None, :]
    sine_part = direction * jnp.sin(angles)[:, None, :]
    per_head = values.reshape(count_of_rows, head_count, HEAD_WIDTH)
    front_half = per_head[:, :, :half_size]
    back_half = per_head[:, :, half_size:]
    turned = jnp.concatenate(
        [front_half * cosine - back_half * sine_part, back_half * cosine + front_half * sine_part],
        axis=-1,
    )
    return turned.reshape(count_of_rows, head_count * HEAD_WIDTH)


def mixer_inputs(
    extended, seg_extended, seg_own, conv_taps, conv_shift, step_raw, step_shift, decay_logs
):
    count_of_rows = seg_own.shape[0]
    mixed = conv_shift[None, :]
    for tap_index in range(conv_taps.shape[0]):
        same_doc = (seg_extended[tap_index : tap_index + count_of_rows] == seg_own).astype(
            jnp.float32
        )
        mixed = (
            mixed
            + conv_taps[tap_index][None, :]
            * extended[tap_index : tap_index + count_of_rows]
            * same_doc[:, None]
        )
    activated = jax.nn.silu(mixed)
    step_size = jax.nn.softplus(step_raw + step_shift[None, :])
    log_rate = step_size * (-jnp.exp(decay_logs))[None, :]
    return (activated, step_size, log_rate)


def decay_terms(log_rate, seg_own, seg_before):
    count_of_rows = log_rate.shape[0]
    index_rows = jnp.arange(count_of_rows)
    lower = (index_rows[:, None] >= index_rows[None, :]).astype(jnp.float32)
    running = jnp.dot(lower, log_rate, precision=lax.Precision.HIGHEST)
    entry = jnp.exp(running) * (seg_own == seg_before).astype(jnp.float32)[:, None]
    leaving = (
        jnp.exp(running[-1][None, :] - running)
        * (seg_own == seg_own[-1]).astype(jnp.float32)[:, None]
    )
    carried = jnp.exp(running[-1]) * (seg_own[-1] == seg_before).astype(jnp.float32)
    return (running, entry, leaving, carried)


def heads_to_columns(values):
    spread = jnp.repeat(jnp.eye(MH, dtype=jnp.float32), MP, axis=1)
    return jnp.dot(values, spread, precision=lax.Precision.HIGH)


def columns_to_heads(values):
    spread = jnp.repeat(jnp.eye(MH, dtype=jnp.float32), MP, axis=1)
    return jnp.einsum("ic,hc->ih", values, spread, precision=lax.Precision.HIGH)


def matmul(left, right, sides=((1,), (0,))):
    return lax.dot_general(left, right, (sides, ((), ())), preferred_element_type=jnp.float32)


def attend_kernel(*refs):
    query_ref, slots, bias_ref = refs[0], refs[1:9], refs[9]
    out_ref, total_ref, heads_ref, turned_ref = refs[10:]
    head = pl.program_id(0)
    rows = slots[0].shape[0]

    @pl.when(head == 0)
    def _():
        for place, slot in enumerate(slots):
            block = slot[...]
            span = slice(place * rows, (place + 1) * rows)
            for part in range(4):
                heads_ref[part, span, :] = block[:, part * HEAD_WIDTH : (part + 1) * HEAD_WIDTH]
            turned_ref[:, span] = block.astype(jnp.float32).T.astype(jnp.bfloat16)

    group = head // 4
    value_rows = pl.ds(pl.multiple_of((2 + group) * HEAD_WIDTH, HEAD_WIDTH), HEAD_WIDTH)
    scores = matmul(heads_ref[group], query_ref[...]) + bias_ref[...].astype(jnp.float32)
    top = jnp.max(scores, axis=0, keepdims=True)
    exponent = jnp.exp(scores - top)
    total = jnp.sum(exponent, axis=0, keepdims=True)
    probs = (exponent * (1.0 / total)).astype(jnp.bfloat16)
    out_ref[...] = matmul(turned_ref[value_rows, :], probs).astype(jnp.bfloat16)
    total_ref[0] = top + jnp.log(total)


def attend_back_kernel(
    query_t_ref,
    query_ref,
    out_t_ref,
    out_ref,
    key_ref,
    value_ref,
    key_t_ref,
    bias_ref,
    total_ref,
    d_query_ref,
    d_key_ref,
):
    scores = matmul(key_ref[0], query_t_ref[...]) + bias_ref[...].astype(jnp.float32)
    probs = jnp.exp(scores - total_ref[0])
    d_probs = matmul(value_ref[0], out_t_ref[...])
    delta = jnp.sum(probs * d_probs, axis=0, keepdims=True)
    d_scores = (probs * (d_probs - delta)).astype(jnp.bfloat16)
    d_query_ref[...] = matmul(key_t_ref[...], d_scores)
    d_key = matmul(d_scores, query_ref[0])
    d_value = matmul(probs.astype(jnp.bfloat16), out_ref[0])
    both = jnp.concatenate([d_key, d_value], axis=1)
    first = pl.program_id(0) % 4 == 0

    @pl.when(first)
    def _():
        d_key_ref[0] = both

    @pl.when(jnp.logical_not(first))
    def _():
        d_key_ref[0] += both


def within_kernel(inputs_ref, inter_ref, bias_ref, column_ref, row_ref, out_ref):
    parts = []
    for p in range(2):
        within = jnp.exp(column_ref[0, :, p : p + 1] - row_ref[0, p : p + 1, :] + bias_ref[...])
        mixing = (inter_ref[...] * within).astype(jnp.bfloat16)
        parts.append(matmul(mixing, inputs_ref[...]))
    lane = lax.broadcasted_iota(jnp.int32, parts[0].shape, 1)
    out_ref[...] = jnp.where(lane < MP, parts[0], parts[1])


def within_back_kernel(
    inputs_ref,
    grad_ref,
    inter_ref,
    bias_ref,
    column_ref,
    row_ref,
    d_inputs_ref,
    d_inter_ref,
    d_column_ref,
    d_row_ref,
):
    lane = lax.broadcasted_iota(jnp.int32, inputs_ref.shape, 1)
    parts, columns, rows, d_inter = [], [], [], None
    for p in range(2):
        within = jnp.exp(row_ref[0, p : p + 1, :] - column_ref[0, :, p : p + 1] + bias_ref[...])
        mixing = inter_ref[...] * within
        parts.append(matmul(mixing.astype(jnp.bfloat16), grad_ref[...]))
        own = (lane < MP) if p == 0 else (lane >= MP)
        own_inputs = jnp.where(own, inputs_ref[...].astype(jnp.float32), 0.0)
        d_mixing = matmul(own_inputs.astype(jnp.bfloat16), grad_ref[...], ((1,), (1,)))
        product = d_mixing * mixing
        rows.append(jnp.sum(product, axis=0, keepdims=True))
        columns.append(jnp.sum(product, axis=1, keepdims=True))
        term = d_mixing * within
        d_inter = term if d_inter is None else d_inter + term
    d_inputs_ref[...] = jnp.where(lane < MP, parts[0], parts[1])
    d_row_ref[0] = jnp.concatenate(rows, axis=0)
    d_column_ref[0] = jnp.concatenate(columns, axis=1)
    first = pl.program_id(0) == 0

    @pl.when(first)
    def _():
        d_inter_ref[...] = d_inter

    @pl.when(jnp.logical_not(first))
    def _():
        d_inter_ref[...] += d_inter


def kernel_call(kernel, steps, ins, outs, flops, args):
    out_shape = [jax.ShapeDtypeStruct(shape, kind) for shape, kind, _, _ in outs]
    return pl.pallas_call(
        kernel,
        grid=(steps,),
        in_specs=[pl.BlockSpec(block, where) for block, where in ins],
        out_specs=[pl.BlockSpec(block, where) for _, _, block, where in outs],
        out_shape=out_shape,
        compiler_params=pltpu.CompilerParams(vmem_limit_bytes=48 * 1024 * 1024),
        cost_estimate=pl.CostEstimate(flops=flops, bytes_accessed=4 << 20, transcendentals=4 << 20),
    )(*args)


def feed_kernel(normed_ref, gate_ref, up_ref, down_ref, gate_lin_ref, up_lin_ref, hidden_ref, out_ref):
    gate = matmul(normed_ref[...], gate_ref[...])
    up = matmul(normed_ref[...], up_ref[...])
    gate_lin_ref[...] = gate
    up_lin_ref[...] = up
    hidden = (jax.nn.silu(gate) * up).astype(jnp.bfloat16)
    hidden_ref[...] = hidden
    out = matmul(hidden, down_ref[...])
    first = pl.program_id(0) == 0

    @pl.when(first)
    def _():
        out_ref[...] = out

    @pl.when(jnp.logical_not(first))
    def _():
        out_ref[...] += out


def feed_back_kernel(
    cotangent_ref,
    gate_lin_ref,
    up_lin_ref,
    gate_ref,
    up_ref,
    down_ref,
    d_gate_ref,
    d_up_ref,
    d_normed_ref,
):
    d_hidden = matmul(cotangent_ref[...], down_ref[...], ((1,), (1,)))
    gate, up = gate_lin_ref[...], up_lin_ref[...]
    sigmoid = jax.nn.sigmoid(gate)
    d_gate = (d_hidden * up * sigmoid * (1.0 + gate * (1.0 - sigmoid))).astype(jnp.bfloat16)
    d_up = (d_hidden * gate * sigmoid).astype(jnp.bfloat16)
    d_gate_ref[...] = d_gate
    d_up_ref[...] = d_up
    back = matmul(d_gate, gate_ref[...], ((1,), (1,))) + matmul(d_up, up_ref[...], ((1,), (1,)))
    first = pl.program_id(0) == 0

    @pl.when(first)
    def _():
        d_normed_ref[...] = back

    @pl.when(jnp.logical_not(first))
    def _():
        d_normed_ref[...] += back


FEED_WEIGHTS = [
    ((1024, 512), lambda j: (0, j)),
    ((1024, 512), lambda j: (0, 4 + j)),
    ((512, 1024), lambda j: (j % 2, 6 + j // 2)),
]


def feed_forward(normed_low, weights):
    rows = normed_low.shape[0]
    part = ((rows, 512), lambda j: (0, j))
    whole = ((rows, 1024), lambda j: (0, 0))
    return kernel_call(
        feed_kernel,
        4,
        [whole] + FEED_WEIGHTS,
        [
            ((rows, 2048), jnp.float32) + part,
            ((rows, 2048), jnp.float32) + part,
            ((rows, 2048), jnp.bfloat16) + part,
            ((rows, 1024), jnp.float32) + whole,
        ],
        6 * rows * 1024 * 2048,
        (normed_low, weights, weights, weights),
    )


def feed_backward(cotangent, gate_lin, up_lin, weights):
    rows = cotangent.shape[0]
    part = ((rows, 512), lambda j: (0, j))
    whole = ((rows, 1024), lambda j: (0, 0))
    return kernel_call(
        feed_back_kernel,
        4,
        [whole, part, part] + FEED_WEIGHTS,
        [
            ((rows, 2048), jnp.bfloat16) + part,
            ((rows, 2048), jnp.bfloat16) + part,
            ((rows, 1024), jnp.float32) + whole,
        ],
        6 * rows * 1024 * 2048,
        (cotangent, gate_lin, up_lin, weights, weights, weights),
    )


def layout_kernel(low_ref, high_ref, gate_ref, up_ref, mix_gate_ref, attn_ref, mix_ref, down_ref):
    for side, source in enumerate((low_ref, high_ref)):
        block = source[...].astype(jnp.float32)
        target = up_ref if side else gate_ref
        for d in range(16):
            target[:, 128 * d : 128 * d + 128] = jnp.concatenate(
                [block[:, 64 * d : 64 * d + 64], block[:, 1024 + 64 * d : 1088 + 64 * d]], axis=1
            )
        mix_gate_ref[:, 768 * side : 768 * side + 768] = block[:, 2048:2816]
        span = slice(512 * side, 512 * side + 512)
        attn_ref[:, span] = block[:32, 2816:3328]
        mix_ref[:32, span] = block[32:, 2816:3328]
        mix_ref[32:, span] = block[:, 3328:3840]
        down_ref[:64, span] = block[:, 3840:4352]
        down_ref[64:, span] = block[:, 4352:4864]


def laid_out(low, high):
    shapes = [(64, 2048), (64, 2048), (64, 1536), (32, 1024), (96, 1024), (128, 1024)]

    def origin(_):
        return (0, 0)

    return kernel_call(
        layout_kernel,
        1,
        [(low.shape, origin), (high.shape, origin)],
        [(shape, jnp.float32, shape, origin) for shape in shapes],
        1 << 20,
        (low, high),
    )


def attend(query_t, slots, bias):
    keys, rows = bias.shape
    size = HEAD_WIDTH
    return kernel_call(
        attend_kernel,
        QUERY_HEADS,
        [((size, rows), lambda h: (h, 0))]
        + [((rows, 4 * size), lambda h: (0, 0))] * 8
        + [((keys, rows), lambda h: (0, 0))],
        [
            ((QUERY_HEADS * size, rows), jnp.bfloat16, (size, rows), lambda h: (h, 0)),
            ((QUERY_HEADS, 1, rows), jnp.float32, (1, 1, rows), lambda h: (h, 0, 0)),
            ((4, keys, size), jnp.bfloat16, (4, keys, size), lambda h: (0, 0, 0)),
            ((4 * size, keys), jnp.bfloat16, (4 * size, keys), lambda h: (0, 0)),
        ],
        4 * QUERY_HEADS * size * rows * keys * 4,
        (query_t, *slots, bias),
    )


def attend_back(query_t, query_heads, out_t, out_heads, kv_heads, kv_t, bias, totals):
    keys, rows = bias.shape
    size = HEAD_WIDTH
    return kernel_call(
        attend_back_kernel,
        QUERY_HEADS,
        [
            ((size, rows), lambda h: (h, 0)),
            ((1, rows, size), lambda h: (h, 0, 0)),
            ((size, rows), lambda h: (h, 0)),
            ((1, rows, size), lambda h: (h, 0, 0)),
            ((1, keys, size), lambda h: (h // 4, 0, 0)),
            ((1, keys, size), lambda h: (2 + h // 4, 0, 0)),
            ((size, keys), lambda h: (h // 4, 0)),
            ((keys, rows), lambda h: (0, 0)),
            ((1, 1, rows), lambda h: (h, 0, 0)),
        ],
        [
            ((QUERY_HEADS * size, rows), jnp.float32, (size, rows), lambda h: (h, 0)),
            (
                (KEY_VALUE_HEADS, keys, 2 * size),
                jnp.float32,
                (1, keys, 2 * size),
                lambda h: (h // 4, 0, 0),
            ),
        ],
        10 * QUERY_HEADS * size * rows * keys * 4,
        (query_t, query_heads, out_t, out_heads, kv_heads, kv_heads, kv_t, bias, totals),
    )


def pair_blocks(rows):
    return (
        ((rows, 2 * MP), lambda i: (0, i)),
        ((rows, rows), lambda i: (0, 0)),
        ((1, rows, 2), lambda i: (i, 0, 0)),
        ((1, 2, rows), lambda i: (i, 0, 0)),
    )


def within_block(inputs_low, inter, bias, columns, rows_of):
    rows = inter.shape[0]
    wide, square, column, row = pair_blocks(rows)
    return kernel_call(
        within_kernel,
        MH // 2,
        [wide, square, square, column, row],
        [((rows, MH * MP), jnp.float32) + wide],
        16 * MH * MP * rows * rows,
        (inputs_low, inter, bias, columns, rows_of),
    )[0]


def within_block_back(inputs_low, grad_low, inter_t, bias_t, columns, rows_of):
    rows = inter_t.shape[0]
    wide, square, column, row = pair_blocks(rows)
    return kernel_call(
        within_back_kernel,
        MH // 2,
        [wide, wide, square, square, column, row],
        [
            ((rows, MH * MP), jnp.float32) + wide,
            ((rows, rows), jnp.float32) + square,
            ((MH // 2, rows, 2), jnp.float32) + column,
            ((MH // 2, 2, rows), jnp.float32) + row,
        ],
        32 * MH * MP * rows * rows,
        (inputs_low, grad_low, inter_t, bias_t, columns, rows_of),
    )


def project(left, right):
    return jnp.dot(left, right, preferred_element_type=jnp.float32)


def input_grad(left, right):
    return jnp.einsum("rk,rj->kj", left, right, preferred_element_type=jnp.float32)


def back_through(grad_low, weight_full):
    return jnp.einsum("rj,kj->rk", grad_low, weight_full, preferred_element_type=jnp.float32)


def swiglu(gate_values, up_values):
    return jax.nn.silu(gate_values) * up_values


def gating(scan_values, gate_values):
    return scan_values * jax.nn.silu(gate_values)


def on_device(
    tokens,
    segments,
    cotangent,
    attention_gain,
    query_weight,
    key_matrix,
    value_matrix,
    attention_out,
    gate_weight,
    mixer_weight,
    step_weight,
    mixer_out,
    conv_weight,
    conv_bias,
    step_bias,
    decay_log,
    skip_gain,
    feed_gain,
    feed_gate,
    feed_up,
    feed_down,
):
    block_index = lax.axis_index("context")
    core = block_index % 2
    chip = block_index // 2
    both = ("dp", "context")
    step_padded = jnp.pad(step_weight, ((0, 0), (0, IN_WIDTH - IN_USED)))
    in_shard = jnp.concatenate(
        [query_weight, key_matrix, value_matrix, gate_weight, mixer_weight, step_padded], axis=1
    )
    in_full = lax.all_gather(
        lax.dynamic_slice_in_dim(in_shard, block_index * 8, 8, 0), both, axis=0, tiled=True
    )
    def hidden_order(block):
        return block.reshape(8, 16, 2, 64).transpose(0, 2, 1, 3).reshape(8, 2048)

    feed_shard = jnp.concatenate(
        [
            hidden_order(lax.dynamic_slice_in_dim(feed_gate, block_index * 8, 8, 0)),
            hidden_order(lax.dynamic_slice_in_dim(feed_up, block_index * 8, 8, 0)),
        ],
        axis=1,
    )
    out_rows_own = jnp.concatenate([attention_out, mixer_out, feed_down], axis=0)
    out_shard = [
        lax.dynamic_slice_in_dim(out_rows_own, group * 64 + block_index * 8, 8, 0)
        for group in range(4)
    ]
    late_full = lax.all_gather(
        jnp.concatenate([feed_shard] + out_shard, axis=1), both, axis=0, tiled=True
    )
    first_rows = late_full[:, 4096:5120].reshape(16, 64, 1024)
    second_rows = late_full[:, 5120:6144].reshape(16, 64, 1024)
    out_full = first_rows[:, :32].reshape(512, 1024)
    mixer_out_full = jnp.concatenate([first_rows[:, 32:], second_rows], axis=1).reshape(1536, 1024)
    count_of_rows = tokens.shape[0]
    tap_count = conv_weight.shape[0]
    inner_width = MH * MP
    width_of_keys = KEY_VALUE_HEADS * HEAD_WIDTH
    query_places = block_index * count_of_rows + jnp.arange(count_of_rows, dtype=jnp.int32)
    place_float = query_places.astype(jnp.float32)
    seg_float = segments.astype(jnp.float32)
    seg_low = segments.astype(jnp.bfloat16)
    seg_all = jnp.concatenate(from_everyone(seg_low))
    owners = jnp.concatenate(
        [(chip - jnp.arange(4)) % 4 * 2 + core, (chip - jnp.arange(4)) % 4 * 2 + 1 - core]
    )
    key_places = (
        owners[:, None] * count_of_rows + jnp.arange(count_of_rows, dtype=jnp.int32)[None, :]
    ).reshape(-1)
    attention_bias = jnp.where(
        (key_places[:, None] <= query_places[None, :]) & (seg_all[:, None] == seg_low[None, :]),
        0.0,
        masked_fill,
    ).astype(jnp.bfloat16)
    halo = 8
    tokens_before, seg_rows_before = from_behind(
        (tokens[count_of_rows - halo :], seg_float[count_of_rows - halo :]), "context", 1
    )
    prev_segs = seg_rows_before[halo - tap_count + 1 :]
    normed_before = rms_norm(tokens_before.astype(jnp.float32), attention_gain)
    hidden_in = tokens.astype(jnp.float32)
    normed, norm_one_back = jax.vjp(rms_norm, hidden_in, attention_gain)
    normed_low = normed.astype(jnp.bfloat16)
    every_lin = project(normed_low, in_full)
    query_lin = every_lin[:, :512]
    key_lin = every_lin[:, 512:640]
    value_lin = every_lin[:, 640:768]
    gate_lin = every_lin[:, 768:2304]
    mixer_lin = every_lin[:, 2304:4096]
    step_lin = every_lin[:, 4096:IN_USED]
    rotated_queries = rotary(query_lin, place_float, 1.0).astype(jnp.bfloat16)
    rotated_keys = rotary(key_lin, place_float, 1.0).astype(jnp.bfloat16)
    value_reduced = value_lin.astype(jnp.bfloat16)
    sent, mixer_lin, gate_lin, step_lin = lax.optimization_barrier(
        (
            jnp.concatenate([rotated_keys, value_reduced], axis=1),
            mixer_lin,
            gate_lin,
            step_lin,
        )
    )
    slots = from_everyone(sent)
    scale_factor = 1.0 / math.sqrt(HEAD_WIDTH)
    query_scaled = rotated_queries * jnp.asarray(scale_factor, jnp.bfloat16)
    prev_rows = project(normed_before.astype(jnp.bfloat16), in_full[:, 2304:4096])
    prev_rows = prev_rows[halo - tap_count + 1 :]
    extended = jnp.concatenate([prev_rows, mixer_lin], axis=0)
    seg_extended = jnp.concatenate([prev_segs, seg_float])
    seg_before = prev_segs[-1]

    def mixer_piece(ext_rows, conv_taps, conv_shift, step_raw, step_shift, decay_logs):
        return mixer_inputs(
            ext_rows,
            seg_extended,
            seg_float,
            conv_taps,
            conv_shift,
            step_raw,
            step_shift,
            decay_logs,
        )

    (activated, step_size, log_rate), mixer_back = jax.vjp(
        mixer_piece, extended, conv_weight, conv_bias, step_lin, step_bias, decay_log
    )
    mixer_x = activated[:, :inner_width]
    bees = activated[:, inner_width : inner_width + NS].astype(jnp.bfloat16)
    seas = activated[:, inner_width + NS :].astype(jnp.bfloat16)

    def decay_piece(rates):
        return decay_terms(rates, seg_float, seg_before)

    (running, entry, leaving, carried), decay_back = jax.vjp(decay_piece, log_rate)
    spread = heads_to_columns(jnp.concatenate([step_size, leaving, entry], axis=0))
    step_wide = spread[:count_of_rows]
    leaving_wide = spread[count_of_rows : 2 * count_of_rows]
    entry_wide = spread[2 * count_of_rows :]
    inputs_low = (mixer_x * step_wide).astype(jnp.bfloat16)
    inputs_low, slots = lax.optimization_barrier((inputs_low, slots))
    weighted_low = (inputs_low.astype(jnp.float32) * leaving_wide).astype(jnp.bfloat16)
    local_state = input_grad(bees, weighted_low)
    decays = chip_decays(jnp.repeat(carried, MP))
    skip_wide = jnp.repeat(skip_gain, MP)[None, :]
    chip_first, chip_low = chip_part(decays, local_state, False)
    query_t, chip_low = lax.optimization_barrier((query_scaled.T, chip_low))
    attended_t, totals, kv_heads, kv_t = attend(query_t, slots, attention_bias)
    parts, attended_t = from_chips(chip_low, False, attended_t)
    incoming_low = carried_in(decays, chip_first, parts, False)
    attended_low = attended_t.T
    attention_branch = project(attended_low, out_full)
    index_rows = jnp.arange(count_of_rows)
    block_allowed = (index_rows[:, None] >= index_rows[None, :]) & (
        seg_float[:, None] == seg_float[None, :]
    )
    block_bias = jnp.where(block_allowed, 0.0, masked_fill)
    running_rows = running.T.reshape(MH // 2, 2, count_of_rows)
    running_columns = running_rows.transpose(0, 2, 1)
    intersection = matmul(seas, bees, ((1,), (1,)))
    inner = within_block(inputs_low, intersection, block_bias, running_columns, running_rows)
    from_state = project(seas, incoming_low)
    scanned = inner + from_state * entry_wide + skip_wide * mixer_x
    gated, gating_back = jax.vjp(gating, scanned, gate_lin)
    gated_low = gated.astype(jnp.bfloat16)
    mixer_branch = project(gated_low, mixer_out_full)
    residual = hidden_in + attention_multiplier * attention_branch + mixer_multiplier * mixer_branch
    normed_two, norm_two_back = jax.vjp(rms_norm, residual, feed_gain)
    normed_two_low = normed_two.astype(jnp.bfloat16)
    ffn_gate_lin, ffn_up_lin, hidden_low, feed_out = feed_forward(normed_two_low, late_full)
    output = (residual + feed_out).astype(jnp.bfloat16)
    upstream = cotangent.astype(jnp.float32)
    d_ffn_gate, d_ffn_up, d_normed_two = feed_backward(
        cotangent, ffn_gate_lin, ffn_up_lin, late_full
    )
    d_feed_low = jnp.stack([d_ffn_gate, d_ffn_up])
    d_resid_norm, grad_feed_gain = norm_two_back(d_normed_two)
    d_residual = upstream + d_resid_norm
    d_attn_low = (attention_multiplier * d_residual).astype(jnp.bfloat16)
    d_mixer_low = (mixer_multiplier * d_residual).astype(jnp.bfloat16)

    feed_got = swap_cores(
        input_grad(normed_two_low, d_feed_low[1 - core]).astype(jnp.bfloat16)
    )
    feed_own = (
        input_grad(normed_two_low, d_feed_low[core]) + feed_got.astype(jnp.float32)
    ).astype(jnp.bfloat16)
    attended_gradient = back_through(d_attn_low, out_full).astype(jnp.bfloat16)
    d_gated = back_through(d_mixer_low, mixer_out_full)
    d_scan_flat, d_gate_lin = gating_back(d_gated)
    d_gate_low = d_gate_lin.astype(jnp.bfloat16)

    def out_grads(which):
        attn = input_grad(attended_low, half(d_attn_low, which, 1)).astype(jnp.bfloat16)
        mix = input_grad(gated_low, half(d_mixer_low, which, 1)).astype(jnp.bfloat16)
        down = input_grad(hidden_low, half(cotangent, which, 1)).astype(jnp.bfloat16)
        gate = input_grad(normed_low, half(d_gate_low, which, 1)).astype(jnp.bfloat16)
        return (attn, mix, down, gate)

    out_got = jax.tree.map(swap_cores, out_grads(1 - core))
    early = jax.tree.map(lambda a, b: a + b, out_grads(core), out_got)
    mix_rows = early[1].reshape(16, 96, 512)
    early_rows = jnp.concatenate(
        [
            feed_own,
            early[3],
            jnp.concatenate([early[0].reshape(16, 32, 512), mix_rows[:, :32]], axis=1).reshape(
                1024, 512
            ),
            mix_rows[:, 32:].reshape(1024, 512),
            early[2][:1024],
            early[2][1024:],
        ],
        axis=1,
    )
    d_scan_low = d_scan_flat.astype(jnp.bfloat16)
    d_scan = d_scan_low.astype(jnp.float32)
    d_from_low = (d_scan * entry_wide).astype(jnp.bfloat16)
    d_incoming = input_grad(seas, d_from_low)
    chip_last, chip_low_back = chip_part(decays, d_incoming, True)
    attended_gradient, early_rows, chip_low_back = lax.optimization_barrier(
        (attended_gradient, early_rows, chip_low_back)
    )
    early_shard = lax.psum_scatter(early_rows, "dp", scatter_dimension=0, tiled=True)
    d_query_t, d_kv = attend_back(
        query_t,
        query_scaled.reshape(count_of_rows, QUERY_HEADS, HEAD_WIDTH).transpose(1, 0, 2),
        attended_gradient.T,
        attended_gradient.reshape(count_of_rows, QUERY_HEADS, HEAD_WIDTH).transpose(1, 0, 2),
        kv_heads,
        kv_t,
        attention_bias,
        totals,
    )
    parts, d_kv = from_chips(chip_low_back, True, d_kv)
    d_state_low = carried_in(decays, chip_last, parts, True)
    d_scan_low, d_kv, d_state_low = lax.optimization_barrier((d_scan_low, d_kv, d_state_low))
    d_query_rot = d_query_t.T * scale_factor
    slot_grads = d_kv.astype(jnp.bfloat16).reshape(KEY_VALUE_HEADS, 2, 4, count_of_rows, -1)
    chip_grads = slot_grads[:, 0].astype(jnp.float32) + swap_cores(slot_grads[:, 1]).astype(
        jnp.float32
    )
    chip_low = chip_grads.astype(jnp.bfloat16)
    own_grads = chip_grads[:, 0]
    for k in range(1, 4):
        own_grads = own_grads + shift_chips(chip_low[:, k], -k).astype(jnp.float32)
    key_grads = jnp.concatenate(
        [
            own_grads[0, :, :HEAD_WIDTH],
            own_grads[1, :, :HEAD_WIDTH],
            own_grads[0, :, HEAD_WIDTH:],
            own_grads[1, :, HEAD_WIDTH:],
        ],
        axis=1,
    )
    d_query_low = rotary(d_query_rot, place_float, -1.0).astype(jnp.bfloat16)
    d_key_low = rotary(key_grads[:, :width_of_keys], place_float, -1.0).astype(jnp.bfloat16)
    d_value_low = key_grads[:, width_of_keys:].astype(jnp.bfloat16)
    d_inputs, d_inter_t, d_columns, d_rows = within_block_back(
        inputs_low, d_scan_low, intersection.T, block_bias.T, running_columns, running_rows
    )
    d_running = (d_rows - d_columns.transpose(0, 2, 1)).reshape(MH, count_of_rows).T
    d_inter_low = d_inter_t.astype(jnp.bfloat16)
    d_seas = back_through(d_from_low, incoming_low) + input_grad(d_inter_low, bees)
    d_bees = project(d_inter_low, seas) + back_through(weighted_low, d_state_low)
    d_weighted = project(bees, d_state_low)
    d_inputs = d_inputs + d_weighted * leaving_wide
    d_mixer_x = skip_wide * d_scan + d_inputs * step_wide
    d_entry = columns_to_heads(d_scan * from_state)
    d_leaving = columns_to_heads(d_weighted * inputs_low.astype(jnp.float32))
    d_step = columns_to_heads(d_inputs * mixer_x)
    sums = columns_to_heads(
        jnp.concatenate(
            [
                jnp.sum(d_scan * mixer_x, axis=0, keepdims=True),
                jnp.sum(
                    d_state_low.astype(jnp.float32) * incoming_low.astype(jnp.float32),
                    axis=0,
                    keepdims=True,
                ),
            ],
            axis=0,
        )
    )
    grad_skip_gain, d_carried = sums[0], sums[1]
    (d_rate,) = decay_back((d_running, d_entry, d_leaving, d_carried))
    d_activated = jnp.concatenate([d_mixer_x, d_bees, d_seas], axis=1)
    d_activated, early_shard = lax.optimization_barrier((d_activated, early_shard))
    one, two, three = (shift_chips(early_shard, k).astype(jnp.float32) for k in range(1, 4))
    early_mine = ((early_shard.astype(jnp.float32) + two) + (one + three)).astype(jnp.bfloat16)
    d_extended, grad_conv_weight, grad_conv_bias, d_step_lin, grad_step_bias, grad_decay_log = (
        mixer_back((d_activated, d_step, d_rate))
    )
    rim_back = from_behind(d_extended[: tap_count - 1], "context", -1)
    d_mixer_lin = d_extended[tap_count - 1 :] + jnp.pad(
        rim_back, ((count_of_rows - tap_count + 1, 0), (0, 0))
    )
    d_late_low = jnp.concatenate(
        [
            d_query_low,
            d_key_low,
            d_value_low,
            d_mixer_lin.astype(jnp.bfloat16),
            jnp.pad(d_step_lin, ((0, 0), (0, IN_WIDTH - IN_USED))).astype(jnp.bfloat16),
        ],
        axis=1,
    )

    width = IN_WIDTH // 2 - 768
    late_got = swap_cores(
        input_grad(normed_low, half(d_late_low, 1 - core, 1)).astype(jnp.bfloat16)
    )
    d_late_low, early_mine = lax.optimization_barrier((d_late_low, early_mine))
    early_other = swap_cores(early_mine)
    late_own = input_grad(normed_low, half(d_late_low, core, 1)) + late_got.astype(jnp.float32)
    late_own = late_own.astype(jnp.bfloat16)
    late_own, d_late_low = lax.optimization_barrier((late_own, d_late_low))
    d_every_low = jnp.concatenate([d_late_low[:, :768], d_gate_low, d_late_low[:, 768:]], axis=1)
    d_normed = back_through(d_every_low, in_full)
    d_tokens_norm, grad_attention_gain = norm_one_back(d_normed)
    grad_tokens = d_residual + d_tokens_norm

    def flat(part):
        part = part.reshape(-1)
        return jnp.pad(part, (0, -part.size % 128))

    pieces = (
        grad_attention_gain,
        grad_conv_weight,
        grad_conv_bias,
        grad_step_bias,
        grad_decay_log,
        grad_skip_gain,
        grad_feed_gain,
    )
    packed = jnp.concatenate([flat(part) for part in pieces])
    packed = jnp.pad(packed, (0, -packed.size % 1024)).reshape(-1, 128)
    late_parts = lax.all_to_all(
        late_own.reshape(64, 16, width), both, 0, 0, axis_index_groups=CORE_GROUPS
    )
    packed = sum_near(packed)
    late_total = jnp.sum(late_parts.astype(jnp.float32), axis=0).astype(jnp.bfloat16)
    early_low = jnp.where(core == 0, early_mine, early_other)
    early_high = jnp.where(core == 0, early_other, early_mine)
    late_total, early_low, early_high, packed = lax.optimization_barrier(
        (late_total, early_low, early_high, packed)
    )
    packed = sum_of_four(packed, lambda part, k: shift_rows(part, k, 4)).reshape(-1)
    late_all = copies_of(late_total).reshape(4, 2, 16, width).astype(jnp.float32)
    late_all = late_all.transpose(0, 2, 1, 3).reshape(64, 2 * width)
    grad_feed_gate, grad_feed_up, grad_gate_weight, grad_attn, grad_mix, grad_down = laid_out(
        early_low, early_high
    )
    small, start = [], 0
    for part in pieces:
        small.append(packed[start : start + part.size].reshape(part.shape))
        start += part.size + -part.size % 128
    summed = (
        late_all[:, :512],
        late_all[:, 512:640],
        late_all[:, 640:768],
        grad_attn,
        grad_gate_weight,
        late_all[:, 768:2560],
        late_all[:, 2560 : 2560 + MH],
        grad_mix,
        grad_feed_gate,
        grad_feed_up,
        grad_down,
    )
    return (
        output,
        grad_tokens,
        small[0],
        summed[0],
        summed[1],
        summed[2],
        summed[3],
        summed[4],
        summed[5],
        summed[6],
        summed[7],
        small[1],
        small[2],
        small[3],
        small[4],
        small[5],
        small[6],
        summed[8],
        summed[9],
        summed[10],
    )


def solution(mesh):
    return jax.shard_map(
        on_device,
        mesh=mesh,
        in_specs=(
            P(("dp", "context"), None),
            P(("dp", "context")),
            P(("dp", "context"), None),
            P(),
            P("dp", None),
            P("dp", None),
            P("dp", None),
            P("dp", None),
            P("dp", None),
            P("dp", None),
            P("dp", None),
            P("dp", None),
            P(),
            P(),
            P(),
            P(),
            P(),
            P(),
            P("dp", None),
            P("dp", None),
            P("dp", None),
        ),
        out_specs=(
            P(("dp", "context"), None),
            P(("dp", "context"), None),
            P(),
            P("dp", None),
            P("dp", None),
            P("dp", None),
            P("dp", None),
            P("dp", None),
            P("dp", None),
            P("dp", None),
            P("dp", None),
            P(),
            P(),
            P(),
            P(),
            P(),
            P(),
            P("dp", None),
            P("dp", None),
            P("dp", None),
        ),
        check_vma=False,
    )
```
